32 devices in a mesh: gx: 4 (over z), gy: 2 (over x), gz: 4 (over y, core).
Axes of the slice: x: 2, y: 2, z: 4, core: 2. Of those that a mesh axis runs over, the one named last changes fastest.
Arguments:
- inputs: bfloat16 [1, 32, 16, 8, 512], P(None, None, 'gx', 'gy', 'gz'), may hold values from -40 to 40
- noise: bfloat16 [1, 32, 16, 8, 512], P(None, None, 'gx', 'gy', 'gz'), may hold values from -6 to 6
- w_first: bfloat16 [32, 864], replicated, may hold values from -0.21875 to 0.21875
- w_second: bfloat16 [32, 864], replicated, may hold values from -0.21875 to 0.21875
Outputs:
- prediction: bfloat16 [1, 32, 16, 8, 512], P(None, None, 'gx', 'gy', 'gz')
- fisher_first: float32 [32, 864], replicated
- fisher_second: float32 [32, 864], replicated
The draws below stay inside these ranges and needn't reach their ends.
All inputs are finite; a program needn't handle non-finite values.
Results may differ from the reference program's by a relative error of at most 0.0049.
Values may be sent and summed in bfloat16 or wider, within the bound.
No kernel may reach another device: no remote copies, remote signals or barrier semaphores. Data moves between devices by JAX's collectives and lax.ppermute only.
A program may use at most 128 MiB of HBM per device.

```python
import math
import jax
import jax.numpy as jnp
from jax import lax

C = 32
B = 1
NX = 16
NY = 8
NZ = 512


def draw_inputs(key, part):
    key = jax.random.fold_in(key, 11)
    key_base, key_cells, key_chans = jax.random.split(key, 3)
    shape = (B, C, NX, NY, NZ)
    cell_scale = jnp.exp(jax.random.uniform(key_cells, (B, 1, NX, NY, NZ), jnp.float32, 0.0, math.log(10.0)))
    chan_scale = jnp.exp(jax.random.uniform(key_chans, (1, C, 1, 1, 1), jnp.float32, 0.0, math.log(4.0)))
    base = jax.random.truncated_normal(key_base, -4.0, 4.0, shape, jnp.float32)
    return (base * cell_scale * chan_scale * 0.25).astype(jnp.bfloat16)


def block_levels(key, dims, shards, least, largest):
    gain = 1.0
    for dim, parts in shards:
        heights = jax.random.uniform(jax.random.fold_in(jax.random.fold_in(key, 6), dim), (parts,), jnp.float32, least / len(shards), largest / len(shards))
        gain = gain * jnp.repeat(jnp.exp(heights), dims[dim] // parts).reshape((-1,) + (1,) * (len(dims) - 1 - dim))
    return gain


def gaussian(own_key, dims, deviation, bound, pieces=(), held_as=jnp.bfloat16):
    drawn = deviation * jax.random.normal(own_key, dims, jnp.float32)
    if pieces:
        drawn = drawn * block_levels(own_key, dims, pieces, -0.22, 0.18)
    return jnp.clip(drawn, -bound, bound).astype(held_as)


def setup_inputs(seed: int = 0) -> dict:
    streams_of = jax.random.split(jax.random.key(seed), 5)
    return {
        "inputs": draw_inputs(jax.random.fold_in(streams_of[4], 71), 0),
        "noise": gaussian(streams_of[1], (B, C, NX, NY, NZ), 1.0, 6.0, ((2, 4), (3, 2), (4, 4))),
        "w_first": gaussian(streams_of[2], (C, 27 * C), (27 * C) ** -0.5, 0.21875),
        "w_second": gaussian(streams_of[3], (C, 27 * C), (27 * C) ** -0.5, 0.21875),
    }


def as_kernel(flat_weight):
    channels = flat_weight.shape[0]
    return flat_weight.reshape(channels, 3, 3, 3, channels).transpose(0, 4, 1, 2, 3)

def convolve(flat_weight, field):
    result = lax.conv_general_dilated(field[None], as_kernel(flat_weight), (1, 1, 1), 'SAME', dimension_numbers=('NCDHW', 'OIDHW', 'NCDHW'), precision=lax.Precision.HIGHEST)
    return result[0]

def silu_slope(pre_act):
    sigmoid_value = jax.nn.sigmoid(pre_act)
    return sigmoid_value * (1.0 + pre_act * (1.0 - sigmoid_value))

def reference(inputs, noise, w_first, w_second):
    first_weight = w_first.astype(jnp.float32)
    second_weight = w_second.astype(jnp.float32)
    norm_factor = 1.0 / jnp.sqrt(jnp.float32(NX * NY * NZ))

    def per_sample(pair):
        field, noise_field = pair
        field_wide = field.astype(jnp.float32)
        pre_act = convolve(first_weight, field_wide)
        hidden = lax.optimization_barrier(jax.nn.silu(pre_act).astype(jnp.bfloat16))
        hidden_wide = hidden.astype(jnp.float32)
        output_value, pullback = jax.vjp(convolve, second_weight, hidden_wide)
        second_grad, back_grad = pullback(noise_field.astype(jnp.float32))
        pre_grad = lax.optimization_barrier((back_grad * silu_slope(pre_act)).astype(jnp.bfloat16))
        first_pull = jax.vjp(lambda weight_flat: convolve(weight_flat, field_wide), first_weight)[1]
        first_grad = first_pull(pre_grad.astype(jnp.float32))[0]
        return (output_value.astype(jnp.bfloat16), first_grad * norm_factor, second_grad * norm_factor)
    prediction, first_grads, second_grads = lax.map(per_sample, (inputs, noise))
    fisher_first = lax.optimization_barrier(jnp.mean(jnp.square(first_grads), axis=0))
    fisher_second = lax.optimization_barrier(jnp.mean(jnp.square(second_grads), axis=0))
    return (prediction, fisher_first, fisher_second)
```

```python
import functools
import math

import jax
import jax.numpy as jnp
from jax import lax
from jax.experimental import pallas as pl
from jax.experimental.pallas import tpu as pltpu
from jax.sharding import PartitionSpec as P

F32 = jnp.float32
BF16 = jnp.bfloat16
C = 32


def call(body, out_shapes, scratch=(), flops=1_000_000, moved=1_000_000, vmem=24, **more):
    return pl.pallas_call(
        body,
        **more,
        out_shape=out_shapes,
        scratch_shapes=list(scratch),
        compiler_params=pltpu.CompilerParams(vmem_limit_bytes=vmem * 1024 * 1024),
        cost_estimate=pl.CostEstimate(flops=flops, bytes_accessed=moved, transcendentals=0),
    )


def struct(shape, dtype):
    return jax.ShapeDtypeStruct(shape, dtype)


def even_index(axis):
    return lax.rem(lax.axis_index(axis), 2) == 0


def partner(index, side, size):
    other = index ^ 1 if side == 0 else ((index + 1) ^ 1) - 1
    return other if 0 <= other < size else None


def swap(x, moves):
    axes = tuple(axis for axis, _ in moves)
    sizes = [lax.axis_size(axis) for axis in axes]
    pairs = []
    for source in range(math.prod(sizes)):
        rest, target, factor = source, 0, 1
        for (_, side), size in zip(moves[::-1], sizes[::-1]):
            other = partner(rest % size, side, size)
            if other is None:
                target = None
                break
            target += other * factor
            rest //= size
            factor *= size
        if target is not None:
            pairs.append((source, target))
    return lax.ppermute(x, axes, pairs) if pairs else None


def exchange(face_a, face_b, axis):
    got = [swap(face_a, [(axis, 0)]), swap(face_b, [(axis, 1)])]
    return [g for g in got if g is not None]


def choose(flag, a, b):
    if a is None and b is None:
        return None
    a = jnp.zeros_like(b) if a is None else a
    b = jnp.zeros_like(a) if b is None else b
    return jnp.where(flag, a, b)


def pack_faces(y_sides, in_ref, noise_ref, field_ref, wide_noise_ref, *faces):
    size_x = in_ref.shape[0]
    lanes = in_ref.shape[1]
    for x in range(size_x):
        field_ref[x] = in_ref[x].T
        wide_noise_ref[x] = noise_ref[x].T
    even_x, even_y = even_index("gx"), even_index("gy")
    face_x = faces[:2]
    face_y = faces[2 : 2 + y_sides]
    corner = faces[2 + y_sides :]

    for side in range(2):
        high = even_x if side == 0 else jnp.logical_not(even_x)
        face_x[side][0] = jnp.where(high, field_ref[size_x - 2], field_ref[0])
        face_x[side][1] = jnp.where(high, field_ref[size_x - 1], field_ref[1])
        face_x[side][2] = jnp.where(high, wide_noise_ref[size_x - 1], wide_noise_ref[0])

    for k in range(y_sides):
        high = even_y if k == 0 else jnp.logical_not(even_y)
        two = lambda p: jnp.where(high, p[:, lanes - 2 * C :], p[:, : 2 * C])
        one = lambda p: jnp.where(high, p[:, lanes - C :], p[:, :C])
        for j in range(0, size_x, 2):
            face_y[k][j // 2] = jnp.concatenate([two(field_ref[j]), two(field_ref[j + 1])], axis=1)
        for j in range(0, size_x, 4):
            face_y[k][size_x // 2 + j // 4] = jnp.concatenate([one(wide_noise_ref[j + i]) for i in range(4)], axis=1)
        for side in range(2):
            ref = corner[2 * k + side]
            ref[:128] = jnp.concatenate([two(face_x[side][0]), two(face_x[side][1])], axis=1)
            strip = one(face_x[side][2])
            ref[128:] = jnp.concatenate([strip[i * 32 : (i + 1) * 32] for i in range(4)], axis=1)


class Pieces:
    def __init__(self, y_sides, field, noise, face_x, face_y, corner):
        self.field, self.noise = field, noise
        self.size_x, self.size_z = field.shape[0], field.shape[1]
        even_x, even_y = even_index("gx"), even_index("gy")
        self.flag_x = {"below": even_x, "above": jnp.logical_not(even_x)}
        self.flag_y = {"below": even_y, "above": jnp.logical_not(even_y)}
        self.face_x = list(face_x)
        self.face_y = list(face_y) + [None] * (2 - y_sides)
        self.corner = [list(corner[2 * k : 2 * k + 2]) for k in range(y_sides)] + [[None, None]] * (2 - y_sides)

    def from_x(self, where, index, rows):
        return choose(self.flag_x[where], self.face_x[1][index, rows], self.face_x[0][index, rows])

    def from_y(self, where, read):
        a = [None if ref is None else read(ref) for ref in self.face_y]
        return choose(self.flag_y[where], a[1], a[0])

    def from_corner(self, where_x, where_y, read):
        a = []
        for pair in self.corner:
            if pair[0] is None:
                a.append(None)
            else:
                a.append(choose(self.flag_x[where_x], read(pair[1]), read(pair[0])))
        return choose(self.flag_y[where_y], a[1], a[0])

    def side_of(self, x, width):
        if x < width:
            return "below", x
        if x >= self.size_x + width:
            return "above", x - self.size_x - width
        return "own", x - width

    def field_plane(self, x, z0, z1):
        rows = slice(z0, z1)
        where, i = self.side_of(x, 2)
        if where == "own":
            middle = self.field[i, rows]
            read = lambda ref: ref[i // 2, rows, (i % 2) * 2 * C : (i % 2 + 1) * 2 * C]
            low, high = self.from_y("below", read), self.from_y("above", read)
        else:
            middle = self.from_x(where, i, rows)
            read = lambda ref: ref[rows, i * 2 * C : (i + 1) * 2 * C]
            low, high = self.from_corner(where, "below", read), self.from_corner(where, "above", read)
        return jnp.concatenate([low, middle, high], axis=1)

    def noise_plane(self, x, z0, z1):
        rows = slice(z0, z1)
        where, i = self.side_of(x, 1)
        if where == "own":
            middle = self.noise[i, rows]
            read = lambda ref: ref[self.size_x // 2 + i // 4, rows, (i % 4) * C : (i % 4 + 1) * C]
            low, high = self.from_y("below", read), self.from_y("above", read)
        else:
            middle = self.from_x(where, 2, rows)

            def read(ref):
                parts = []
                for b in range(4):
                    first, last = max(z0, b * 32), min(z1, (b + 1) * 32)
                    if first < last:
                        parts.append(ref[128 + first - b * 32 : 128 + last - b * 32, b * C : (b + 1) * C])
                return jnp.concatenate(parts, axis=0) if len(parts) > 1 else parts[0]

            low, high = self.from_corner(where, "below", read), self.from_corner(where, "above", read)
        return jnp.concatenate([low, middle, high, jnp.zeros((z1 - z0, 2 * C), BF16)], axis=1)


def take_pieces(y_sides, refs):
    n = 4 + 3 * y_sides
    return Pieces(y_sides, refs[0], refs[1], refs[2:4], refs[4 : 4 + y_sides], refs[4 + y_sides : n]), refs[n:]


def pack_z(y_sides, *refs):
    pieces, (low_out, high_out, face_a, face_b) = take_pieces(y_sides, refs)
    n_field, n_noise, size_z = pieces.size_x + 4, pieces.size_x + 2, pieces.size_z

    def gather(tile, first, noise_row):
        planes = [pieces.field_plane(x, tile, tile + 16).astype(F32) for x in range(n_field)]
        rows = [plane[first + k - tile : first + k - tile + 1] for k in range(2) for plane in planes]
        for x in range(n_noise):
            rows.append(pieces.noise_plane(x, tile, tile + 16).astype(F32)[noise_row - tile : noise_row - tile + 1])
        while len(rows) % 16:
            rows.append(jnp.zeros_like(rows[0]))
        return jnp.concatenate(rows, axis=0).astype(BF16)

    low = gather(0, 0, 0)
    high = gather(size_z - 16, size_z - 2, size_z - 1)
    low_out[...] = low
    high_out[...] = high
    even = even_index("gz")
    face_a[...] = jnp.where(even, high, low)
    face_b[...] = jnp.where(even, low, high)


def stack(ref, dz, first, count):
    return ref[dz, first : first + count].reshape(count * ref.shape[2], 256)


def taps(ref, count):
    return jnp.concatenate([stack(ref, dz, dx, count) for dx in range(3) for dz in range(3)], axis=1)


def widen(y_sides, *refs):
    pieces, (a1_ref, xs_ref, ns_ref, pre_ref) = take_pieces(y_sides, refs)
    size_z = pieces.size_z
    for ref, read in ((xs_ref, pieces.field_plane), (ns_ref, pieces.noise_plane)):
        for x in range(ref.shape[1]):
            plane = read(x, 0, size_z)
            ref[1, x] = plane
            ref[0, x] = shifted(plane, 0.0, True)
            ref[2, x] = shifted(plane, 0.0, False)
    n_noise = pre_ref.shape[0]
    total = jnp.dot(taps(xs_ref, n_noise), a1_ref[...], preferred_element_type=F32)
    pre_ref[...] = total.reshape(n_noise, size_z, 256)


def band(ref, row, taps, shift, lo, hi):
    moved = pltpu.roll(taps, shift % 128, 1) if shift % 128 else taps
    lane = lax.broadcasted_iota(jnp.int32, moved.shape, 1)
    for half in range(ref.shape[1] // 128):
        first = max(shift, lo) - 128 * half
        last = min(shift + 3 * C, hi) - 128 * half
        if last <= 0 or first >= 128:
            value = jnp.zeros_like(moved)
        else:
            value = jnp.where((lane >= first) & (lane < last), moved, 0.0)
        ref[row : row + C, half * 128 : (half + 1) * 128] = value.astype(BF16)


def spread_weights(both_ref, a1_ref, ab_ref, second_out):
    def columns(rows):
        wide = both_ref[rows].astype(F32)
        return jnp.concatenate([wide, jnp.zeros((C, 896 - wide.shape[1]), F32)], axis=1)

    def transposed(wide):
        return jnp.concatenate([wide[:, t * 128 : (t + 1) * 128].T for t in range(7)], axis=0)

    first = transposed(columns(slice(0, C)))
    second_rows = columns(slice(C, 2 * C))
    second = transposed(second_rows)
    fill = jnp.zeros((C, C), F32)
    for dx in range(3):
        for dz in range(3):
            t = 3 * dx + dz
            picks = [9 * dx + 3 * dy + dz for dy in range(3)]
            one = jnp.concatenate([first[k * C : (k + 1) * C, :] for k in picks[::-1]] + [fill], axis=1)
            two = jnp.concatenate([second[k * C : (k + 1) * C, :] for k in picks[::-1]] + [fill], axis=1)
            second_out[t] = two
            picks = [9 * (2 - dx) + 3 * dy + 2 - dz for dy in range(3)]
            back = jnp.concatenate([second_rows[:, k * C : (k + 1) * C] for k in picks] + [fill], axis=1)
            for yi in range(8):
                band(a1_ref, t * 256 + yi * C, one, (yi - 2) * C, 0, 6 * C)
            for yi in range(8):
                if yi < 6:
                    band(ab_ref, t * 256 + yi * C, back, (yi - 1) * C, C, 5 * C)
                else:
                    ab_ref[t * 256 + yi * C : t * 256 + (yi + 1) * C, :] = jnp.zeros((C, 256), BF16)


def shifted(plane, row, down):
    wide = plane.astype(F32)
    rows = wide.shape[0]
    index = lax.broadcasted_iota(jnp.int32, wide.shape, 0)
    if down:
        moved, place = pltpu.roll(wide, 1, 0), 0
    else:
        moved, place = pltpu.roll(wide, rows - 1, 0), rows - 1
    return jnp.where(index == place, row, moved).astype(BF16)


def silu_parts(value):
    s = 0.5 + 0.5 * jnp.tanh(0.5 * value)
    return value * s, s


def patch(ref, dz, x, row, last):
    rows = ref.shape[2]
    at = slice(rows - 16, rows) if last else slice(0, 16)
    tile = ref[dz, x, at, :].astype(F32)
    index = lax.broadcasted_iota(jnp.int32, tile.shape, 0)
    ref[dz, x, at, :] = jnp.where(index == (15 if last else 0), row, tile).astype(BF16)


def activate(n_recv, *refs):
    pre_ref, wide_field_ref, wide_noise_ref, low_ref, high_ref, a1_ref = refs[:6]
    recv = refs[6 : 6 + n_recv]
    hid_ref, slope_ref, xs_ref, ns_ref = refs[6 + n_recv :]
    n_field, size_z = xs_ref.shape[1], xs_ref.shape[2]
    n_noise = ns_ref.shape[1]
    size_x = n_noise - 2
    even = even_index("gz")
    recv_b = recv[1][...] if n_recv > 1 else None
    below_rows = choose(even, recv_b, recv[0][...]).astype(F32)
    above_rows = choose(even, recv[0][...], recv_b).astype(F32)
    own_low = low_ref[...].astype(F32)
    own_high = high_ref[...].astype(F32)

    gx, gy, gz = lax.axis_index("gx"), lax.axis_index("gy"), lax.axis_index("gz")
    first_x, last_x = gx == 0, gx == lax.axis_size("gx") - 1
    first_y, last_y = gy == 0, gy == lax.axis_size("gy") - 1
    first_z, last_z = gz == 0, gz == lax.axis_size("gz") - 1

    before = jnp.concatenate([below_rows[:n_field], own_high[n_field : 2 * n_field]], axis=0).astype(BF16)
    halo = jnp.concatenate([below_rows[n_field : 2 * n_field], above_rows[:n_field]], axis=0).astype(BF16)
    after = jnp.concatenate([own_low[:n_field], above_rows[n_field : 2 * n_field]], axis=0).astype(BF16)
    rows = 2 * n_field
    edge_total, row_total = None, None
    for dx in range(3):
        weight = lambda dz: a1_ref[(3 * dx + dz) * 256 : (3 * dx + dz + 1) * 256]
        first = jnp.dot(jnp.concatenate([before, halo], axis=0), weight(0), preferred_element_type=F32)
        middle = jnp.dot(halo, weight(1), preferred_element_type=F32)
        last = jnp.dot(jnp.concatenate([after, halo], axis=0), weight(2), preferred_element_type=F32)
        edge = first[:rows] + middle + last[:rows]
        row = jnp.concatenate([first[rows : rows + n_field], last[rows + n_field :]], axis=0)
        if dx:
            edge = pltpu.roll(edge, rows - dx, 0)
            row = pltpu.roll(row, rows - dx, 0)
        edge_total = edge if edge_total is None else edge_total + edge
        row_total = row if row_total is None else row_total + row

    lane = lax.broadcasted_iota(jnp.int32, (1, 256), 1)
    drop_y = ((lane < C) & first_y) | ((lane >= 5 * C) & last_y)
    edge_hidden = silu_parts(edge_total)[0]
    row = lax.broadcasted_iota(jnp.int32, edge_hidden.shape, 0)
    drop = drop_y | ((row < n_field) & first_z) | ((row >= n_field) & last_z)
    x_row = jnp.where(row < n_field, row, row - n_field)
    drop = drop | ((x_row == 0) & first_x) | ((x_row == n_noise - 1) & last_x)
    edge_hidden = jnp.where(drop, 0.0, edge_hidden).astype(BF16).astype(F32)

    index = lax.broadcasted_iota(jnp.int32, (size_z, 256), 0)
    for x in range(n_noise):
        value = pre_ref[x]
        value = value + jnp.where(index == 0, row_total[x : x + 1], 0.0)
        value = value + jnp.where(index == size_z - 1, row_total[n_field + x : n_field + x + 1], 0.0)
        hidden, s = silu_parts(value)
        gone = drop_y
        if x == 0:
            gone = gone | first_x
        if x == n_noise - 1:
            gone = gone | last_x
        hidden = jnp.where(gone, 0.0, hidden).astype(BF16)
        hid_ref[1, x] = hidden
        hid_ref[0, x] = shifted(hidden, edge_hidden[x : x + 1], True)
        hid_ref[2, x] = shifted(hidden, edge_hidden[n_field + x : n_field + x + 1], False)
        if 1 <= x <= size_x:
            slope_ref[x - 1] = s * (1.0 + value * (1.0 - s))

    xs_ref[...] = wide_field_ref[...]
    ns_ref[...] = wide_noise_ref[...]
    for x in range(n_field):
        patch(xs_ref, 0, x, below_rows[n_field + x : n_field + x + 1], False)
        patch(xs_ref, 2, x, above_rows[x : x + 1], True)
    base = 2 * n_field
    for x in range(n_noise):
        patch(ns_ref, 0, x, below_rows[base + x : base + x + 1], False)
        patch(ns_ref, 2, x, above_rows[base + x : base + x + 1], True)


def backward(ns_ref, slope_ref, ab_ref, out_ref, acc_ref):
    size_x, size_z = slope_ref.shape[:2]
    total = jnp.dot(taps(ns_ref, size_x), ab_ref[...], preferred_element_type=F32)
    acc_ref[...] = total.reshape(size_x, size_z, 256)
    for x in range(size_x):
        value = (acc_ref[x] * slope_ref[x]).astype(BF16)
        rows = jnp.concatenate([value[:, :128].T, value[:, 128:].T], axis=0)
        out_ref[:, x * size_z : (x + 1) * size_z] = rows[C : 5 * C, :]


def collect(left, ref, size_x, skip, offset):
    tiles = [jnp.zeros((C, 128), F32) for _ in range(7)]
    lanes = lax.broadcasted_iota(jnp.int32, (C, 128), 1)
    for dx in range(3):
        for dz in range(3):
            block = jnp.dot(left, stack(ref, dz, dx + skip, size_x), preferred_element_type=F32)
            total = None
            for y in range(4):
                part = block[y * C : (y + 1) * C, :]
                shift = (256 - (y + offset) * C) % 256
                part = pltpu.roll(part, shift, 1) if shift else part
                total = part if total is None else total + part
            total = total[:, :128]
            for dy in range(3):
                tap = 9 * dx + 3 * dy + dz
                shift = ((tap - dy) * C) % 128
                moved = pltpu.roll(total, shift, 1) if shift else total
                at = (tap % 4) * C
                tiles[tap // 4] = jnp.where((lanes >= at) & (lanes < at + C), moved, tiles[tap // 4])
    return jnp.concatenate(tiles, axis=1)


def weight_grad(give, xs_ref, hid_ref, pre_grad_ref, rows_ref, out_ref):
    size_x = rows_ref.shape[0]
    even = even_index("gz")

    @pl.when(even if give else jnp.logical_not(even))
    def _():
        noise_rows = jnp.concatenate([rows_ref[x] for x in range(size_x)], axis=1)
        out_ref[...] = collect(noise_rows, hid_ref, size_x, 0, 0)

    @pl.when(jnp.logical_not(even) if give else even)
    def _():
        out_ref[...] = collect(pre_grad_ref[...], xs_ref, size_x, 1, 1)


def predict(hid_ref, second_ref, out_ref, acc_ref, a2_ref):
    size_x, size_z = out_ref.shape[0], out_ref.shape[2]
    for t in range(9):
        for yi in range(8):
            band(a2_ref, t * 256 + yi * C, second_ref[t], (yi - 2) * C, 0, 4 * C)
    total = jnp.dot(taps(hid_ref, size_x), a2_ref[...], preferred_element_type=F32)
    acc_ref[...] = total.reshape(size_x, size_z, 128)
    for x in range(size_x):
        out_ref[x] = acc_ref[x].astype(BF16).T


def finish(norm, mine_ref, other_ref, first_ref, second_ref):
    even = even_index("gz")
    mine = mine_ref[...]
    other = other_ref[...]
    first = jnp.where(even, mine, other) * norm
    second = jnp.where(even, other, mine) * norm
    first_ref[...] = (first * first)[:, : 27 * C]
    second_ref[...] = (second * second)[:, : 27 * C]


def first_sum(keep_ref, taken_ref, send_ref):
    send_ref[...] = (keep_ref[...] + taken_ref[...]).astype(BF16)


def round_sum(own_ref, *refs):
    got, out_ref = refs[:-1], refs[-1]
    total = own_ref[...].astype(F32) + got[0][...].astype(F32)
    if len(got) == 3:
        total = total + (got[1][...].astype(F32) + got[2][...].astype(F32))
    out_ref[...] = total.astype(out_ref.dtype)


def butterfly(x, axis, bit):
    size = lax.axis_size(axis)
    return lax.ppermute(x, axis, [(i, i ^ bit) for i in range(size)])


AXES = ("gx", "gy", "gz")


def masked_swap(x, flip_even, flip_odd):
    sizes = [lax.axis_size(axis) for axis in AXES]
    pairs = []
    for gx in range(sizes[0]):
        for gy in range(sizes[1]):
            for gz in range(sizes[2]):
                at = [gx, gy, gz]
                to = list(at)
                for axis, bit in flip_odd if gz % 2 else flip_even:
                    to[AXES.index(axis)] ^= bit
                source, target = [(p[0] * sizes[1] + p[1]) * sizes[2] + p[2] for p in (at, to)]
                pairs.append((source, target))
    return lax.ppermute(x, AXES, pairs)


def local(inputs, noise, w_first, w_second):
    _, channels, size_x, size_y, size_z = inputs.shape
    cells = size_x * size_y * size_z
    devices = lax.axis_size("gx") * lax.axis_size("gy") * lax.axis_size("gz")
    norm = 1.0 / math.sqrt(cells * devices)
    lanes = size_y * channels

    def rows(x):
        return x[0].transpose(1, 2, 0, 3).reshape(size_x, lanes, size_z)

    in_rows, noise_rows = rows(inputs), rows(noise)
    plane = (size_z, lanes)
    y_sides = 2 if lax.axis_size("gy") > 2 else 1
    y_planes = size_x // 2 + size_x // 4
    field, wide_noise, *faces = call(
        functools.partial(pack_faces, y_sides),
        [struct((size_x,) + plane, BF16)] * 2
        + [struct((3,) + plane, BF16)] * 2
        + [struct((y_planes,) + plane, BF16)] * y_sides
        + [struct((160, 128), BF16)] * (2 * y_sides),
    )(in_rows, noise_rows)
    moves = [[("gx", side)] for side in range(2)]
    moves += [[("gy", side)] for side in range(y_sides)]
    moves += [[("gx", side), ("gy", k)] for k in range(y_sides) for side in range(2)]
    order = sorted(range(len(moves)), key=lambda k: (moves[k][0] == ("gx", 1), len(moves[k]), moves[k]))
    sent = {k: swap(faces[k], moves[k]) for k in order}
    got = [sent[k] for k in range(len(moves))]

    a1, ab, second = call(
        spread_weights,
        [struct((9 * 256, 256), BF16), struct((9 * 256, 256), BF16), struct((9, C, 128), F32)],
        moved=4_000_000,
    )(jnp.concatenate([w_first, w_second], axis=0))
    *got, a1, ab, second = lax.optimization_barrier((*got, a1, ab, second))

    n_field, n_noise = size_x + 4, size_x + 2
    z_rows = -(-(2 * n_field + n_noise) // 16) * 16
    low, high, face_a, face_b = call(
        functools.partial(pack_z, y_sides), [struct((z_rows, 256), BF16)] * 4
    )(field, wide_noise, *got)
    z_got = exchange(face_a, face_b, "gz")
    pre_shape = (n_noise, size_z, 256)
    xs, ns, pre = call(
        functools.partial(widen, y_sides),
        [struct((3, n_field, size_z, 256), BF16), struct((3,) + pre_shape, BF16), struct(pre_shape, F32)],
        flops=1_000_000_000,
    )(field, wide_noise, *got, a1)
    *z_got, xs, ns, pre = lax.optimization_barrier((*z_got, xs, ns, pre))

    slope_shape = (size_x, size_z, 256)
    hidden, slope, xs, ns = call(
        functools.partial(activate, len(z_got)),
        [struct((3,) + pre_shape, BF16), struct(slope_shape, F32), struct(xs.shape, BF16), struct(ns.shape, BF16)],
    )(pre, xs, ns, low, high, a1, *z_got)
    pre_grad = call(
        backward,
        struct((lanes, size_x * size_z), BF16),
        scratch=[pltpu.VMEM(slope_shape, F32)],
        flops=1_000_000_000,
    )(ns, slope, ab)

    half = struct((C, 896), F32)
    rounded = struct((C, 896), BF16)
    parts = (xs, hidden, pre_grad, noise_rows)
    give = call(functools.partial(weight_grad, True), half, flops=1_000_000_000)(*parts)
    taken = butterfly(give, "gz", 1)
    keep = call(functools.partial(weight_grad, False), half, flops=1_000_000_000)(*parts)
    send = call(first_sum, rounded)(keep, taken)

    prediction_rows = call(
        predict,
        struct((size_x, lanes, size_z), BF16),
        scratch=[pltpu.VMEM((size_x, size_z, lanes), F32), pltpu.VMEM((9 * 256, 128), BF16)],
        flops=500_000_000,
    )(hidden, second)
    prediction = prediction_rows.reshape(size_x, size_y, channels, size_z).transpose(2, 0, 1, 3)[None]

    steps = []
    for axis, start in (("gx", 1), ("gz", 2), ("gy", 1)):
        bit = start
        while bit < lax.axis_size(axis):
            steps.append((axis, bit))
            bit *= 2
    rounds = [steps[k : k + 2] for k in range(0, len(steps), 2)]
    turn = len(rounds) // 2 if len(steps) % 2 == 0 else 0
    for k, even in enumerate(rounds):
        odd = rounds[(k + turn) % len(rounds)]
        flips = [(even[:1], odd[:1])]
        if len(even) == 2:
            flips += [(even[1:], odd[1:]), (even, odd)]
        got = [masked_swap(send, *flip) for flip in flips]
        if k == 0:
            *got, prediction = lax.optimization_barrier((*got, prediction))
        send = call(round_sum, half if k == len(rounds) - 1 else rounded)(send, *got)
    mine = send
    other = butterfly(mine, "gz", 1)
    fisher_first, fisher_second = call(
        functools.partial(finish, norm), [struct((C, 27 * C), F32)] * 2
    )(mine, other)
    return prediction, fisher_first, fisher_second


def solution(mesh):
    in_specs = (P(None, None, "gx", "gy", "gz"), P(None, None, "gx", "gy", "gz"), P(), P())
    out_specs = (P(None, None, "gx", "gy", "gz"), P(), P())
    return jax.shard_map(local, mesh=mesh, in_specs=in_specs, out_specs=out_specs, check_vma=False)
```

```python
import functools
import math

import jax
import jax.numpy as jnp
from jax import lax
from jax.experimental import pallas as pl
from jax.experimental.pallas import tpu as pltpu
from jax.sharding import PartitionSpec as P

F32 = jnp.float32
BF16 = jnp.bfloat16
C = 32


def call(body, out_shapes, scratch=(), flops=1_000_000, moved=1_000_000, vmem=24, **more):
    return pl.pallas_call(
        body,
        **more,
        out_shape=out_shapes,
        scratch_shapes=list(scratch),
        compiler_params=pltpu.CompilerParams(vmem_limit_bytes=vmem * 1024 * 1024),
        cost_estimate=pl.CostEstimate(flops=flops, bytes_accessed=moved, transcendentals=0),
    )


def struct(shape, dtype):
    return jax.ShapeDtypeStruct(shape, dtype)


def even_index(axis):
    return lax.rem(lax.axis_index(axis), 2) == 0


def partner(index, side, size):
    other = index ^ 1 if side == 0 else ((index + 1) ^ 1) - 1
    return other if 0 <= other < size else None


def swap(x, moves):
    axes = ("gx", "gy")
    sizes = [lax.axis_size(axis) for axis in axes]
    side = dict(moves)
    places = [(i, j) for i in range(sizes[0]) for j in range(sizes[1])]
    target = {}
    for place in places:
        to = [partner(i, side[axis], size) if axis in side else i for i, axis, size in zip(place, axes, sizes)]
        if None not in to:
            target[place] = tuple(to)
    if not target:
        return None
    alone = [place for place in places if place not in target]
    for fill in (lambda i, j: (i, j ^ 1), lambda i, j: (i ^ 1, j), lambda i, j: (i, j)):
        if all(fill(*place) in alone for place in alone):
            target.update({place: fill(*place) for place in alone})
            break
    number = lambda place: place[0] * sizes[1] + place[1]
    return lax.ppermute(x, axes, [(number(place), number(target[place])) for place in places])


def choose(flag, a, b):
    if a is None and b is None:
        return None
    a = jnp.zeros_like(b) if a is None else a
    b = jnp.zeros_like(a) if b is None else b
    return jnp.where(flag, a, b)


def pack_faces(y_sides, in_ref, noise_ref, field_ref, wide_noise_ref, *faces):
    size_x = in_ref.shape[0]
    lanes = in_ref.shape[1]
    for x in range(size_x):
        field_ref[x] = in_ref[x].T
        wide_noise_ref[x] = noise_ref[x].T
    even_x, even_y = even_index("gx"), even_index("gy")
    face_x = faces[:2]
    face_y = faces[2 : 2 + y_sides]
    corner = faces[2 + y_sides :]

    for side in range(2):
        high = even_x if side == 0 else jnp.logical_not(even_x)
        face_x[side][0] = jnp.where(high, field_ref[size_x - 2], field_ref[0])
        face_x[side][1] = jnp.where(high, field_ref[size_x - 1], field_ref[1])
        face_x[side][2] = jnp.where(high, wide_noise_ref[size_x - 1], wide_noise_ref[0])

    for k in range(y_sides):
        high = even_y if k == 0 else jnp.logical_not(even_y)
        two = lambda p: jnp.where(high, p[:, lanes - 2 * C :], p[:, : 2 * C])
        one = lambda p: jnp.where(high, p[:, lanes - C :], p[:, :C])
        for j in range(0, size_x, 2):
            face_y[k][j // 2] = jnp.concatenate([two(field_ref[j]), two(field_ref[j + 1])], axis=1)
        for j in range(0, size_x, 4):
            face_y[k][size_x // 2 + j // 4] = jnp.concatenate([one(wide_noise_ref[j + i]) for i in range(4)], axis=1)
        for side in range(2):
            ref = corner[2 * k + side]
            ref[:128] = jnp.concatenate([two(face_x[side][0]), two(face_x[side][1])], axis=1)
            strip = one(face_x[side][2])
            ref[128:] = jnp.concatenate([strip[i * 32 : (i + 1) * 32] for i in range(4)], axis=1)


class Pieces:
    def __init__(self, y_sides, field, noise, face_x, face_y, corner):
        self.field, self.noise = field, noise
        self.size_x, self.size_z = field.shape[0], field.shape[1]
        even_x, even_y = even_index("gx"), even_index("gy")
        self.flag_x = {"below": even_x, "above": jnp.logical_not(even_x)}
        self.flag_y = {"below": even_y, "above": jnp.logical_not(even_y)}
        ends = lambda axis: (lax.axis_index(axis) == 0, lax.axis_index(axis) == lax.axis_size(axis) - 1)
        self.outside_x = dict(zip(("below", "above"), ends("gx")))
        self.outside_y = dict(zip(("below", "above"), ends("gy")))
        self.face_x = list(face_x)
        self.face_y = list(face_y) + [None] * (2 - y_sides)
        self.corner = [list(corner[2 * k : 2 * k + 2]) for k in range(y_sides)] + [[None, None]] * (2 - y_sides)

    def from_x(self, where, index, rows):
        value = choose(self.flag_x[where], self.face_x[1][index, rows], self.face_x[0][index, rows])
        return jnp.where(self.outside_x[where], jnp.zeros_like(value), value)

    def from_y(self, where, read):
        a = [None if ref is None else read(ref) for ref in self.face_y]
        value = choose(self.flag_y[where], a[1], a[0])
        return jnp.where(self.outside_y[where], jnp.zeros_like(value), value)

    def from_corner(self, where_x, where_y, read):
        a = []
        for pair in self.corner:
            if pair[0] is None:
                a.append(None)
            else:
                a.append(choose(self.flag_x[where_x], read(pair[1]), read(pair[0])))
        value = choose(self.flag_y[where_y], a[1], a[0])
        outside = self.outside_x[where_x] | self.outside_y[where_y]
        return jnp.where(outside, jnp.zeros_like(value), value)

    def side_of(self, x, width):
        if x < width:
            return "below", x
        if x >= self.size_x + width:
            return "above", x - self.size_x - width
        return "own", x - width

    def field_plane(self, x, z0, z1):
        rows = slice(z0, z1)
        where, i = self.side_of(x, 2)
        if where == "own":
            middle = self.field[i, rows]
            read = lambda ref: ref[i // 2, rows, (i % 2) * 2 * C : (i % 2 + 1) * 2 * C]
            low, high = self.from_y("below", read), self.from_y("above", read)
        else:
            middle = self.from_x(where, i, rows)
            read = lambda ref: ref[rows, i * 2 * C : (i + 1) * 2 * C]
            low, high = self.from_corner(where, "below", read), self.from_corner(where, "above", read)
        return jnp.concatenate([low, middle, high], axis=1)

    def noise_plane(self, x, z0, z1):
        rows = slice(z0, z1)
        where, i = self.side_of(x, 1)
        if where == "own":
            middle = self.noise[i, rows]
            read = lambda ref: ref[self.size_x // 2 + i // 4, rows, (i % 4) * C : (i % 4 + 1) * C]
            low, high = self.from_y("below", read), self.from_y("above", read)
        else:
            middle = self.from_x(where, 2, rows)

            def read(ref):
                parts = []
                for b in range(4):
                    first, last = max(z0, b * 32), min(z1, (b + 1) * 32)
                    if first < last:
                        parts.append(ref[128 + first - b * 32 : 128 + last - b * 32, b * C : (b + 1) * C])
                return jnp.concatenate(parts, axis=0) if len(parts) > 1 else parts[0]

            low, high = self.from_corner(where, "below", read), self.from_corner(where, "above", read)
        return jnp.concatenate([low, middle, high, jnp.zeros((z1 - z0, 2 * C), BF16)], axis=1)


def take_pieces(y_sides, refs):
    n = 4 + 3 * y_sides
    return Pieces(y_sides, refs[0], refs[1], refs[2:4], refs[4 : 4 + y_sides], refs[4 + y_sides : n]), refs[n:]


def pack_z(y_sides, *refs):
    pieces, (low_out, high_out, middle_out) = take_pieces(y_sides, refs)
    n_field, n_noise, size_z = pieces.size_x + 4, pieces.size_x + 2, pieces.size_z

    def gather(tile, first, noise_row):
        planes = [pieces.field_plane(x, tile, tile + 16).astype(F32) for x in range(n_field)]
        rows = [plane[first + k - tile : first + k - tile + 1] for k in range(2) for plane in planes]
        for x in range(n_noise):
            rows.append(pieces.noise_plane(x, tile, tile + 16).astype(F32)[noise_row - tile : noise_row - tile + 1])
        while len(rows) % 16:
            rows.append(jnp.zeros_like(rows[0]))
        return jnp.concatenate(rows, axis=0).astype(BF16)

    low = gather(0, 0, 0)
    high = gather(size_z - 16, size_z - 2, size_z - 1)
    low_out[...] = low
    high_out[...] = high
    middle_out[...] = jnp.where(lax.axis_index("gz") == 1, high, low)


def pack_pair(low_ref, high_ref, passed_ref, out_ref):
    out_ref[0] = jnp.where(even_index("gz"), high_ref[...], low_ref[...])
    out_ref[1] = passed_ref[...]


def stack(ref, dz, first, count):
    return ref[dz, first : first + count].reshape(count * ref.shape[2], 256)


def taps(ref, count):
    return jnp.concatenate([stack(ref, dz, dx, count) for dx in range(3) for dz in range(3)], axis=1)


def widen(y_sides, *refs):
    pieces, (a1_ref, xs_ref, ns_ref, pre_ref) = take_pieces(y_sides, refs)
    size_z = pieces.size_z
    for ref, read in ((xs_ref, pieces.field_plane), (ns_ref, pieces.noise_plane)):
        for x in range(ref.shape[1]):
            plane = read(x, 0, size_z)
            ref[1, x] = plane
            ref[0, x] = shifted(plane, 0.0, True)
            ref[2, x] = shifted(plane, 0.0, False)
    n_noise = pre_ref.shape[0]
    total = jnp.dot(taps(xs_ref, n_noise), a1_ref[...], preferred_element_type=F32)
    pre_ref[...] = total.reshape(n_noise, size_z, 256)


def band(ref, row, taps, shift, lo, hi):
    moved = pltpu.roll(taps, shift % 128, 1) if shift % 128 else taps
    lane = lax.broadcasted_iota(jnp.int32, moved.shape, 1)
    for half in range(ref.shape[1] // 128):
        first = max(shift, lo) - 128 * half
        last = min(shift + 3 * C, hi) - 128 * half
        if last <= 0 or first >= 128:
            value = jnp.zeros_like(moved)
        else:
            value = jnp.where((lane >= first) & (lane < last), moved, 0.0)
        ref[row : row + C, half * 128 : (half + 1) * 128] = value.astype(BF16)


def spread_weights(both_ref, a1_ref, ab_ref, second_out):
    def columns(rows):
        wide = both_ref[rows].astype(F32)
        return jnp.concatenate([wide, jnp.zeros((C, 896 - wide.shape[1]), F32)], axis=1)

    def transposed(wide):
        return jnp.concatenate([wide[:, t * 128 : (t + 1) * 128].T for t in range(7)], axis=0)

    first = transposed(columns(slice(0, C)))
    second_rows = columns(slice(C, 2 * C))
    second = transposed(second_rows)
    fill = jnp.zeros((C, C), F32)
    for dx in range(3):
        for dz in range(3):
            t = 3 * dx + dz
            picks = [9 * dx + 3 * dy + dz for dy in range(3)]
            one = jnp.concatenate([first[k * C : (k + 1) * C, :] for k in picks[::-1]] + [fill], axis=1)
            two = jnp.concatenate([second[k * C : (k + 1) * C, :] for k in picks[::-1]] + [fill], axis=1)
            second_out[t] = two
            picks = [9 * (2 - dx) + 3 * dy + 2 - dz for dy in range(3)]
            back = jnp.concatenate([second_rows[:, k * C : (k + 1) * C] for k in picks] + [fill], axis=1)
            for yi in range(8):
                band(a1_ref, t * 256 + yi * C, one, (yi - 2) * C, 0, 6 * C)
            for yi in range(8):
                if yi < 6:
                    band(ab_ref, t * 256 + yi * C, back, (yi - 1) * C, C, 5 * C)
                else:
                    ab_ref[t * 256 + yi * C : t * 256 + (yi + 1) * C, :] = jnp.zeros((C, 256), BF16)


def shifted(plane, row, down):
    wide = plane.astype(F32)
    rows = wide.shape[0]
    index = lax.broadcasted_iota(jnp.int32, wide.shape, 0)
    if down:
        moved, place = pltpu.roll(wide, 1, 0), 0
    else:
        moved, place = pltpu.roll(wide, rows - 1, 0), rows - 1
    return jnp.where(index == place, row, moved).astype(BF16)


def silu_parts(value):
    s = 0.5 + 0.5 * jnp.tanh(0.5 * value)
    return value * s, s


def patch(ref, dz, x, row, last):
    rows = ref.shape[2]
    at = slice(rows - 16, rows) if last else slice(0, 16)
    tile = ref[dz, x, at, :].astype(F32)
    index = lax.broadcasted_iota(jnp.int32, tile.shape, 0)
    ref[dz, x, at, :] = jnp.where(index == (15 if last else 0), row, tile).astype(BF16)


def activate(
    pre_ref, wide_field_ref, wide_noise_ref, low_ref, high_ref, a1_ref, recv_ref, hid_ref, slope_ref, xs_ref, ns_ref
):
    n_field, size_z = xs_ref.shape[1], xs_ref.shape[2]
    n_noise = ns_ref.shape[1]
    size_x = n_noise - 2
    even = even_index("gz")
    near, far = recv_ref[0].astype(F32), recv_ref[1].astype(F32)
    index = lax.axis_index("gz")
    below_rows = jnp.where(even, jnp.where(index == 2, far, 0.0), near)
    above_rows = jnp.where(even, near, jnp.where(index == 1, far, 0.0))
    own_low = low_ref[...].astype(F32)
    own_high = high_ref[...].astype(F32)

    gx, gy, gz = lax.axis_index("gx"), lax.axis_index("gy"), lax.axis_index("gz")
    first_x, last_x = gx == 0, gx == lax.axis_size("gx") - 1
    first_y, last_y = gy == 0, gy == lax.axis_size("gy") - 1
    first_z, last_z = gz == 0, gz == lax.axis_size("gz") - 1

    before = jnp.concatenate([below_rows[:n_field], own_high[n_field : 2 * n_field]], axis=0).astype(BF16)
    halo = jnp.concatenate([below_rows[n_field : 2 * n_field], above_rows[:n_field]], axis=0).astype(BF16)
    after = jnp.concatenate([own_low[:n_field], above_rows[n_field : 2 * n_field]], axis=0).astype(BF16)
    rows = 2 * n_field
    edge_total, row_total = None, None
    for dx in range(3):
        weight = lambda dz: a1_ref[(3 * dx + dz) * 256 : (3 * dx + dz + 1) * 256]
        first = jnp.dot(jnp.concatenate([before, halo], axis=0), weight(0), preferred_element_type=F32)
        middle = jnp.dot(halo, weight(1), preferred_element_type=F32)
        last = jnp.dot(jnp.concatenate([after, halo], axis=0), weight(2), preferred_element_type=F32)
        edge = first[:rows] + middle + last[:rows]
        row = jnp.concatenate([first[rows : rows + n_field], last[rows + n_field :]], axis=0)
        if dx:
            edge = pltpu.roll(edge, rows - dx, 0)
            row = pltpu.roll(row, rows - dx, 0)
        edge_total = edge if edge_total is None else edge_total + edge
        row_total = row if row_total is None else row_total + row

    lane = lax.broadcasted_iota(jnp.int32, (1, 256), 1)
    drop_y = ((lane < C) & first_y) | ((lane >= 5 * C) & last_y)
    edge_hidden = silu_parts(edge_total)[0]
    row = lax.broadcasted_iota(jnp.int32, edge_hidden.shape, 0)
    drop = drop_y | ((row < n_field) & first_z) | ((row >= n_field) & last_z)
    x_row = jnp.where(row < n_field, row, row - n_field)
    drop = drop | ((x_row == 0) & first_x) | ((x_row == n_noise - 1) & last_x)
    edge_hidden = jnp.where(drop, 0.0, edge_hidden).astype(BF16).astype(F32)

    row = lax.broadcasted_iota(jnp.int32, (size_z, 256), 0)
    for x in range(n_noise):
        value = pre_ref[x]
        value = value + jnp.where(row == 0, row_total[x : x + 1], 0.0)
        value = value + jnp.where(row == size_z - 1, row_total[n_field + x : n_field + x + 1], 0.0)
        hidden, s = silu_parts(value)
        gone = drop_y
        if x == 0:
            gone = gone | first_x
        if x == n_noise - 1:
            gone = gone | last_x
        hidden = jnp.where(gone, 0.0, hidden).astype(BF16)
        hid_ref[1, x] = hidden
        hid_ref[0, x] = shifted(hidden, edge_hidden[x : x + 1], True)
        hid_ref[2, x] = shifted(hidden, edge_hidden[n_field + x : n_field + x + 1], False)
        if 1 <= x <= size_x:
            slope_ref[x - 1] = s * (1.0 + value * (1.0 - s))

    xs_ref[...] = wide_field_ref[...]
    ns_ref[...] = wide_noise_ref[...]
    for x in range(n_field):
        patch(xs_ref, 0, x, below_rows[n_field + x : n_field + x + 1], False)
        patch(xs_ref, 2, x, above_rows[x : x + 1], True)
    base = 2 * n_field
    for x in range(n_noise):
        patch(ns_ref, 0, x, below_rows[base + x : base + x + 1], False)
        patch(ns_ref, 2, x, above_rows[base + x : base + x + 1], True)


def backward(ns_ref, slope_ref, ab_ref, out_ref, acc_ref):
    size_x, size_z = slope_ref.shape[:2]
    total = jnp.dot(taps(ns_ref, size_x), ab_ref[...], preferred_element_type=F32)
    acc_ref[...] = total.reshape(size_x, size_z, 256)
    for x in range(size_x):
        value = (acc_ref[x] * slope_ref[x]).astype(BF16)
        rows = jnp.concatenate([value[:, :128].T, value[:, 128:].T], axis=0)
        out_ref[:, x * size_z : (x + 1) * size_z] = rows[C : 5 * C, :]


def collect(left, ref, size_x, skip, offset):
    tiles = [jnp.zeros((C, 128), F32) for _ in range(7)]
    lanes = lax.broadcasted_iota(jnp.int32, (C, 128), 1)
    for dx in range(3):
        for dz in range(3):
            block = jnp.dot(left, stack(ref, dz, dx + skip, size_x), preferred_element_type=F32)
            total = None
            for y in range(4):
                part = block[y * C : (y + 1) * C, :]
                shift = (256 - (y + offset) * C) % 256
                part = pltpu.roll(part, shift, 1) if shift else part
                total = part if total is None else total + part
            total = total[:, :128]
            for dy in range(3):
                tap = 9 * dx + 3 * dy + dz
                shift = ((tap - dy) * C) % 128
                moved = pltpu.roll(total, shift, 1) if shift else total
                at = (tap % 4) * C
                tiles[tap // 4] = jnp.where((lanes >= at) & (lanes < at + C), moved, tiles[tap // 4])
    return jnp.concatenate(tiles, axis=1)


def weight_grad(give, xs_ref, hid_ref, pre_grad_ref, rows_ref, out_ref):
    size_x = rows_ref.shape[0]
    even = even_index("gz")

    @pl.when(even if give else jnp.logical_not(even))
    def _():
        noise_rows = jnp.concatenate([rows_ref[x] for x in range(size_x)], axis=1)
        out_ref[...] = collect(noise_rows, hid_ref, size_x, 0, 0)

    @pl.when(jnp.logical_not(even) if give else even)
    def _():
        out_ref[...] = collect(pre_grad_ref[...], xs_ref, size_x, 1, 1)


def predict(hid_ref, second_ref, out_ref, acc_ref, a2_ref):
    size_x, size_z = out_ref.shape[0], out_ref.shape[2]
    for t in range(9):
        for yi in range(8):
            band(a2_ref, t * 256 + yi * C, second_ref[t], (yi - 2) * C, 0, 4 * C)
    total = jnp.dot(taps(hid_ref, size_x), a2_ref[...], preferred_element_type=F32)
    acc_ref[...] = total.reshape(size_x, size_z, 128)
    for x in range(size_x):
        out_ref[x] = acc_ref[x].astype(BF16).T


def finish(norm, mine_ref, other_ref, first_ref, second_ref):
    even = even_index("gz")
    mine = mine_ref[...]
    other = other_ref[...]
    first = jnp.where(even, mine, other) * norm
    second = jnp.where(even, other, mine) * norm
    first_ref[...] = (first * first)[:, : 27 * C]
    second_ref[...] = (second * second)[:, : 27 * C]


def first_sum(keep_ref, taken_ref, send_ref):
    send_ref[...] = (keep_ref[...] + taken_ref[...]).astype(BF16)


def round_sum(own_ref, *refs):
    got, out_ref = refs[:-1], refs[-1]
    total = own_ref[...].astype(F32) + got[0][...].astype(F32)
    if len(got) == 3:
        total = total + (got[1][...].astype(F32) + got[2][...].astype(F32))
    out_ref[...] = total.astype(out_ref.dtype)


def flip(x, axis, bit):
    size = lax.axis_size(axis)
    return lax.ppermute(x, axis, [(i, i ^ bit) for i in range(size)])


AXES = ("gx", "gy", "gz")


def masked_swap(x, flip_even, flip_odd):
    sizes = [lax.axis_size(axis) for axis in AXES]
    pairs = []
    for gx in range(sizes[0]):
        for gy in range(sizes[1]):
            for gz in range(sizes[2]):
                at = [gx, gy, gz]
                to = list(at)
                for axis, bit in flip_odd if gz % 2 else flip_even:
                    to[AXES.index(axis)] ^= bit
                source, target = [(p[0] * sizes[1] + p[1]) * sizes[2] + p[2] for p in (at, to)]
                pairs.append((source, target))
    return lax.ppermute(x, AXES, pairs)


def local(inputs, noise, w_first, w_second):
    _, channels, size_x, size_y, size_z = inputs.shape
    cells = size_x * size_y * size_z
    devices = lax.axis_size("gx") * lax.axis_size("gy") * lax.axis_size("gz")
    norm = 1.0 / math.sqrt(cells * devices)
    lanes = size_y * channels

    def rows(x):
        return x[0].transpose(1, 2, 0, 3).reshape(size_x, lanes, size_z)

    in_rows, noise_rows = rows(inputs), rows(noise)
    plane = (size_z, lanes)
    y_sides = 2 if lax.axis_size("gy") > 2 else 1
    y_planes = size_x // 2 + size_x // 4
    field, wide_noise, *faces = call(
        functools.partial(pack_faces, y_sides),
        [struct((size_x,) + plane, BF16)] * 2
        + [struct((3,) + plane, BF16)] * 2
        + [struct((y_planes,) + plane, BF16)] * y_sides
        + [struct((160, 128), BF16)] * (2 * y_sides),
    )(in_rows, noise_rows)
    moves = [[("gx", side)] for side in range(2)]
    moves += [[("gy", side)] for side in range(y_sides)]
    moves += [[("gx", side), ("gy", k)] for k in range(y_sides) for side in range(2)]
    both = jnp.concatenate([w_first, w_second], axis=0)
    near = 2 + y_sides
    *faces[near:], both = lax.optimization_barrier((*faces[near:], both))
    got = [swap(face, move) for face, move in zip(faces, moves)]

    a1, ab, second = call(
        spread_weights,
        [struct((9 * 256, 256), BF16), struct((9 * 256, 256), BF16), struct((9, C, 128), F32)],
        moved=4_000_000,
    )(both)
    *got, a1, ab, second = lax.optimization_barrier((*got, a1, ab, second))

    n_field, n_noise = size_x + 4, size_x + 2
    z_rows = -(-(2 * n_field + n_noise) // 16) * 16
    low, high, middle = call(
        functools.partial(pack_z, y_sides), [struct((z_rows, 256), BF16)] * 3
    )(field, wide_noise, *got)
    passed = flip(middle, "gz", 2)
    pre_shape = (n_noise, size_z, 256)
    xs, ns, pre = call(
        functools.partial(widen, y_sides),
        [struct((3, n_field, size_z, 256), BF16), struct((3,) + pre_shape, BF16), struct(pre_shape, F32)],
        flops=1_000_000_000,
    )(field, wide_noise, *got, a1)
    passed, xs, ns, pre = lax.optimization_barrier((passed, xs, ns, pre))
    z_got = flip(call(pack_pair, struct((2, z_rows, 256), BF16))(low, high, passed), "gz", 1)

    slope_shape = (size_x, size_z, 256)
    hidden, slope, xs, ns = call(
        activate,
        [struct((3,) + pre_shape, BF16), struct(slope_shape, F32), struct(xs.shape, BF16), struct(ns.shape, BF16)],
    )(pre, xs, ns, low, high, a1, z_got)
    pre_grad = call(
        backward,
        struct((lanes, size_x * size_z), BF16),
        scratch=[pltpu.VMEM(slope_shape, F32)],
        flops=1_000_000_000,
    )(ns, slope, ab)

    half = struct((C, 896), F32)
    rounded = struct((C, 896), BF16)
    parts = (xs, hidden, pre_grad, noise_rows)
    give = call(functools.partial(weight_grad, True), half, flops=1_000_000_000)(*parts)
    taken = flip(give, "gz", 1)
    keep = call(functools.partial(weight_grad, False), half, flops=1_000_000_000)(*parts)
    send = call(first_sum, rounded)(keep, taken)

    prediction_rows = call(
        predict,
        struct((size_x, lanes, size_z), BF16),
        scratch=[pltpu.VMEM((size_x, size_z, lanes), F32), pltpu.VMEM((9 * 256, 128), BF16)],
        flops=500_000_000,
    )(hidden, second)
    prediction = prediction_rows.reshape(size_x, size_y, channels, size_z).transpose(2, 0, 1, 3)[None]

    steps = []
    for axis, start in (("gx", 1), ("gz", 2), ("gy", 1)):
        bit = start
        while bit < lax.axis_size(axis):
            steps.append((axis, bit))
            bit *= 2
    rounds = [steps[k : k + 2] for k in range(0, len(steps), 2)]
    turn = len(rounds) // 2 if len(steps) % 2 == 0 else 0
    for k, even in enumerate(rounds):
        odd = rounds[(k + turn) % len(rounds)]
        flips = [(even[:1], odd[:1])]
        if len(even) == 2:
            flips += [(even[1:], odd[1:]), (even, odd)]
        got = [masked_swap(send, *pair) for pair in flips]
        if k == 0:
            *got, prediction = lax.optimization_barrier((*got, prediction))
        send = call(round_sum, half if k == len(rounds) - 1 else rounded)(send, *got)
    mine = send
    other = flip(mine, "gz", 1)
    fisher_first, fisher_second = call(
        functools.partial(finish, norm), [struct((C, 27 * C), F32)] * 2
    )(mine, other)
    return prediction, fisher_first, fisher_second


def solution(mesh):
    in_specs = (P(None, None, "gx", "gy", "gz"), P(None, None, "gx", "gy", "gz"), P(), P())
    out_specs = (P(None, None, "gx", "gy", "gz"), P(), P())
    return jax.shard_map(local, mesh=mesh, in_specs=in_specs, out_specs=out_specs, check_vma=False)
```

```python
import functools
import math

import jax
import jax.numpy as jnp
from jax import lax
from jax.experimental import pallas as pl
from jax.experimental.pallas import tpu as pltpu
from jax.sharding import PartitionSpec as P

F32 = jnp.float32
BF16 = jnp.bfloat16
C = 32


def call(body, out_shapes, scratch=(), flops=1_000_000, moved=1_000_000, vmem=24, **more):
    return pl.pallas_call(
        body,
        **more,
        out_shape=out_shapes,
        scratch_shapes=list(scratch),
        compiler_params=pltpu.CompilerParams(vmem_limit_bytes=vmem * 1024 * 1024),
        cost_estimate=pl.CostEstimate(flops=flops, bytes_accessed=moved, transcendentals=0),
    )


def struct(shape, dtype):
    return jax.ShapeDtypeStruct(shape, dtype)


def even_index(axis):
    return lax.rem(lax.axis_index(axis), 2) == 0


def partner(index, side, size):
    other = index ^ 1 if side == 0 else ((index + 1) ^ 1) - 1
    return other if 0 <= other < size else None


AXES = ("gx", "gy", "gz")


def all_places():
    sizes = [lax.axis_size(axis) for axis in AXES]
    return [(i, j, k) for i in range(sizes[0]) for j in range(sizes[1]) for k in range(sizes[2])]


def permute(x, target):
    sizes = [lax.axis_size(axis) for axis in AXES]
    number = lambda place: (place[0] * sizes[1] + place[1]) * sizes[2] + place[2]
    return lax.ppermute(x, AXES, [(number(place), number(to)) for place, to in target.items()])


def swap(x, moves):
    sizes = [lax.axis_size(axis) for axis in AXES]
    side = dict(moves)
    places = all_places()
    target = {}
    for place in places:
        to = [partner(i, side[axis], size) if axis in side else i for i, axis, size in zip(place, AXES, sizes)]
        if None not in to:
            target[place] = tuple(to)
    if not target:
        return None
    alone = [place for place in places if place not in target]
    fills = (
        lambda i, j, k: (i, j, k ^ 2),
        lambda i, j, k: (i, j ^ 1, k),
        lambda i, j, k: (i ^ 1, j, k),
        lambda i, j, k: (i, j, k),
    )
    for fill in fills:
        if all(fill(*place) in alone for place in alone):
            target.update({place: fill(*place) for place in alone})
            break
    return permute(x, target)


def choose(flag, a, b):
    if a is None and b is None:
        return None
    a = jnp.zeros_like(b) if a is None else a
    b = jnp.zeros_like(a) if b is None else b
    return jnp.where(flag, a, b)


def pack_faces(y_sides, raw_ref, noise_rows_ref, field_ref, wide_noise_ref, *face_y):
    size_x, size_z = raw_ref.shape[2], raw_ref.shape[4]
    lanes = raw_ref.shape[1] * raw_ref.shape[3]
    for x in range(size_x):
        for a, ref in enumerate((field_ref, wide_noise_ref)):
            rows = jnp.transpose(raw_ref[a, :, x].astype(F32), (1, 0, 2)).reshape(lanes, size_z).astype(BF16)
            if a:
                noise_rows_ref[x] = rows
            ref[x] = rows.T
    even_y = even_index("gy")
    for k in range(y_sides):
        two, one = cut_y(even_y if k == 0 else jnp.logical_not(even_y))
        for j in range(0, size_x, 2):
            face_y[k][j // 2] = jnp.concatenate([two(field_ref[j]), two(field_ref[j + 1])], axis=1)
        for j in range(0, size_x, 4):
            face_y[k][size_x // 2 + j // 4] = jnp.concatenate([one(wide_noise_ref[j + i]) for i in range(4)], axis=1)


def cut_y(high):
    two = lambda p: jnp.where(high, p[:, p.shape[1] - 2 * C :], p[:, : 2 * C])
    one = lambda p: jnp.where(high, p[:, p.shape[1] - C :], p[:, :C])
    return two, one


def pack_corners(y_sides, field_ref, wide_noise_ref, token_ref, *faces):
    token_ref[...] = jnp.zeros_like(token_ref)
    even_x, even_y = even_index("gx"), even_index("gy")
    size_x = field_ref.shape[0]
    face_x, corners = faces[:2], faces[2:]
    for side in range(2):
        high = even_x if side == 0 else jnp.logical_not(even_x)
        face_x[side][0] = jnp.where(high, field_ref[size_x - 2], field_ref[0])
        face_x[side][1] = jnp.where(high, field_ref[size_x - 1], field_ref[1])
        face_x[side][2] = jnp.where(high, wide_noise_ref[size_x - 1], wide_noise_ref[0])
    for k in range(y_sides):
        two, one = cut_y(even_y if k == 0 else jnp.logical_not(even_y))
        for side, face in enumerate(face_x):
            ref = corners[2 * k + side]
            ref[:128] = jnp.concatenate([two(face[0]), two(face[1])], axis=1)
            strip = one(face[2])
            ref[128:] = jnp.concatenate([strip[i * 32 : (i + 1) * 32] for i in range(4)], axis=1)


class Pieces:
    def __init__(self, y_sides, field, noise, face_x, face_y, corner):
        self.field, self.noise = field, noise
        self.size_x, self.size_z = field.shape[0], field.shape[1]
        even_x, even_y = even_index("gx"), even_index("gy")
        self.flag_x = {"below": even_x, "above": jnp.logical_not(even_x)}
        self.flag_y = {"below": even_y, "above": jnp.logical_not(even_y)}
        ends = lambda axis: (lax.axis_index(axis) == 0, lax.axis_index(axis) == lax.axis_size(axis) - 1)
        self.outside_x = dict(zip(("below", "above"), ends("gx")))
        self.outside_y = dict(zip(("below", "above"), ends("gy")))
        self.face_x = list(face_x)
        self.face_y = list(face_y) + [None] * (2 - y_sides)
        self.corner = [list(corner[2 * k : 2 * k + 2]) for k in range(y_sides)] + [[None, None]] * (2 - y_sides)

    def from_x(self, where, index, rows):
        value = choose(self.flag_x[where], self.face_x[1][index, rows], self.face_x[0][index, rows])
        return jnp.where(self.outside_x[where], jnp.zeros_like(value), value)

    def from_y(self, where, read):
        a = [None if ref is None else read(ref) for ref in self.face_y]
        value = choose(self.flag_y[where], a[1], a[0])
        return jnp.where(self.outside_y[where], jnp.zeros_like(value), value)

    def from_corner(self, where_x, where_y, read):
        a = []
        for pair in self.corner:
            if pair[0] is None:
                a.append(None)
            else:
                a.append(choose(self.flag_x[where_x], read(pair[1]), read(pair[0])))
        value = choose(self.flag_y[where_y], a[1], a[0])
        outside = self.outside_x[where_x] | self.outside_y[where_y]
        return jnp.where(outside, jnp.zeros_like(value), value)

    def side_of(self, x, width):
        if x < width:
            return "below", x
        if x >= self.size_x + width:
            return "above", x - self.size_x - width
        return "own", x - width

    def field_plane(self, x, z0, z1):
        rows = slice(z0, z1)
        where, i = self.side_of(x, 2)
        if where == "own":
            middle = self.field[i, rows]
            read = lambda ref: ref[i // 2, rows, (i % 2) * 2 * C : (i % 2 + 1) * 2 * C]
            low, high = self.from_y("below", read), self.from_y("above", read)
        else:
            middle = self.from_x(where, i, rows)
            read = lambda ref: ref[rows, i * 2 * C : (i + 1) * 2 * C]
            low, high = self.from_corner(where, "below", read), self.from_corner(where, "above", read)
        return jnp.concatenate([low, middle, high], axis=1)

    def noise_plane(self, x, z0, z1):
        rows = slice(z0, z1)
        where, i = self.side_of(x, 1)
        if where == "own":
            middle = self.noise[i, rows]
            read = lambda ref: ref[self.size_x // 2 + i // 4, rows, (i % 4) * C : (i % 4 + 1) * C]
            low, high = self.from_y("below", read), self.from_y("above", read)
        else:
            middle = self.from_x(where, 2, rows)

            def read(ref):
                parts = []
                for b in range(4):
                    first, last = max(z0, b * 32), min(z1, (b + 1) * 32)
                    if first < last:
                        parts.append(ref[128 + first - b * 32 : 128 + last - b * 32, b * C : (b + 1) * C])
                return jnp.concatenate(parts, axis=0) if len(parts) > 1 else parts[0]

            low, high = self.from_corner(where, "below", read), self.from_corner(where, "above", read)
        return jnp.concatenate([low, middle, high, jnp.zeros((z1 - z0, 2 * C), BF16)], axis=1)


def take_pieces(y_sides, refs):
    n = 4 + 3 * y_sides
    return Pieces(y_sides, refs[0], refs[1], refs[2:4], refs[4 : 4 + y_sides], refs[4 + y_sides : n]), refs[n:]


def pack_z(y_sides, *refs):
    pieces, (low_out, high_out, face_a, face_b) = take_pieces(y_sides, refs)
    n_field, n_noise, size_z = pieces.size_x + 4, pieces.size_x + 2, pieces.size_z

    def gather(tile, first, noise_row):
        planes = [pieces.field_plane(x, tile, tile + 16).astype(F32) for x in range(n_field)]
        rows = [plane[first + k - tile : first + k - tile + 1] for k in range(2) for plane in planes]
        for x in range(n_noise):
            rows.append(pieces.noise_plane(x, tile, tile + 16).astype(F32)[noise_row - tile : noise_row - tile + 1])
        while len(rows) % 16:
            rows.append(jnp.zeros_like(rows[0]))
        return jnp.concatenate(rows, axis=0).astype(BF16)

    low = gather(0, 0, 0)
    high = gather(size_z - 16, size_z - 2, size_z - 1)
    low_out[...] = low
    high_out[...] = high
    even = even_index("gz")
    face_a[...] = jnp.where(even, high, low)
    face_b[...] = jnp.where(even, low, high)


def stack(ref, dz, first, count):
    if isinstance(ref, Edged):
        return ref.stack(dz, first, count)
    return ref[dz, first : first + count].reshape(count * ref.shape[2], 256)


def taps(ref, count):
    return jnp.concatenate([stack(ref, dz, dx, count) for dx in range(3) for dz in range(3)], axis=1)


def widen(y_sides, *refs):
    pieces, (a1_ref, xs_ref, ns_ref, pre_ref) = take_pieces(y_sides, refs)
    size_z = pieces.size_z
    for ref, read in ((xs_ref, pieces.field_plane), (ns_ref, pieces.noise_plane)):
        for x in range(ref.shape[1]):
            plane = read(x, 0, size_z)
            ref[1, x] = plane
            ref[0, x] = shifted(plane, 0.0, True)
            ref[2, x] = shifted(plane, 0.0, False)
    n_noise = pre_ref.shape[0]
    total = jnp.dot(taps(xs_ref, n_noise), a1_ref[...], preferred_element_type=F32)
    pre_ref[...] = total.reshape(n_noise, size_z, 256)


def band(ref, row, taps, shift, lo, hi):
    moved = pltpu.roll(taps, shift % 128, 1) if shift % 128 else taps
    lane = lax.broadcasted_iota(jnp.int32, moved.shape, 1)
    for half in range(ref.shape[1] // 128):
        first = max(shift, lo) - 128 * half
        last = min(shift + 3 * C, hi) - 128 * half
        if last <= 0 or first >= 128:
            value = jnp.zeros_like(moved)
        else:
            value = jnp.where((lane >= first) & (lane < last), moved, 0.0)
        ref[row : row + C, half * 128 : (half + 1) * 128] = value.astype(BF16)


def spread_weights(both_ref, _, a1_ref, ab_ref, second_out):
    def columns(rows):
        wide = both_ref[rows].astype(F32)
        return jnp.concatenate([wide, jnp.zeros((C, 896 - wide.shape[1]), F32)], axis=1)

    def transposed(wide):
        return jnp.concatenate([wide[:, t * 128 : (t + 1) * 128].T for t in range(7)], axis=0)

    first = transposed(columns(slice(0, C)))
    second_rows = columns(slice(C, 2 * C))
    second = transposed(second_rows)
    fill = jnp.zeros((C, C), F32)
    for dx in range(3):
        for dz in range(3):
            t = 3 * dx + dz
            picks = [9 * dx + 3 * dy + dz for dy in range(3)]
            one = jnp.concatenate([first[k * C : (k + 1) * C, :] for k in picks[::-1]] + [fill], axis=1)
            two = jnp.concatenate([second[k * C : (k + 1) * C, :] for k in picks[::-1]] + [fill], axis=1)
            second_out[t] = two
            picks = [9 * (2 - dx) + 3 * dy + 2 - dz for dy in range(3)]
            back = jnp.concatenate([second_rows[:, k * C : (k + 1) * C] for k in picks] + [fill], axis=1)
            for yi in range(8):
                band(a1_ref, t * 256 + yi * C, one, (yi - 2) * C, 0, 6 * C)
            for yi in range(8):
                if yi < 6:
                    band(ab_ref, t * 256 + yi * C, back, (yi - 1) * C, C, 5 * C)
                else:
                    ab_ref[t * 256 + yi * C : t * 256 + (yi + 1) * C, :] = jnp.zeros((C, 256), BF16)


def shifted(plane, row, down):
    wide = plane.astype(F32)
    rows = wide.shape[0]
    index = lax.broadcasted_iota(jnp.int32, wide.shape, 0)
    if down:
        moved, place = pltpu.roll(wide, 1, 0), 0
    else:
        moved, place = pltpu.roll(wide, rows - 1, 0), rows - 1
    return jnp.where(index == place, row, moved).astype(BF16)


def silu_parts(value):
    s = 0.5 + 0.5 * jnp.tanh(0.5 * value)
    return value * s, s


def edge_tile(ref, dz, x, row):
    rows = ref.shape[2]
    at = slice(rows - 16, rows) if dz else slice(0, 16)
    tile = ref[dz, x, at, :].astype(F32)
    index = lax.broadcasted_iota(jnp.int32, tile.shape, 0)
    return jnp.where(index == (15 if dz else 0), row, tile).astype(BF16)


class Edged:
    def __init__(self, ref, edge_ref):
        self.ref, self.edge_ref = ref, edge_ref

    def stack(self, dz, first, count):
        parts = []
        for x in range(first, first + count):
            if dz == 0:
                parts += [self.edge_ref[0, x], self.ref[0, x, 16:]]
            elif dz == 1:
                parts += [self.ref[1, x]]
            else:
                parts += [self.ref[2, x, : self.ref.shape[2] - 16], self.edge_ref[1, x]]
        return jnp.concatenate(parts, axis=0)


def activate(
    pre_ref, wide_field_ref, wide_noise_ref, low_ref, high_ref, a1_ref, side_0, side_1, hid_ref, slope_ref, xs_edge, ns_edge
):
    n_field, size_z = wide_field_ref.shape[1], wide_field_ref.shape[2]
    n_noise = wide_noise_ref.shape[1]
    size_x = n_noise - 2
    even = even_index("gz")
    own_low = low_ref[...].astype(F32)
    own_high = high_ref[...].astype(F32)

    gx, gy, gz = lax.axis_index("gx"), lax.axis_index("gy"), lax.axis_index("gz")
    first_x, last_x = gx == 0, gx == lax.axis_size("gx") - 1
    first_y, last_y = gy == 0, gy == lax.axis_size("gy") - 1
    first_z, last_z = gz == 0, gz == lax.axis_size("gz") - 1

    below_rows = jnp.where(first_z, 0.0, jnp.where(even, side_1[...], side_0[...]).astype(F32))
    above_rows = jnp.where(last_z, 0.0, jnp.where(even, side_0[...], side_1[...]).astype(F32))

    before = jnp.concatenate([below_rows[:n_field], own_high[n_field : 2 * n_field]], axis=0).astype(BF16)
    halo = jnp.concatenate([below_rows[n_field : 2 * n_field], above_rows[:n_field]], axis=0).astype(BF16)
    after = jnp.concatenate([own_low[:n_field], above_rows[n_field : 2 * n_field]], axis=0).astype(BF16)
    rows = 2 * n_field
    edge_total, row_total = None, None
    for dx in range(3):
        weight = lambda dz: a1_ref[(3 * dx + dz) * 256 : (3 * dx + dz + 1) * 256]
        first = jnp.dot(jnp.concatenate([before, halo], axis=0), weight(0), preferred_element_type=F32)
        middle = jnp.dot(halo, weight(1), preferred_element_type=F32)
        last = jnp.dot(jnp.concatenate([after, halo], axis=0), weight(2), preferred_element_type=F32)
        edge = first[:rows] + middle + last[:rows]
        row = jnp.concatenate([first[rows : rows + n_field], last[rows + n_field :]], axis=0)
        if dx:
            edge = pltpu.roll(edge, rows - dx, 0)
            row = pltpu.roll(row, rows - dx, 0)
        edge_total = edge if edge_total is None else edge_total + edge
        row_total = row if row_total is None else row_total + row

    lane = lax.broadcasted_iota(jnp.int32, (1, 256), 1)
    drop_y = ((lane < C) & first_y) | ((lane >= 5 * C) & last_y)
    edge_hidden = silu_parts(edge_total)[0]
    row = lax.broadcasted_iota(jnp.int32, edge_hidden.shape, 0)
    drop = drop_y | ((row < n_field) & first_z) | ((row >= n_field) & last_z)
    x_row = jnp.where(row < n_field, row, row - n_field)
    drop = drop | ((x_row == 0) & first_x) | ((x_row == n_noise - 1) & last_x)
    edge_hidden = jnp.where(drop, 0.0, edge_hidden).astype(BF16).astype(F32)

    row = lax.broadcasted_iota(jnp.int32, (size_z, 256), 0)
    for x in range(n_noise):
        value = pre_ref[x]
        value = value + jnp.where(row == 0, row_total[x : x + 1], 0.0)
        value = value + jnp.where(row == size_z - 1, row_total[n_field + x : n_field + x + 1], 0.0)
        hidden, s = silu_parts(value)
        gone = drop_y
        if x == 0:
            gone = gone | first_x
        if x == n_noise - 1:
            gone = gone | last_x
        hidden = jnp.where(gone, 0.0, hidden).astype(BF16)
        hid_ref[1, x] = hidden
        hid_ref[0, x] = shifted(hidden, edge_hidden[x : x + 1], True)
        hid_ref[2, x] = shifted(hidden, edge_hidden[n_field + x : n_field + x + 1], False)
        if 1 <= x <= size_x:
            slope_ref[x - 1] = s * (1.0 + value * (1.0 - s))

    for x in range(n_field):
        xs_edge[0, x] = edge_tile(wide_field_ref, 0, x, below_rows[n_field + x : n_field + x + 1])
        xs_edge[1, x] = edge_tile(wide_field_ref, 2, x, above_rows[x : x + 1])
    base = 2 * n_field
    for x in range(n_noise):
        ns_edge[0, x] = edge_tile(wide_noise_ref, 0, x, below_rows[base + x : base + x + 1])
        ns_edge[1, x] = edge_tile(wide_noise_ref, 2, x, above_rows[base + x : base + x + 1])


def backward(ns_ref, ns_edge, slope_ref, ab_ref, out_ref, acc_ref):
    size_x, size_z = slope_ref.shape[:2]
    total = jnp.dot(taps(Edged(ns_ref, ns_edge), size_x), ab_ref[...], preferred_element_type=F32)
    acc_ref[...] = total.reshape(size_x, size_z, 256)
    for x in range(size_x):
        value = (acc_ref[x] * slope_ref[x]).astype(BF16)
        rows = jnp.concatenate([value[:, :128].T, value[:, 128:].T], axis=0)
        out_ref[:, x * size_z : (x + 1) * size_z] = rows[C : 5 * C, :]


def collect(left, ref, size_x, skip, offset):
    tiles = [jnp.zeros((C, 128), F32) for _ in range(7)]
    lanes = lax.broadcasted_iota(jnp.int32, (C, 128), 1)
    for dx in range(3):
        for dz in range(3):
            block = jnp.dot(left, stack(ref, dz, dx + skip, size_x), preferred_element_type=F32)
            total = None
            for y in range(4):
                part = block[y * C : (y + 1) * C, :]
                shift = (256 - (y + offset) * C) % 256
                part = pltpu.roll(part, shift, 1) if shift else part
                total = part if total is None else total + part
            total = total[:, :128]
            for dy in range(3):
                tap = 9 * dx + 3 * dy + dz
                shift = ((tap - dy) * C) % 128
                moved = pltpu.roll(total, shift, 1) if shift else total
                at = (tap % 4) * C
                tiles[tap // 4] = jnp.where((lanes >= at) & (lanes < at + C), moved, tiles[tap // 4])
    return jnp.concatenate(tiles, axis=1)


def weight_grad(give, xs_ref, xs_edge, hid_ref, pre_grad_ref, rows_ref, out_ref):
    size_x = rows_ref.shape[0]
    even = even_index("gz")

    @pl.when(even if give else jnp.logical_not(even))
    def _():
        noise_rows = jnp.concatenate([rows_ref[x] for x in range(size_x)], axis=1)
        out_ref[...] = collect(noise_rows, hid_ref, size_x, 0, 0)

    @pl.when(jnp.logical_not(even) if give else even)
    def _():
        out_ref[...] = collect(pre_grad_ref[...], Edged(xs_ref, xs_edge), size_x, 1, 1)


def predict(hid_ref, second_ref, out_ref, acc_ref, a2_ref):
    size_x, size_z = out_ref.shape[0], out_ref.shape[2]
    for t in range(9):
        for yi in range(8):
            band(a2_ref, t * 256 + yi * C, second_ref[t], (yi - 2) * C, 0, 4 * C)
    total = jnp.dot(taps(hid_ref, size_x), a2_ref[...], preferred_element_type=F32)
    acc_ref[...] = total.reshape(size_x, size_z, 128)
    for x in range(size_x):
        out_ref[x] = acc_ref[x].astype(BF16).T


def finish(norm, mine_ref, other_ref, first_ref, second_ref):
    even = even_index("gz")
    mine = mine_ref[...]
    other = other_ref[...]
    first = jnp.where(even, mine, other) * norm
    second = jnp.where(even, other, mine) * norm
    first_ref[...] = (first * first)[:, : 27 * C]
    second_ref[...] = (second * second)[:, : 27 * C]


def first_sum(keep_ref, taken_ref, send_ref):
    send_ref[...] = (keep_ref[...] + taken_ref[...]).astype(BF16)


def round_sum(own_ref, *refs):
    got, out_ref = refs[:-1], refs[-1]
    total = own_ref[...].astype(F32) + got[0][...].astype(F32)
    if len(got) == 3:
        total = total + (got[1][...].astype(F32) + got[2][...].astype(F32))
    out_ref[...] = total.astype(out_ref.dtype)


def flip(x, axis, bit):
    size = lax.axis_size(axis)
    return lax.ppermute(x, axis, [(i, i ^ bit) for i in range(size)])


def masked_swap(x, flip_even, flip_odd):
    target = {}
    for place in all_places():
        to = list(place)
        for axis, bit in flip_odd if place[2] % 2 else flip_even:
            to[AXES.index(axis)] ^= bit
        target[place] = tuple(to)
    return permute(x, target)


def local(inputs, noise, w_first, w_second):
    _, channels, size_x, size_y, size_z = inputs.shape
    cells = size_x * size_y * size_z
    devices = lax.axis_size("gx") * lax.axis_size("gy") * lax.axis_size("gz")
    norm = 1.0 / math.sqrt(cells * devices)
    lanes = size_y * channels

    plane = (size_z, lanes)
    y_sides = 2 if lax.axis_size("gy") > 2 else 1
    y_planes = size_x // 2 + size_x // 4
    noise_rows, field, wide_noise, *face_y = call(
        functools.partial(pack_faces, y_sides),
        [struct((size_x, lanes, size_z), BF16)]
        + [struct((size_x,) + plane, BF16)] * 2
        + [struct((y_planes,) + plane, BF16)] * y_sides,
    )(jnp.concatenate([inputs, noise], axis=0))
    token, *faces = call(
        functools.partial(pack_corners, y_sides),
        [struct((8, 128), F32)]
        + [struct((3,) + plane, BF16)] * 2
        + [struct((160, 128), BF16)] * (2 * y_sides),
    )(field, wide_noise)
    faces[2:2] = face_y
    moves = [[("gx", side)] for side in range(2)]
    moves += [[("gy", side)] for side in range(y_sides)]
    moves += [[("gx", side), ("gy", k)] for k in range(y_sides) for side in range(2)]
    got = [swap(face, move) for face, move in zip(faces, moves)]

    a1, ab, second = call(
        spread_weights,
        [struct((9 * 256, 256), BF16), struct((9 * 256, 256), BF16), struct((9, C, 128), F32)],
        moved=4_000_000,
    )(jnp.concatenate([w_first, w_second], axis=0), token)
    order = [1, 0] + list(range(2, 2 + y_sides)) + list(range(2 + y_sides, len(moves)))[::-1]
    *sent, a1, ab, second = lax.optimization_barrier((*[got[k] for k in order], a1, ab, second))
    got = [sent[order.index(k)] for k in range(len(moves))]

    n_field, n_noise = size_x + 4, size_x + 2
    z_rows = -(-(2 * n_field + n_noise) // 16) * 16
    low, high, face_a, face_b = call(
        functools.partial(pack_z, y_sides), [struct((z_rows, 256), BF16)] * 4
    )(field, wide_noise, *got)
    z_got = [swap(face, [("gz", side)]) for side, face in enumerate((face_a, face_b))]
    pre_shape = (n_noise, size_z, 256)
    xs, ns, pre = call(
        functools.partial(widen, y_sides),
        [struct((3, n_field, size_z, 256), BF16), struct((3,) + pre_shape, BF16), struct(pre_shape, F32)],
        flops=1_000_000_000,
    )(field, wide_noise, *got, a1)
    *z_got, xs, ns, pre = lax.optimization_barrier((*z_got, xs, ns, pre))

    slope_shape = (size_x, size_z, 256)
    hidden, slope, xs_edge, ns_edge = call(
        activate,
        [
            struct((3,) + pre_shape, BF16),
            struct(slope_shape, F32),
            struct((2, n_field, 16, 256), BF16),
            struct((2, n_noise, 16, 256), BF16),
        ],
    )(pre, xs, ns, low, high, a1, *z_got)
    pre_grad = call(
        backward,
        struct((lanes, size_x * size_z), BF16),
        scratch=[pltpu.VMEM(slope_shape, F32)],
        flops=1_000_000_000,
    )(ns, ns_edge, slope, ab)

    half = struct((C, 896), F32)
    rounded = struct((C, 896), BF16)
    parts = (xs, xs_edge, hidden, pre_grad, noise_rows)
    give = call(functools.partial(weight_grad, True), half, flops=1_000_000_000)(*parts)
    taken = flip(give, "gz", 1)
    keep = call(functools.partial(weight_grad, False), half, flops=1_000_000_000)(*parts)
    send = call(first_sum, rounded)(keep, taken)

    prediction_rows = call(
        predict,
        struct((size_x, lanes, size_z), BF16),
        scratch=[pltpu.VMEM((size_x, size_z, lanes), F32), pltpu.VMEM((9 * 256, 128), BF16)],
        flops=500_000_000,
    )(hidden, second)
    prediction = prediction_rows.reshape(size_x, size_y, channels, size_z).transpose(2, 0, 1, 3)[None]

    steps = []
    for axis, start in (("gx", 1), ("gz", 2), ("gy", 1)):
        bit = start
        while bit < lax.axis_size(axis):
            steps.append((axis, bit))
            bit *= 2
    rounds = [steps[k : k + 2] for k in range(0, len(steps), 2)]
    turn = len(rounds) // 2 if len(steps) % 2 == 0 else 0
    for k, even in enumerate(rounds):
        odd = rounds[(k + turn) % len(rounds)]
        flips = [(even[:1], odd[:1])]
        if len(even) == 2:
            flips += [(even[1:], odd[1:]), (even, odd)]
        got = [masked_swap(send, *pair) for pair in flips]
        if k == 0:
            *got, prediction = lax.optimization_barrier((*got, prediction))
        send = call(round_sum, half if k == len(rounds) - 1 else rounded)(send, *got)
    mine = send
    other = flip(mine, "gz", 1)
    fisher_first, fisher_second = call(
        functools.partial(finish, norm), [struct((C, 27 * C), F32)] * 2
    )(mine, other)
    return prediction, fisher_first, fisher_second


def solution(mesh):
    in_specs = (P(None, None, "gx", "gy", "gz"), P(None, None, "gx", "gy", "gz"), P(), P())
    out_specs = (P(None, None, "gx", "gy", "gz"), P(), P())
    return jax.shard_map(local, mesh=mesh, in_specs=in_specs, out_specs=out_specs, check_vma=False)
```

```python
import functools
import math

import jax
import jax.numpy as jnp
from jax import lax
from jax.experimental import pallas as pl
from jax.experimental.pallas import tpu as pltpu
from jax.sharding import PartitionSpec as P

F32 = jnp.float32
BF16 = jnp.bfloat16
C = 32


def call(body, out_shapes, scratch=(), flops=1_000_000, moved=1_000_000, vmem=24, **more):
    return pl.pallas_call(
        body,
        **more,
        out_shape=out_shapes,
        scratch_shapes=list(scratch),
        compiler_params=pltpu.CompilerParams(vmem_limit_bytes=vmem * 1024 * 1024),
        cost_estimate=pl.CostEstimate(flops=flops, bytes_accessed=moved, transcendentals=0),
    )


def struct(shape, dtype):
    return jax.ShapeDtypeStruct(shape, dtype)


def even_index(axis):
    return lax.rem(lax.axis_index(axis), 2) == 0


def partner(index, side, size):
    other = index ^ 1 if side == 0 else ((index + 1) ^ 1) - 1
    return other if 0 <= other < size else None


AXES = ("gx", "gy", "gz")


def all_places():
    sizes = [lax.axis_size(axis) for axis in AXES]
    return [(i, j, k) for i in range(sizes[0]) for j in range(sizes[1]) for k in range(sizes[2])]


def permute(x, target):
    sizes = [lax.axis_size(axis) for axis in AXES]
    number = lambda place: (place[0] * sizes[1] + place[1]) * sizes[2] + place[2]
    return lax.ppermute(x, AXES, [(number(place), number(to)) for place, to in target.items()])


def swap(x, moves):
    sizes = [lax.axis_size(axis) for axis in AXES]
    side = dict(moves)
    places = all_places()
    target = {}
    for place in places:
        to = [partner(i, side[axis], size) if axis in side else i for i, axis, size in zip(place, AXES, sizes)]
        if None not in to:
            target[place] = tuple(to)
    if not target:
        return None
    alone = [place for place in places if place not in target]
    fills = (
        lambda i, j, k: (i, j, k ^ 2),
        lambda i, j, k: (i, j ^ 1, k),
        lambda i, j, k: (i ^ 1, j, k),
        lambda i, j, k: (i, j, k),
    )
    for fill in fills:
        if all(fill(*place) in alone for place in alone):
            target.update({place: fill(*place) for place in alone})
            break
    return permute(x, target)


def choose(flag, a, b):
    if a is None and b is None:
        return None
    a = jnp.zeros_like(b) if a is None else a
    b = jnp.zeros_like(a) if b is None else b
    return jnp.where(flag, a, b)


def pack_faces(y_sides, raw_ref, noise_rows_ref, field_ref, wide_noise_ref, *face_y):
    size_x, size_z = raw_ref.shape[2], raw_ref.shape[4]
    lanes = raw_ref.shape[1] * raw_ref.shape[3]
    for x in range(size_x):
        for a, ref in enumerate((field_ref, wide_noise_ref)):
            rows = jnp.transpose(raw_ref[a, :, x].astype(F32), (1, 0, 2)).reshape(lanes, size_z).astype(BF16)
            if a:
                noise_rows_ref[x] = rows
            ref[x] = rows.T
    even_y = even_index("gy")
    for k in range(y_sides):
        two, one = cut_y(even_y if k == 0 else jnp.logical_not(even_y))
        for j in range(0, size_x, 2):
            face_y[k][j // 2] = jnp.concatenate([two(field_ref[j]), two(field_ref[j + 1])], axis=1)
        for j in range(0, size_x, 4):
            face_y[k][size_x // 2 + j // 4] = jnp.concatenate([one(wide_noise_ref[j + i]) for i in range(4)], axis=1)


def cut_y(high):
    two = lambda p: jnp.where(high, p[:, p.shape[1] - 2 * C :], p[:, : 2 * C])
    one = lambda p: jnp.where(high, p[:, p.shape[1] - C :], p[:, :C])
    return two, one


def pack_corners(y_sides, field_ref, wide_noise_ref, token_ref, *faces):
    token_ref[...] = jnp.zeros_like(token_ref)
    even_x, even_y = even_index("gx"), even_index("gy")
    size_x = field_ref.shape[0]
    face_x, corners = faces[:2], faces[2:]
    for side in range(2):
        high = even_x if side == 0 else jnp.logical_not(even_x)
        face_x[side][0] = jnp.where(high, field_ref[size_x - 2], field_ref[0])
        face_x[side][1] = jnp.where(high, field_ref[size_x - 1], field_ref[1])
        face_x[side][2] = jnp.where(high, wide_noise_ref[size_x - 1], wide_noise_ref[0])
    for k in range(y_sides):
        two, one = cut_y(even_y if k == 0 else jnp.logical_not(even_y))
        for side, face in enumerate(face_x):
            ref = corners[2 * k + side]
            ref[:128] = jnp.concatenate([two(face[0]), two(face[1])], axis=1)
            strip = one(face[2])
            ref[128:] = jnp.concatenate([strip[i * 32 : (i + 1) * 32] for i in range(4)], axis=1)


class Pieces:
    def __init__(self, y_sides, field, noise, face_x, face_y, corner):
        self.field, self.noise = field, noise
        self.size_x, self.size_z = field.shape[0], field.shape[1]
        even_x, even_y = even_index("gx"), even_index("gy")
        self.flag_x = {"below": even_x, "above": jnp.logical_not(even_x)}
        self.flag_y = {"below": even_y, "above": jnp.logical_not(even_y)}
        ends = lambda axis: (lax.axis_index(axis) == 0, lax.axis_index(axis) == lax.axis_size(axis) - 1)
        self.outside_x = dict(zip(("below", "above"), ends("gx")))
        self.outside_y = dict(zip(("below", "above"), ends("gy")))
        self.face_x = list(face_x)
        self.face_y = list(face_y) + [None] * (2 - y_sides)
        self.corner = [list(corner[2 * k : 2 * k + 2]) for k in range(y_sides)] + [[None, None]] * (2 - y_sides)

    def from_x(self, where, index, rows):
        value = choose(self.flag_x[where], self.face_x[1][index, rows], self.face_x[0][index, rows])
        return jnp.where(self.outside_x[where], jnp.zeros_like(value), value)

    def from_y(self, where, read):
        a = [None if ref is None else read(ref) for ref in self.face_y]
        value = choose(self.flag_y[where], a[1], a[0])
        return jnp.where(self.outside_y[where], jnp.zeros_like(value), value)

    def from_corner(self, where_x, where_y, read):
        a = []
        for pair in self.corner:
            if pair[0] is None:
                a.append(None)
            else:
                a.append(choose(self.flag_x[where_x], read(pair[1]), read(pair[0])))
        value = choose(self.flag_y[where_y], a[1], a[0])
        outside = self.outside_x[where_x] | self.outside_y[where_y]
        return jnp.where(outside, jnp.zeros_like(value), value)

    def side_of(self, x, width):
        if x < width:
            return "below", x
        if x >= self.size_x + width:
            return "above", x - self.size_x - width
        return "own", x - width

    def field_plane(self, x, z0, z1):
        rows = slice(z0, z1)
        where, i = self.side_of(x, 2)
        if where == "own":
            middle = self.field[i, rows]
            read = lambda ref: ref[i // 2, rows, (i % 2) * 2 * C : (i % 2 + 1) * 2 * C]
            low, high = self.from_y("below", read), self.from_y("above", read)
        else:
            middle = self.from_x(where, i, rows)
            read = lambda ref: ref[rows, i * 2 * C : (i + 1) * 2 * C]
            low, high = self.from_corner(where, "below", read), self.from_corner(where, "above", read)
        return jnp.concatenate([low, middle, high], axis=1)

    def noise_plane(self, x, z0, z1):
        rows = slice(z0, z1)
        where, i = self.side_of(x, 1)
        if where == "own":
            middle = self.noise[i, rows]
            read = lambda ref: ref[self.size_x // 2 + i // 4, rows, (i % 4) * C : (i % 4 + 1) * C]
            low, high = self.from_y("below", read), self.from_y("above", read)
        else:
            middle = self.from_x(where, 2, rows)

            def read(ref):
                parts = []
                for b in range(4):
                    first, last = max(z0, b * 32), min(z1, (b + 1) * 32)
                    if first < last:
                        parts.append(ref[128 + first - b * 32 : 128 + last - b * 32, b * C : (b + 1) * C])
                return jnp.concatenate(parts, axis=0) if len(parts) > 1 else parts[0]

            low, high = self.from_corner(where, "below", read), self.from_corner(where, "above", read)
        return jnp.concatenate([low, middle, high, jnp.zeros((z1 - z0, 2 * C), BF16)], axis=1)


def take_pieces(y_sides, refs):
    n = 4 + 3 * y_sides
    return Pieces(y_sides, refs[0], refs[1], refs[2:4], refs[4 : 4 + y_sides], refs[4 + y_sides : n]), refs[n:]


def pack_z(y_sides, *refs):
    pieces, (low_out, high_out, face_a, face_b) = take_pieces(y_sides, refs)
    n_field, n_noise, size_z = pieces.size_x + 4, pieces.size_x + 2, pieces.size_z

    def gather(tile, first, noise_row):
        planes = [pieces.field_plane(x, tile, tile + 16).astype(F32) for x in range(n_field)]
        rows = [plane[first + k - tile : first + k - tile + 1] for k in range(2) for plane in planes]
        for x in range(n_noise):
            rows.append(pieces.noise_plane(x, tile, tile + 16).astype(F32)[noise_row - tile : noise_row - tile + 1])
        while len(rows) % 16:
            rows.append(jnp.zeros_like(rows[0]))
        return jnp.concatenate(rows, axis=0).astype(BF16)

    low = gather(0, 0, 0)
    high = gather(size_z - 16, size_z - 2, size_z - 1)
    low_out[...] = low
    high_out[...] = high
    even = even_index("gz")
    face_a[...] = jnp.where(even, high, low)
    face_b[...] = jnp.where(even, low, high)


def stack(ref, dz, first, count):
    if isinstance(ref, Edged):
        return ref.stack(dz, first, count)
    return ref[dz, first : first + count].reshape(count * ref.shape[2], 256)


def taps(ref, count):
    return jnp.concatenate([stack(ref, dz, dx, count) for dx in range(3) for dz in range(3)], axis=1)


def widen(y_sides, *refs):
    pieces, (a1_ref, xs_ref, ns_ref, pre_ref) = take_pieces(y_sides, refs)
    size_z = pieces.size_z
    for ref, read in ((xs_ref, pieces.field_plane), (ns_ref, pieces.noise_plane)):
        for x in range(ref.shape[1]):
            plane = read(x, 0, size_z)
            ref[1, x] = plane
            ref[0, x] = shifted(plane, 0.0, True)
            ref[2, x] = shifted(plane, 0.0, False)
    n_noise = pre_ref.shape[0]
    total = jnp.dot(taps(xs_ref, n_noise), a1_ref[...], preferred_element_type=F32)
    pre_ref[...] = total.reshape(n_noise, size_z, 256)


def band(ref, row, taps, shift, lo, hi):
    moved = pltpu.roll(taps, shift % 128, 1) if shift % 128 else taps
    lane = lax.broadcasted_iota(jnp.int32, moved.shape, 1)
    for half in range(ref.shape[1] // 128):
        first = max(shift, lo) - 128 * half
        last = min(shift + 3 * C, hi) - 128 * half
        if last <= 0 or first >= 128:
            value = jnp.zeros_like(moved)
        else:
            value = jnp.where((lane >= first) & (lane < last), moved, 0.0)
        ref[row : row + C, half * 128 : (half + 1) * 128] = value.astype(BF16)


def spread_weights(both_ref, _, a1_ref, ab_ref, second_out):
    def columns(rows):
        wide = both_ref[rows].astype(F32)
        return jnp.concatenate([wide, jnp.zeros((C, 896 - wide.shape[1]), F32)], axis=1)

    def transposed(wide):
        return jnp.concatenate([wide[:, t * 128 : (t + 1) * 128].T for t in range(7)], axis=0)

    first = transposed(columns(slice(0, C)))
    second_rows = columns(slice(C, 2 * C))
    second = transposed(second_rows)
    fill = jnp.zeros((C, C), F32)
    for dx in range(3):
        for dz in range(3):
            t = 3 * dx + dz
            picks = [9 * dx + 3 * dy + dz for dy in range(3)]
            one = jnp.concatenate([first[k * C : (k + 1) * C, :] for k in picks[::-1]] + [fill], axis=1)
            two = jnp.concatenate([second[k * C : (k + 1) * C, :] for k in picks[::-1]] + [fill], axis=1)
            second_out[t] = two
            picks = [9 * (2 - dx) + 3 * dy + 2 - dz for dy in range(3)]
            back = jnp.concatenate([second_rows[:, k * C : (k + 1) * C] for k in picks] + [fill], axis=1)
            for yi in range(8):
                band(a1_ref, t * 256 + yi * C, one, (yi - 2) * C, 0, 6 * C)
            for yi in range(8):
                if yi < 6:
                    band(ab_ref, t * 256 + yi * C, back, (yi - 1) * C, C, 5 * C)
                else:
                    ab_ref[t * 256 + yi * C : t * 256 + (yi + 1) * C, :] = jnp.zeros((C, 256), BF16)


def shifted(plane, row, down):
    wide = plane.astype(F32)
    rows = wide.shape[0]
    index = lax.broadcasted_iota(jnp.int32, wide.shape, 0)
    if down:
        moved, place = pltpu.roll(wide, 1, 0), 0
    else:
        moved, place = pltpu.roll(wide, rows - 1, 0), rows - 1
    return jnp.where(index == place, row, moved).astype(BF16)


def silu_parts(value):
    s = 0.5 + 0.5 * jnp.tanh(0.5 * value)
    return value * s, s


def edge_tile(ref, dz, x, row):
    rows = ref.shape[2]
    at = slice(rows - 16, rows) if dz else slice(0, 16)
    tile = ref[dz, x, at, :].astype(F32)
    index = lax.broadcasted_iota(jnp.int32, tile.shape, 0)
    return jnp.where(index == (15 if dz else 0), row, tile).astype(BF16)


class Edged:
    def __init__(self, ref, edge_ref):
        self.ref, self.edge_ref = ref, edge_ref

    def stack(self, dz, first, count):
        parts = []
        for x in range(first, first + count):
            if dz == 0:
                parts += [self.edge_ref[0, x], self.ref[0, x, 16:]]
            elif dz == 1:
                parts += [self.ref[1, x]]
            else:
                parts += [self.ref[2, x, : self.ref.shape[2] - 16], self.edge_ref[1, x]]
        return jnp.concatenate(parts, axis=0)


def activate(
    pre_ref, wide_field_ref, wide_noise_ref, low_ref, high_ref, a1_ref, side_0, side_1, hid_ref, slope_ref, xs_edge, ns_edge
):
    n_field, size_z = wide_field_ref.shape[1], wide_field_ref.shape[2]
    n_noise = wide_noise_ref.shape[1]
    size_x = n_noise - 2
    even = even_index("gz")
    own_low = low_ref[...].astype(F32)
    own_high = high_ref[...].astype(F32)

    gx, gy, gz = lax.axis_index("gx"), lax.axis_index("gy"), lax.axis_index("gz")
    first_x, last_x = gx == 0, gx == lax.axis_size("gx") - 1
    first_y, last_y = gy == 0, gy == lax.axis_size("gy") - 1
    first_z, last_z = gz == 0, gz == lax.axis_size("gz") - 1

    below_rows = jnp.where(first_z, 0.0, jnp.where(even, side_1[...], side_0[...]).astype(F32))
    above_rows = jnp.where(last_z, 0.0, jnp.where(even, side_0[...], side_1[...]).astype(F32))

    before = jnp.concatenate([below_rows[:n_field], own_high[n_field : 2 * n_field]], axis=0).astype(BF16)
    halo = jnp.concatenate([below_rows[n_field : 2 * n_field], above_rows[:n_field]], axis=0).astype(BF16)
    after = jnp.concatenate([own_low[:n_field], above_rows[n_field : 2 * n_field]], axis=0).astype(BF16)
    rows = 2 * n_field
    edge_total, row_total = None, None
    for dx in range(3):
        weight = lambda dz: a1_ref[(3 * dx + dz) * 256 : (3 * dx + dz + 1) * 256]
        first = jnp.dot(jnp.concatenate([before, halo], axis=0), weight(0), preferred_element_type=F32)
        middle = jnp.dot(halo, weight(1), preferred_element_type=F32)
        last = jnp.dot(jnp.concatenate([after, halo], axis=0), weight(2), preferred_element_type=F32)
        edge = first[:rows] + middle + last[:rows]
        row = jnp.concatenate([first[rows : rows + n_field], last[rows + n_field :]], axis=0)
        if dx:
            edge = pltpu.roll(edge, rows - dx, 0)
            row = pltpu.roll(row, rows - dx, 0)
        edge_total = edge if edge_total is None else edge_total + edge
        row_total = row if row_total is None else row_total + row

    lane = lax.broadcasted_iota(jnp.int32, (1, 256), 1)
    drop_y = ((lane < C) & first_y) | ((lane >= 5 * C) & last_y)
    edge_hidden = silu_parts(edge_total)[0]
    row = lax.broadcasted_iota(jnp.int32, edge_hidden.shape, 0)
    drop = drop_y | ((row < n_field) & first_z) | ((row >= n_field) & last_z)
    x_row = jnp.where(row < n_field, row, row - n_field)
    drop = drop | ((x_row == 0) & first_x) | ((x_row == n_noise - 1) & last_x)
    edge_hidden = jnp.where(drop, 0.0, edge_hidden).astype(BF16).astype(F32)

    row = lax.broadcasted_iota(jnp.int32, (size_z, 256), 0)
    for x in range(n_noise):
        value = pre_ref[x]
        value = value + jnp.where(row == 0, row_total[x : x + 1], 0.0)
        value = value + jnp.where(row == size_z - 1, row_total[n_field + x : n_field + x + 1], 0.0)
        hidden, s = silu_parts(value)
        gone = drop_y
        if x == 0:
            gone = gone | first_x
        if x == n_noise - 1:
            gone = gone | last_x
        hidden = jnp.where(gone, 0.0, hidden).astype(BF16)
        hid_ref[1, x] = hidden
        hid_ref[0, x] = shifted(hidden, edge_hidden[x : x + 1], True)
        hid_ref[2, x] = shifted(hidden, edge_hidden[n_field + x : n_field + x + 1], False)
        if 1 <= x <= size_x:
            slope_ref[x - 1] = s * (1.0 + value * (1.0 - s))

    for x in range(n_field):
        xs_edge[0, x] = edge_tile(wide_field_ref, 0, x, below_rows[n_field + x : n_field + x + 1])
        xs_edge[1, x] = edge_tile(wide_field_ref, 2, x, above_rows[x : x + 1])
    base = 2 * n_field
    for x in range(n_noise):
        ns_edge[0, x] = edge_tile(wide_noise_ref, 0, x, below_rows[base + x : base + x + 1])
        ns_edge[1, x] = edge_tile(wide_noise_ref, 2, x, above_rows[base + x : base + x + 1])


def backward(ns_ref, ns_edge, slope_ref, ab_ref, out_ref, acc_ref):
    size_x, size_z = slope_ref.shape[:2]
    total = jnp.dot(taps(Edged(ns_ref, ns_edge), size_x), ab_ref[...], preferred_element_type=F32)
    acc_ref[...] = total.reshape(size_x, size_z, 256)
    for x in range(size_x):
        value = (acc_ref[x] * slope_ref[x]).astype(BF16)
        rows = jnp.concatenate([value[:, :128].T, value[:, 128:].T], axis=0)
        out_ref[:, x * size_z : (x + 1) * size_z] = rows[C : 5 * C, :]


def collect(left, ref, size_x, skip, offset):
    tiles = [jnp.zeros((C, 128), F32) for _ in range(7)]
    lanes = lax.broadcasted_iota(jnp.int32, (C, 128), 1)
    for dx in range(3):
        for dz in range(3):
            block = jnp.dot(left, stack(ref, dz, dx + skip, size_x), preferred_element_type=F32)
            total = None
            for y in range(4):
                part = block[y * C : (y + 1) * C, :]
                shift = (256 - (y + offset) * C) % 256
                part = pltpu.roll(part, shift, 1) if shift else part
                total = part if total is None else total + part
            total = total[:, :128]
            for dy in range(3):
                tap = 9 * dx + 3 * dy + dz
                shift = ((tap - dy) * C) % 128
                moved = pltpu.roll(total, shift, 1) if shift else total
                at = (tap % 4) * C
                tiles[tap // 4] = jnp.where((lanes >= at) & (lanes < at + C), moved, tiles[tap // 4])
    return jnp.concatenate(tiles, axis=1)


def weight_grad(give, xs_ref, xs_edge, hid_ref, pre_grad_ref, rows_ref, out_ref):
    size_x = rows_ref.shape[0]
    even = even_index("gz")

    @pl.when(even if give else jnp.logical_not(even))
    def _():
        noise_rows = jnp.concatenate([rows_ref[x] for x in range(size_x)], axis=1)
        out_ref[...] = collect(noise_rows, hid_ref, size_x, 0, 0)

    @pl.when(jnp.logical_not(even) if give else even)
    def _():
        out_ref[...] = collect(pre_grad_ref[...], Edged(xs_ref, xs_edge), size_x, 1, 1)


def predict(hid_ref, second_ref, out_ref, acc_ref, a2_ref):
    size_x, size_z = out_ref.shape[0], out_ref.shape[2]
    for t in range(9):
        for yi in range(8):
            band(a2_ref, t * 256 + yi * C, second_ref[t], (yi - 2) * C, 0, 4 * C)
    total = jnp.dot(taps(hid_ref, size_x), a2_ref[...], preferred_element_type=F32)
    acc_ref[...] = total.reshape(size_x, size_z, 128)
    for x in range(size_x):
        out_ref[x] = acc_ref[x].astype(BF16).T


def finish(norm, mine_ref, other_ref, first_ref, second_ref):
    even = even_index("gz")
    mine = mine_ref[...]
    other = other_ref[...]
    first = jnp.where(even, mine, other) * norm
    second = jnp.where(even, other, mine) * norm
    first_ref[...] = (first * first)[:, : 27 * C]
    second_ref[...] = (second * second)[:, : 27 * C]


def first_sum(keep_ref, taken_ref, send_ref):
    send_ref[...] = (keep_ref[...] + taken_ref[...]).astype(BF16)


def round_sum(own_ref, *refs):
    got, out_ref = refs[:-1], refs[-1]
    total = own_ref[...].astype(F32) + got[0][...].astype(F32)
    if len(got) == 3:
        total = total + (got[1][...].astype(F32) + got[2][...].astype(F32))
    out_ref[...] = total.astype(out_ref.dtype)


def flip(x, axis, bit):
    size = lax.axis_size(axis)
    return lax.ppermute(x, axis, [(i, i ^ bit) for i in range(size)])


def masked_swap(x, flip_even, flip_odd):
    target = {}
    for place in all_places():
        to = list(place)
        for axis, bit in flip_odd if place[2] % 2 else flip_even:
            to[AXES.index(axis)] ^= bit
        target[place] = tuple(to)
    return permute(x, target)


def local(inputs, noise, w_first, w_second):
    _, channels, size_x, size_y, size_z = inputs.shape
    cells = size_x * size_y * size_z
    devices = lax.axis_size("gx") * lax.axis_size("gy") * lax.axis_size("gz")
    norm = 1.0 / math.sqrt(cells * devices)
    lanes = size_y * channels

    plane = (size_z, lanes)
    y_sides = 2 if lax.axis_size("gy") > 2 else 1
    y_planes = size_x // 2 + size_x // 4
    noise_rows, field, wide_noise, *face_y = call(
        functools.partial(pack_faces, y_sides),
        [struct((size_x, lanes, size_z), BF16)]
        + [struct((size_x,) + plane, BF16)] * 2
        + [struct((y_planes,) + plane, BF16)] * y_sides,
    )(jnp.concatenate([inputs, noise], axis=0))
    token, *faces = call(
        functools.partial(pack_corners, y_sides),
        [struct((8, 128), F32)]
        + [struct((3,) + plane, BF16)] * 2
        + [struct((160, 128), BF16)] * (2 * y_sides),
    )(field, wide_noise)
    faces[2:2] = face_y
    moves = [[("gx", side)] for side in range(2)]
    moves += [[("gy", side)] for side in range(y_sides)]
    moves += [[("gx", side), ("gy", k)] for k in range(y_sides) for side in range(2)]
    got = [swap(face, move) for face, move in zip(faces, moves)]

    a1, ab, second = call(
        spread_weights,
        [struct((9 * 256, 256), BF16), struct((9 * 256, 256), BF16), struct((9, C, 128), F32)],
        moved=4_000_000,
    )(jnp.concatenate([w_first, w_second], axis=0), token)
    order = [1, 0] + list(range(2, 2 + y_sides)) + list(range(2 + y_sides, len(moves)))[::-1]
    *sent, a1, ab, second = lax.optimization_barrier((*[got[k] for k in order], a1, ab, second))
    got = [sent[order.index(k)] for k in range(len(moves))]

    n_field, n_noise = size_x + 4, size_x + 2
    z_rows = -(-(2 * n_field + n_noise) // 16) * 16
    low, high, face_a, face_b = call(
        functools.partial(pack_z, y_sides), [struct((z_rows, 256), BF16)] * 4
    )(field, wide_noise, *got)
    z_got = [swap(face, [("gz", side)]) for side, face in enumerate((face_a, face_b))]
    pre_shape = (n_noise, size_z, 256)
    xs, ns, pre = call(
        functools.partial(widen, y_sides),
        [struct((3, n_field, size_z, 256), BF16), struct((3,) + pre_shape, BF16), struct(pre_shape, F32)],
        flops=1_000_000_000,
    )(field, wide_noise, *got, a1)
    *z_got, xs, ns, pre = lax.optimization_barrier((*z_got, xs, ns, pre))

    slope_shape = (size_x, size_z, 256)
    hidden, slope, xs_edge, ns_edge = call(
        activate,
        [
            struct((3,) + pre_shape, BF16),
            struct(slope_shape, F32),
            struct((2, n_field, 16, 256), BF16),
            struct((2, n_noise, 16, 256), BF16),
        ],
    )(pre, xs, ns, low, high, a1, *z_got)
    pre_grad = call(
        backward,
        struct((lanes, size_x * size_z), BF16),
        scratch=[pltpu.VMEM(slope_shape, F32)],
        flops=1_000_000_000,
    )(ns, ns_edge, slope, ab)

    half = struct((C, 896), F32)
    rounded = struct((C, 896), BF16)
    parts = (xs, xs_edge, hidden, pre_grad, noise_rows)
    give = call(functools.partial(weight_grad, True), half, flops=1_000_000_000)(*parts)
    taken = flip(give, "gz", 1)
    keep = call(functools.partial(weight_grad, False), half, flops=1_000_000_000)(*parts)
    send = call(first_sum, rounded)(keep, taken)

    prediction_rows = call(
        predict,
        struct((size_x, lanes, size_z), BF16),
        scratch=[pltpu.VMEM((size_x, size_z, lanes), F32), pltpu.VMEM((9 * 256, 128), BF16)],
        flops=500_000_000,
    )(hidden, second)
    prediction = prediction_rows.reshape(size_x, size_y, channels, size_z).transpose(2, 0, 1, 3)[None]

    steps = []
    for axis, start in (("gz", 2), ("gy", 1), ("gx", 1)):
        bit = start
        while bit < lax.axis_size(axis):
            steps.append((axis, bit))
            bit *= 2
    rounds = [steps[k : k + 2] for k in range(0, len(steps), 2)]
    turn = len(rounds) // 2 if len(steps) % 2 == 0 else 0
    for k, even in enumerate(rounds):
        odd = rounds[(k + turn) % len(rounds)]
        flips = [(even[:1], odd[:1])]
        if len(even) == 2:
            flips += [(even[1:], odd[1:]), (even, odd)]
        got = [masked_swap(send, *pair) for pair in flips]
        if k == 0:
            *got, prediction = lax.optimization_barrier((*got, prediction))
        send = call(round_sum, half if k == len(rounds) - 1 else rounded)(send, *got)
    mine = send
    other = flip(mine, "gz", 1)
    fisher_first, fisher_second = call(
        functools.partial(finish, norm), [struct((C, 27 * C), F32)] * 2
    )(mine, other)
    return prediction, fisher_first, fisher_second


def solution(mesh):
    in_specs = (P(None, None, "gx", "gy", "gz"), P(None, None, "gx", "gy", "gz"), P(), P())
    out_specs = (P(None, None, "gx", "gy", "gz"), P(), P())
    return jax.shard_map(local, mesh=mesh, in_specs=in_specs, out_specs=out_specs, check_vma=False)
```

```python
import functools
import math

import jax
import jax.numpy as jnp
from jax import lax
from jax.experimental import pallas as pl
from jax.experimental.pallas import tpu as pltpu
from jax.sharding import PartitionSpec as P

F32 = jnp.float32
BF16 = jnp.bfloat16
C = 32


def call(body, out_shapes, scratch=(), flops=1_000_000, moved=1_000_000, vmem=24, **more):
    return pl.pallas_call(
        body,
        **more,
        out_shape=out_shapes,
        scratch_shapes=list(scratch),
        compiler_params=pltpu.CompilerParams(vmem_limit_bytes=vmem * 1024 * 1024),
        cost_estimate=pl.CostEstimate(flops=flops, bytes_accessed=moved, transcendentals=0),
    )


def struct(shape, dtype):
    return jax.ShapeDtypeStruct(shape, dtype)


def even_index(axis):
    return lax.rem(lax.axis_index(axis), 2) == 0


def partner(index, side, size):
    other = index ^ 1 if side == 0 else ((index + 1) ^ 1) - 1
    return other if 0 <= other < size else None


AXES = ("gx", "gy", "gz")


def all_places():
    sizes = [lax.axis_size(axis) for axis in AXES]
    return [(i, j, k) for i in range(sizes[0]) for j in range(sizes[1]) for k in range(sizes[2])]


def permute(x, target):
    sizes = [lax.axis_size(axis) for axis in AXES]
    number = lambda place: (place[0] * sizes[1] + place[1]) * sizes[2] + place[2]
    return lax.ppermute(x, AXES, [(number(place), number(to)) for place, to in target.items()])


def swap(x, moves):
    sizes = [lax.axis_size(axis) for axis in AXES]
    side = dict(moves)
    places = all_places()
    target = {}
    for place in places:
        to = [partner(i, side[axis], size) if axis in side else i for i, axis, size in zip(place, AXES, sizes)]
        if None not in to:
            target[place] = tuple(to)
    if not target:
        return None
    alone = [place for place in places if place not in target]
    fills = (
        lambda i, j, k: (i, j, k ^ 2),
        lambda i, j, k: (i, j ^ 1, k),
        lambda i, j, k: (i ^ 1, j, k),
        lambda i, j, k: (i, j, k),
    )
    for fill in fills:
        if all(fill(*place) in alone for place in alone):
            target.update({place: fill(*place) for place in alone})
            break
    return permute(x, target)


def choose(flag, a, b):
    if a is None and b is None:
        return None
    a = jnp.zeros_like(b) if a is None else a
    b = jnp.zeros_like(a) if b is None else b
    return jnp.where(flag, a, b)


def pack_faces(y_sides, raw_ref, noise_rows_ref, field_ref, wide_noise_ref, *faces):
    size_x, size_z = raw_ref.shape[2], raw_ref.shape[4]
    lanes = raw_ref.shape[1] * raw_ref.shape[3]
    for x in range(size_x):
        for a, ref in enumerate((field_ref, wide_noise_ref)):
            rows = jnp.transpose(raw_ref[a, :, x].astype(F32), (1, 0, 2)).reshape(lanes, size_z).astype(BF16)
            if a:
                noise_rows_ref[x] = rows
            ref[x] = rows.T
    face_x, face_y = faces[:2], faces[2:]
    even = even_index("gx")
    for side in range(2):
        high = even if side == 0 else jnp.logical_not(even)
        face_x[side][0] = jnp.where(high, field_ref[size_x - 2], field_ref[0])
        face_x[side][1] = jnp.where(high, field_ref[size_x - 1], field_ref[1])
        face_x[side][2] = jnp.where(high, wide_noise_ref[size_x - 1], wide_noise_ref[0])
    even = even_index("gy")
    for k in range(y_sides):
        two, one = cut_y(even if k == 0 else jnp.logical_not(even))
        for j in range(0, size_x, 2):
            face_y[k][j // 2] = jnp.concatenate([two(field_ref[j]), two(field_ref[j + 1])], axis=1)
        for j in range(0, size_x, 4):
            face_y[k][size_x // 2 + j // 4] = jnp.concatenate([one(wide_noise_ref[j + i]) for i in range(4)], axis=1)


def cut_y(high):
    two = lambda p: jnp.where(high, p[:, p.shape[1] - 2 * C :], p[:, : 2 * C])
    one = lambda p: jnp.where(high, p[:, p.shape[1] - C :], p[:, :C])
    return two, one


def pack_corners(y_sides, face_0, face_1, *refs):
    corners = refs[y_sides:]
    even = even_index("gy")
    for k in range(y_sides):
        two, one = cut_y(even if k == 0 else jnp.logical_not(even))
        for side, face in enumerate((face_0, face_1)):
            ref = corners[2 * k + side]
            ref[:128] = jnp.concatenate([two(face[0]), two(face[1])], axis=1)
            strip = one(face[2])
            ref[128:] = jnp.concatenate([strip[i * 32 : (i + 1) * 32] for i in range(4)], axis=1)


def sort_faces(y_sides, *refs):
    x_refs, y_refs, out = refs[:2], list(refs[2 : 2 + y_sides]), refs[2 + y_sides :]
    y_refs += [None] * (2 - y_sides)
    for axis, pair, below_ref, above_ref in (("gx", x_refs, *out[:2]), ("gy", y_refs, *out[2:])):
        even = even_index(axis)
        index = lax.axis_index(axis)
        side_0, side_1 = [None if ref is None else ref[...] for ref in pair]
        below, above = choose(even, side_1, side_0), choose(even, side_0, side_1)
        below_ref[...] = jnp.where(index == 0, jnp.zeros_like(below), below)
        above_ref[...] = jnp.where(index == lax.axis_size(axis) - 1, jnp.zeros_like(above), above)


class Pieces:
    def __init__(self, y_sides, field, noise, face_x, face_y, corner):
        self.field, self.noise = field, noise
        self.size_x, self.size_z = field.shape[0], field.shape[1]
        even_x, even_y = even_index("gx"), even_index("gy")
        self.flag_x = {"below": even_x, "above": jnp.logical_not(even_x)}
        self.flag_y = {"below": even_y, "above": jnp.logical_not(even_y)}
        ends = lambda axis: (lax.axis_index(axis) == 0, lax.axis_index(axis) == lax.axis_size(axis) - 1)
        self.outside_x = dict(zip(("below", "above"), ends("gx")))
        self.outside_y = dict(zip(("below", "above"), ends("gy")))
        self.face_x = dict(zip(("below", "above"), face_x))
        self.face_y = dict(zip(("below", "above"), face_y))
        self.corner = [list(corner[2 * k : 2 * k + 2]) for k in range(y_sides)] + [[None, None]] * (2 - y_sides)

    def from_x(self, where, index, rows):
        return self.face_x[where][index, rows]

    def from_y(self, where, read):
        return read(self.face_y[where])

    def from_corner(self, where_x, where_y, read):
        a = []
        for pair in self.corner:
            if pair[0] is None:
                a.append(None)
            else:
                a.append(choose(self.flag_x[where_x], read(pair[1]), read(pair[0])))
        value = choose(self.flag_y[where_y], a[1], a[0])
        outside = self.outside_x[where_x] | self.outside_y[where_y]
        return jnp.where(outside, jnp.zeros_like(value), value)

    def side_of(self, x, width):
        if x < width:
            return "below", x
        if x >= self.size_x + width:
            return "above", x - self.size_x - width
        return "own", x - width

    def field_plane(self, x, z0, z1):
        rows = slice(z0, z1)
        where, i = self.side_of(x, 2)
        if where == "own":
            middle = self.field[i, rows]
            read = lambda ref: ref[i // 2, rows, (i % 2) * 2 * C : (i % 2 + 1) * 2 * C]
            low, high = self.from_y("below", read), self.from_y("above", read)
        else:
            middle = self.from_x(where, i, rows)
            read = lambda ref: ref[rows, i * 2 * C : (i + 1) * 2 * C]
            low, high = self.from_corner(where, "below", read), self.from_corner(where, "above", read)
        return jnp.concatenate([low, middle, high], axis=1)

    def noise_plane(self, x, z0, z1):
        rows = slice(z0, z1)
        where, i = self.side_of(x, 1)
        if where == "own":
            middle = self.noise[i, rows]
            read = lambda ref: ref[self.size_x // 2 + i // 4, rows, (i % 4) * C : (i % 4 + 1) * C]
            low, high = self.from_y("below", read), self.from_y("above", read)
        else:
            middle = self.from_x(where, 2, rows)

            def read(ref):
                parts = []
                for b in range(4):
                    first, last = max(z0, b * 32), min(z1, (b + 1) * 32)
                    if first < last:
                        parts.append(ref[128 + first - b * 32 : 128 + last - b * 32, b * C : (b + 1) * C])
                return jnp.concatenate(parts, axis=0) if len(parts) > 1 else parts[0]

            low, high = self.from_corner(where, "below", read), self.from_corner(where, "above", read)
        return jnp.concatenate([low, middle, high, jnp.zeros((z1 - z0, 2 * C), BF16)], axis=1)


def take_pieces(y_sides, refs):
    n = 6 + 2 * y_sides
    return Pieces(y_sides, refs[0], refs[1], refs[2:4], refs[4:6], refs[6:n]), refs[n:]


def pack_z(y_sides, *refs):
    pieces, (low_out, high_out, face_a, face_b) = take_pieces(y_sides, refs)
    n_field, n_noise, size_z = pieces.size_x + 4, pieces.size_x + 2, pieces.size_z

    def gather(tile, first, noise_row):
        planes = [pieces.field_plane(x, tile, tile + 16).astype(F32) for x in range(n_field)]
        rows = [plane[first + k - tile : first + k - tile + 1] for k in range(2) for plane in planes]
        for x in range(n_noise):
            rows.append(pieces.noise_plane(x, tile, tile + 16).astype(F32)[noise_row - tile : noise_row - tile + 1])
        while len(rows) % 16:
            rows.append(jnp.zeros_like(rows[0]))
        return jnp.concatenate(rows, axis=0).astype(BF16)

    low = gather(0, 0, 0)
    high = gather(size_z - 16, size_z - 2, size_z - 1)
    low_out[...] = low
    high_out[...] = high
    even = even_index("gz")
    face_a[...] = jnp.where(even, high, low)
    face_b[...] = jnp.where(even, low, high)


def stack(ref, dz, first, count):
    if isinstance(ref, Edged):
        return ref.stack(dz, first, count)
    return ref[dz, first : first + count].reshape(count * ref.shape[2], 256)


def taps(ref, count):
    return jnp.concatenate([stack(ref, dz, dx, count) for dx in range(3) for dz in range(3)], axis=1)


def widen(y_sides, *refs):
    pieces, (a1_ref, ab_ref, xs_ref, pre_ref, back_ref, hid_ref, slope_ref, ns_ref) = take_pieces(y_sides, refs)
    size_z = pieces.size_z
    for ref, read in ((xs_ref, pieces.field_plane), (ns_ref, pieces.noise_plane)):
        for x in range(ref.shape[1]):
            plane = read(x, 0, size_z)
            ref[1, x] = plane
            ref[0, x] = shifted(plane, 0.0, True)
            ref[2, x] = shifted(plane, 0.0, False)
    n_noise = pre_ref.shape[0]
    total = jnp.dot(taps(xs_ref, n_noise), a1_ref[...], preferred_element_type=F32)
    pre_ref[...] = total.reshape(n_noise, size_z, 256)
    size_x = back_ref.shape[0]
    total = jnp.dot(taps(ns_ref, size_x), ab_ref[...], preferred_element_type=F32)
    back_ref[...] = total.reshape(size_x, size_z, 256)

    index = lax.axis_index("gx")
    for x in range(n_noise):
        value = pre_ref[x]
        hidden, s = silu_parts(value)
        gone = outside_y()
        if x == 0:
            gone = gone | (index == 0)
        if x == n_noise - 1:
            gone = gone | (index == lax.axis_size("gx") - 1)
        hidden = jnp.where(gone, 0.0, hidden).astype(BF16)
        hid_ref[1, x] = hidden
        hid_ref[0, x] = shifted(hidden, 0.0, True)
        hid_ref[2, x] = shifted(hidden, 0.0, False)
        if 1 <= x <= size_x:
            slope_ref[x - 1] = slope_of(value, s)


def band(ref, row, taps, shift, lo, hi):
    moved = pltpu.roll(taps, shift % 128, 1) if shift % 128 else taps
    lane = lax.broadcasted_iota(jnp.int32, moved.shape, 1)
    for half in range(ref.shape[1] // 128):
        first = max(shift, lo) - 128 * half
        last = min(shift + 3 * C, hi) - 128 * half
        if last <= 0 or first >= 128:
            value = jnp.zeros_like(moved)
        else:
            value = jnp.where((lane >= first) & (lane < last), moved, 0.0)
        ref[row : row + C, half * 128 : (half + 1) * 128] = value.astype(BF16)


def spread_weights(both_ref, a1_ref, ab_ref, second_out):
    def columns(rows):
        wide = both_ref[rows].astype(F32)
        return jnp.concatenate([wide, jnp.zeros((C, 896 - wide.shape[1]), F32)], axis=1)

    def transposed(wide):
        return jnp.concatenate([wide[:, t * 128 : (t + 1) * 128].T for t in range(7)], axis=0)

    first = transposed(columns(slice(0, C)))
    second_rows = columns(slice(C, 2 * C))
    second = transposed(second_rows)
    fill = jnp.zeros((C, C), F32)
    for dx in range(3):
        for dz in range(3):
            t = 3 * dx + dz
            picks = [9 * dx + 3 * dy + dz for dy in range(3)]
            one = jnp.concatenate([first[k * C : (k + 1) * C, :] for k in picks[::-1]] + [fill], axis=1)
            two = jnp.concatenate([second[k * C : (k + 1) * C, :] for k in picks[::-1]] + [fill], axis=1)
            second_out[t] = two
            picks = [9 * (2 - dx) + 3 * dy + 2 - dz for dy in range(3)]
            back = jnp.concatenate([second_rows[:, k * C : (k + 1) * C] for k in picks] + [fill], axis=1)
            for yi in range(8):
                band(a1_ref, t * 256 + yi * C, one, (yi - 2) * C, 0, 6 * C)
            for yi in range(8):
                if yi < 6:
                    band(ab_ref, t * 256 + yi * C, back, (yi - 1) * C, C, 5 * C)
                else:
                    ab_ref[t * 256 + yi * C : t * 256 + (yi + 1) * C, :] = jnp.zeros((C, 256), BF16)


def shifted(plane, row, down):
    wide = plane.astype(F32)
    rows = wide.shape[0]
    index = lax.broadcasted_iota(jnp.int32, wide.shape, 0)
    if down:
        moved, place = pltpu.roll(wide, 1, 0), 0
    else:
        moved, place = pltpu.roll(wide, rows - 1, 0), rows - 1
    return jnp.where(index == place, row, moved).astype(BF16)


def silu_parts(value):
    s = 0.5 + 0.5 * jnp.tanh(0.5 * value)
    return value * s, s


def edge_tile(ref, dz, x, row):
    rows = ref.shape[2]
    at = slice(rows - 16, rows) if dz else slice(0, 16)
    tile = ref[dz, x, at, :].astype(F32)
    index = lax.broadcasted_iota(jnp.int32, tile.shape, 0)
    return jnp.where(index == (15 if dz else 0), row, tile).astype(BF16)


class Edged:
    def __init__(self, ref, edge_ref, tiles=((0, None), (None, None), (None, 1))):
        self.ref, self.edge_ref, self.tiles = ref, edge_ref, tiles

    def stack(self, dz, first, count):
        parts = []
        begin, end = self.tiles[dz]
        size_z = self.ref.shape[2]
        for x in range(first, first + count):
            if begin is not None:
                parts.append(self.edge_ref[begin, x])
            parts.append(self.ref[dz, x, 0 if begin is None else 16 : size_z if end is None else size_z - 16])
            if end is not None:
                parts.append(self.edge_ref[end, x])
        return jnp.concatenate(parts, axis=0)


HIDDEN_TILES = ((0, None), (1, 2), (None, 3))


def outside_y():
    lane = lax.broadcasted_iota(jnp.int32, (1, 256), 1)
    index = lax.axis_index("gy")
    return ((lane < C) & (index == 0)) | ((lane >= 5 * C) & (index == lax.axis_size("gy") - 1))


def slope_of(value, s):
    return s * (1.0 + value * (1.0 - s))


def mend(
    pre_ref, hid_ref, wide_field_ref, low_ref, high_ref, a1_ref, ab_ref, side_0, side_1, hid_edge, xs_edge, slope_rows, back_rows
):
    n_field, size_z = wide_field_ref.shape[1], wide_field_ref.shape[2]
    n_noise = pre_ref.shape[0]
    even = even_index("gz")
    own_low = low_ref[...].astype(F32)
    own_high = high_ref[...].astype(F32)

    gx, gz = lax.axis_index("gx"), lax.axis_index("gz")
    first_x, last_x = gx == 0, gx == lax.axis_size("gx") - 1
    first_z, last_z = gz == 0, gz == lax.axis_size("gz") - 1
    below_rows = jnp.where(first_z, 0.0, jnp.where(even, side_1[...], side_0[...]).astype(F32))
    above_rows = jnp.where(last_z, 0.0, jnp.where(even, side_0[...], side_1[...]).astype(F32))

    before = jnp.concatenate([below_rows[:n_field], own_high[n_field : 2 * n_field]], axis=0).astype(BF16)
    halo = jnp.concatenate([below_rows[n_field : 2 * n_field], above_rows[:n_field]], axis=0).astype(BF16)
    after = jnp.concatenate([own_low[:n_field], above_rows[n_field : 2 * n_field]], axis=0).astype(BF16)
    base = 2 * n_field
    noise_halo = jnp.concatenate(
        [below_rows[base : base + n_field], above_rows[base : base + n_field]], axis=0
    ).astype(BF16)
    rows = 2 * n_field
    edge_total, row_total, back_total = None, None, None
    for dx in range(3):
        at = lambda ref, dz: ref[(3 * dx + dz) * 256 : (3 * dx + dz + 1) * 256]
        first = jnp.dot(jnp.concatenate([before, halo], axis=0), at(a1_ref, 0), preferred_element_type=F32)
        middle = jnp.dot(halo, at(a1_ref, 1), preferred_element_type=F32)
        last = jnp.dot(jnp.concatenate([after, halo], axis=0), at(a1_ref, 2), preferred_element_type=F32)
        back_first = jnp.dot(noise_halo, at(ab_ref, 0), preferred_element_type=F32)
        back_last = jnp.dot(noise_halo, at(ab_ref, 2), preferred_element_type=F32)
        edge = first[:rows] + middle + last[:rows]
        row = jnp.concatenate([first[rows : rows + n_field], last[rows + n_field :]], axis=0)
        back = jnp.concatenate([back_first[:n_field], back_last[n_field:]], axis=0)
        if dx:
            edge, row, back = [pltpu.roll(part, rows - dx, 0) for part in (edge, row, back)]
        edge_total = edge if edge_total is None else edge_total + edge
        row_total = row if row_total is None else row_total + row
        back_total = back if back_total is None else back_total + back
    back_rows[...] = back_total

    index = lax.broadcasted_iota(jnp.int32, (rows, 256), 0)
    x_row = jnp.where(index < n_field, index, index - n_field)
    drop = outside_y() | ((x_row == 0) & first_x) | ((x_row == n_noise - 1) & last_x)
    drop_edge = drop | ((index < n_field) & first_z) | ((index >= n_field) & last_z)
    edge_hidden = jnp.where(drop_edge, 0.0, silu_parts(edge_total)[0]).astype(BF16).astype(F32)

    zeros = [jnp.zeros((1, 256), F32)] * (n_field - n_noise)
    ends = [pre_ref[x, 0:8][0:1] for x in range(n_noise)] + zeros
    ends += [pre_ref[x, size_z - 8 :][7:8] for x in range(n_noise)] + zeros
    value = jnp.concatenate(ends, axis=0) + row_total
    row_hidden, s = silu_parts(value)
    row_hidden = jnp.where(drop, 0.0, row_hidden).astype(BF16).astype(F32)
    slope_rows[...] = slope_of(value, s)

    tile_row = lax.broadcasted_iota(jnp.int32, (16, 256), 0)
    for x in range(n_noise):
        low, high = row_hidden[x : x + 1], row_hidden[n_field + x : n_field + x + 1]
        below, above = edge_hidden[x : x + 1], edge_hidden[n_field + x : n_field + x + 1]
        begin = [hid_ref[dz, x, 0:16].astype(F32) for dz in range(2)]
        end = [hid_ref[dz, x, size_z - 16 :].astype(F32) for dz in range(1, 3)]
        hid_edge[0, x] = jnp.where(tile_row == 0, below, jnp.where(tile_row == 1, low, begin[0])).astype(BF16)
        hid_edge[1, x] = jnp.where(tile_row == 0, low, begin[1]).astype(BF16)
        hid_edge[2, x] = jnp.where(tile_row == 15, high, end[0]).astype(BF16)
        hid_edge[3, x] = jnp.where(tile_row == 15, above, jnp.where(tile_row == 14, high, end[1])).astype(BF16)
    for x in range(n_field):
        xs_edge[0, x] = edge_tile(wide_field_ref, 0, x, below_rows[n_field + x : n_field + x + 1])
        xs_edge[1, x] = edge_tile(wide_field_ref, 2, x, above_rows[x : x + 1])


def backward(back_ref, slope_ref, slope_rows, back_rows, out_ref):
    size_x, size_z = slope_ref.shape[:2]
    half = slope_rows.shape[0] // 2
    index = lax.broadcasted_iota(jnp.int32, (size_z, 256), 0)
    for x in range(size_x):
        back, slope = back_ref[x], slope_ref[x]
        for row, at in ((0, 0), (size_z - 1, half)):
            back = jnp.where(index == row, back + back_rows[at + x : at + x + 1], back)
            slope = jnp.where(index == row, slope_rows[at + x + 1 : at + x + 2], slope)
        value = (back * slope).astype(BF16)
        rows = jnp.concatenate([value[:, :128].T, value[:, 128:].T], axis=0)
        out_ref[:, x * size_z : (x + 1) * size_z] = rows[C : 5 * C, :]


def collect(left, ref, size_x, skip, offset):
    tiles = [jnp.zeros((C, 128), F32) for _ in range(7)]
    lanes = lax.broadcasted_iota(jnp.int32, (C, 128), 1)
    for dx in range(3):
        for dz in range(3):
            block = jnp.dot(left, stack(ref, dz, dx + skip, size_x), preferred_element_type=F32)
            total = None
            for y in range(4):
                part = block[y * C : (y + 1) * C, :]
                shift = (256 - (y + offset) * C) % 256
                part = pltpu.roll(part, shift, 1) if shift else part
                total = part if total is None else total + part
            total = total[:, :128]
            for dy in range(3):
                tap = 9 * dx + 3 * dy + dz
                shift = ((tap - dy) * C) % 128
                moved = pltpu.roll(total, shift, 1) if shift else total
                at = (tap % 4) * C
                tiles[tap // 4] = jnp.where((lanes >= at) & (lanes < at + C), moved, tiles[tap // 4])
    return jnp.concatenate(tiles, axis=1)


def weight_grad(give, xs_ref, xs_edge, hid_ref, hid_edge, pre_grad_ref, rows_ref, out_ref):
    size_x = rows_ref.shape[0]
    even = even_index("gz")

    @pl.when(even if give else jnp.logical_not(even))
    def _():
        noise_rows = jnp.concatenate([rows_ref[x] for x in range(size_x)], axis=1)
        out_ref[...] = collect(noise_rows, Edged(hid_ref, hid_edge, HIDDEN_TILES), size_x, 0, 0)

    @pl.when(jnp.logical_not(even) if give else even)
    def _():
        out_ref[...] = collect(pre_grad_ref[...], Edged(xs_ref, xs_edge), size_x, 1, 1)


def predict(hid_ref, hid_edge, second_ref, out_ref, acc_ref, a2_ref):
    size_x, size_z = out_ref.shape[0], out_ref.shape[2]
    for t in range(9):
        for yi in range(8):
            band(a2_ref, t * 256 + yi * C, second_ref[t], (yi - 2) * C, 0, 4 * C)
    total = jnp.dot(taps(Edged(hid_ref, hid_edge, HIDDEN_TILES), size_x), a2_ref[...], preferred_element_type=F32)
    acc_ref[...] = total.reshape(size_x, size_z, 128)
    for x in range(size_x):
        out_ref[x] = acc_ref[x].astype(BF16).T


def finish(norm, mine_ref, other_ref, first_ref, second_ref):
    even = even_index("gz")
    mine = mine_ref[...]
    other = other_ref[...]
    first = jnp.where(even, mine, other) * norm
    second = jnp.where(even, other, mine) * norm
    first_ref[...] = (first * first)[:, : 27 * C]
    second_ref[...] = (second * second)[:, : 27 * C]


def first_sum(keep_ref, taken_ref, send_ref):
    send_ref[...] = (keep_ref[...] + taken_ref[...]).astype(BF16)


def round_sum(own_ref, *refs):
    got, out_ref = refs[:-1], refs[-1]
    total = own_ref[...].astype(F32) + got[0][...].astype(F32)
    if len(got) == 3:
        total = total + (got[1][...].astype(F32) + got[2][...].astype(F32))
    out_ref[...] = total.astype(out_ref.dtype)


def flip(x, axis, bit):
    size = lax.axis_size(axis)
    return lax.ppermute(x, axis, [(i, i ^ bit) for i in range(size)])


def masked_swap(x, flip_even, flip_odd):
    target = {}
    for place in all_places():
        to = list(place)
        for axis, bit in flip_odd if place[2] % 2 else flip_even:
            to[AXES.index(axis)] ^= bit
        target[place] = tuple(to)
    return permute(x, target)


def local(inputs, noise, w_first, w_second):
    _, channels, size_x, size_y, size_z = inputs.shape
    cells = size_x * size_y * size_z
    devices = lax.axis_size("gx") * lax.axis_size("gy") * lax.axis_size("gz")
    norm = 1.0 / math.sqrt(cells * devices)
    lanes = size_y * channels

    plane = (size_z, lanes)
    y_sides = 2 if lax.axis_size("gy") > 2 else 1
    y_planes = size_x // 2 + size_x // 4
    face = struct((3,) + plane, BF16)
    y_face = struct((y_planes,) + plane, BF16)
    n_near = 2 + y_sides
    noise_rows, field, wide_noise, *faces = call(
        functools.partial(pack_faces, y_sides),
        [struct((size_x, lanes, size_z), BF16)]
        + [struct((size_x,) + plane, BF16)] * 2
        + [face] * 2
        + [y_face] * y_sides,
    )(jnp.concatenate([inputs, noise], axis=0))
    corners = call(functools.partial(pack_corners, y_sides), [struct((160, 128), BF16)] * (2 * y_sides))(*faces)
    faces = [*faces, *corners]
    moves = [[("gx", side)] for side in range(2)]
    moves += [[("gy", side)] for side in range(y_sides)]
    moves += [[("gx", side), ("gy", k)] for k in range(y_sides) for side in range(2)]
    got = [swap(face, move) for face, move in zip(faces, moves)]

    a1, ab, second = call(
        spread_weights,
        [struct((9 * 256, 256), BF16), struct((9 * 256, 256), BF16), struct((9, C, 128), F32)],
        moved=4_000_000,
    )(jnp.concatenate([w_first, w_second], axis=0))
    *near, a1, ab, second = lax.optimization_barrier((*got[:n_near], a1, ab, second))
    got = [*call(functools.partial(sort_faces, y_sides), [face] * 2 + [y_face] * 2)(*near), *got[n_near:]]

    n_field, n_noise = size_x + 4, size_x + 2
    z_rows = -(-(2 * n_field + n_noise) // 16) * 16
    low, high, face_a, face_b = call(
        functools.partial(pack_z, y_sides), [struct((z_rows, 256), BF16)] * 4
    )(field, wide_noise, *got)
    z_got = [swap(face, [("gz", side)]) for side, face in enumerate((face_a, face_b))]
    pre_shape = (n_noise, size_z, 256)
    slope_shape = (size_x, size_z, 256)
    xs, pre, back, hidden, slope = call(
        functools.partial(widen, y_sides),
        [
            struct((3, n_field, size_z, 256), BF16),
            struct(pre_shape, F32),
            struct(slope_shape, F32),
            struct((3,) + pre_shape, BF16),
            struct(slope_shape, F32),
        ],
        scratch=[pltpu.VMEM((3,) + pre_shape, BF16)],
        flops=1_000_000_000,
    )(field, wide_noise, *got, a1, ab)
    *z_got, xs, pre, back, hidden, slope = lax.optimization_barrier((*z_got, xs, pre, back, hidden, slope))

    hidden_edge, xs_edge, slope_rows, back_rows = call(
        mend,
        [
            struct((4, n_noise, 16, 256), BF16),
            struct((2, n_field, 16, 256), BF16),
            struct((2 * n_field, 256), F32),
            struct((2 * n_field, 256), F32),
        ],
    )(pre, hidden, xs, low, high, a1, ab, *z_got)
    pre_grad = call(backward, struct((lanes, size_x * size_z), BF16))(back, slope, slope_rows, back_rows)

    half = struct((C, 896), F32)
    rounded = struct((C, 896), BF16)
    parts = (xs, xs_edge, hidden, hidden_edge, pre_grad, noise_rows)
    give = call(functools.partial(weight_grad, True), half, flops=1_000_000_000)(*parts)
    taken = flip(give, "gz", 1)
    keep = call(functools.partial(weight_grad, False), half, flops=1_000_000_000)(*parts)
    send = call(first_sum, rounded)(keep, taken)

    prediction_rows = call(
        predict,
        struct((size_x, lanes, size_z), BF16),
        scratch=[pltpu.VMEM((size_x, size_z, lanes), F32), pltpu.VMEM((9 * 256, 128), BF16)],
        flops=500_000_000,
    )(hidden, hidden_edge, second)
    prediction = prediction_rows.reshape(size_x, size_y, channels, size_z).transpose(2, 0, 1, 3)[None]

    steps = []
    for axis, start in (("gx", 1), ("gz", 2), ("gy", 1)):
        bit = start
        while bit < lax.axis_size(axis):
            steps.append((axis, bit))
            bit *= 2
    rounds = [steps[k : k + 2] for k in range(0, len(steps), 2)]
    turn = len(rounds) // 2 if len(steps) % 2 == 0 else 0
    for k, even in enumerate(rounds):
        odd = rounds[(k + turn) % len(rounds)]
        flips = [(even[:1], odd[:1])]
        if len(even) == 2:
            flips += [(even[1:], odd[1:]), (even, odd)]
        got = [masked_swap(send, *pair) for pair in flips]
        if k == 0:
            *got, prediction = lax.optimization_barrier((*got, prediction))
        send = call(round_sum, half if k == len(rounds) - 1 else rounded)(send, *got)
    mine = send
    other = flip(mine, "gz", 1)
    fisher_first, fisher_second = call(
        functools.partial(finish, norm), [struct((C, 27 * C), F32)] * 2
    )(mine, other)
    return prediction, fisher_first, fisher_second


def solution(mesh):
    in_specs = (P(None, None, "gx", "gy", "gz"), P(None, None, "gx", "gy", "gz"), P(), P())
    out_specs = (P(None, None, "gx", "gy", "gz"), P(), P())
    return jax.shard_map(local, mesh=mesh, in_specs=in_specs, out_specs=out_specs, check_vma=False)
```

```python
import functools
import math

import jax
import jax.numpy as jnp
from jax import lax
from jax.experimental import pallas as pl
from jax.experimental.pallas import tpu as pltpu
from jax.sharding import PartitionSpec as P

F32 = jnp.float32
BF16 = jnp.bfloat16
C = 32


def call(body, out_shapes, scratch=(), flops=1_000_000, moved=1_000_000, vmem=24, **more):
    return pl.pallas_call(
        body,
        **more,
        out_shape=out_shapes,
        scratch_shapes=list(scratch),
        compiler_params=pltpu.CompilerParams(vmem_limit_bytes=vmem * 1024 * 1024),
        cost_estimate=pl.CostEstimate(flops=flops, bytes_accessed=moved, transcendentals=0),
    )


def struct(shape, dtype):
    return jax.ShapeDtypeStruct(shape, dtype)


def even_index(axis):
    return lax.rem(lax.axis_index(axis), 2) == 0


def partner(index, side, size):
    other = index ^ 1 if side == 0 else ((index + 1) ^ 1) - 1
    return other if 0 <= other < size else None


AXES = ("gx", "gy", "gz")


def all_places():
    sizes = [lax.axis_size(axis) for axis in AXES]
    return [(i, j, k) for i in range(sizes[0]) for j in range(sizes[1]) for k in range(sizes[2])]


def permute(x, target):
    sizes = [lax.axis_size(axis) for axis in AXES]
    number = lambda place: (place[0] * sizes[1] + place[1]) * sizes[2] + place[2]
    return lax.ppermute(x, AXES, [(number(place), number(to)) for place, to in target.items()])


def swap(x, moves):
    sizes = [lax.axis_size(axis) for axis in AXES]
    side = dict(moves)
    places = all_places()
    target = {}
    for place in places:
        to = [partner(i, side[axis], size) if axis in side else i for i, axis, size in zip(place, AXES, sizes)]
        if None not in to:
            target[place] = tuple(to)
    if not target:
        return None
    alone = [place for place in places if place not in target]
    fills = (
        lambda i, j, k: (i, j, k ^ 2),
        lambda i, j, k: (i, j ^ 1, k),
        lambda i, j, k: (i ^ 1, j, k),
        lambda i, j, k: (i, j, k),
    )
    for fill in fills:
        if all(fill(*place) in alone for place in alone):
            target.update({place: fill(*place) for place in alone})
            break
    return permute(x, target)


def choose(flag, a, b):
    if a is None and b is None:
        return None
    a = jnp.zeros_like(b) if a is None else a
    b = jnp.zeros_like(a) if b is None else b
    return jnp.where(flag, a, b)


def pack_faces(y_sides, raw_ref, noise_rows_ref, field_ref, wide_noise_ref, *faces):
    size_x, size_z = raw_ref.shape[2], raw_ref.shape[4]
    lanes = raw_ref.shape[1] * raw_ref.shape[3]
    for x in range(size_x):
        for a, ref in enumerate((field_ref, wide_noise_ref)):
            rows = jnp.transpose(raw_ref[a, :, x].astype(F32), (1, 0, 2)).reshape(lanes, size_z).astype(BF16)
            if a:
                noise_rows_ref[x] = rows
            ref[x] = rows.T
    face_x, face_y = faces[:2], faces[2:]
    even = even_index("gx")
    for side in range(2):
        high = even if side == 0 else jnp.logical_not(even)
        face_x[side][0] = jnp.where(high, field_ref[size_x - 2], field_ref[0])
        face_x[side][1] = jnp.where(high, field_ref[size_x - 1], field_ref[1])
        face_x[side][2] = jnp.where(high, wide_noise_ref[size_x - 1], wide_noise_ref[0])
    even = even_index("gy")
    for k in range(y_sides):
        two, one = cut_y(even if k == 0 else jnp.logical_not(even))
        for j in range(0, size_x, 2):
            face_y[k][j // 2] = jnp.concatenate([two(field_ref[j]), two(field_ref[j + 1])], axis=1)
        for j in range(0, size_x, 4):
            face_y[k][size_x // 2 + j // 4] = jnp.concatenate([one(wide_noise_ref[j + i]) for i in range(4)], axis=1)


def cut_y(high):
    two = lambda p: jnp.where(high, p[:, p.shape[1] - 2 * C :], p[:, : 2 * C])
    one = lambda p: jnp.where(high, p[:, p.shape[1] - C :], p[:, :C])
    return two, one


def pack_corners(y_sides, face_0, face_1, *refs):
    corners = refs[y_sides:]
    even = even_index("gy")
    for k in range(y_sides):
        two, one = cut_y(even if k == 0 else jnp.logical_not(even))
        for side, face in enumerate((face_0, face_1)):
            ref = corners[2 * k + side]
            ref[:128] = jnp.concatenate([two(face[0]), two(face[1])], axis=1)
            strip = one(face[2])
            ref[128:] = jnp.concatenate([strip[i * 32 : (i + 1) * 32] for i in range(4)], axis=1)


def sort_faces(y_sides, *refs):
    x_refs, y_refs, out = refs[:2], list(refs[2 : 2 + y_sides]), refs[2 + y_sides :]
    y_refs += [None] * (2 - y_sides)
    for axis, pair, below_ref, above_ref in (("gx", x_refs, *out[:2]), ("gy", y_refs, *out[2:])):
        even = even_index(axis)
        index = lax.axis_index(axis)
        side_0, side_1 = [None if ref is None else ref[...] for ref in pair]
        below, above = choose(even, side_1, side_0), choose(even, side_0, side_1)
        below_ref[...] = jnp.where(index == 0, jnp.zeros_like(below), below)
        above_ref[...] = jnp.where(index == lax.axis_size(axis) - 1, jnp.zeros_like(above), above)


class Pieces:
    def __init__(self, y_sides, field, noise, face_x, face_y, corner):
        self.field, self.noise = field, noise
        self.size_x, self.size_z = field.shape[0], field.shape[1]
        even_x, even_y = even_index("gx"), even_index("gy")
        self.flag_x = {"below": even_x, "above": jnp.logical_not(even_x)}
        self.flag_y = {"below": even_y, "above": jnp.logical_not(even_y)}
        ends = lambda axis: (lax.axis_index(axis) == 0, lax.axis_index(axis) == lax.axis_size(axis) - 1)
        self.outside_x = dict(zip(("below", "above"), ends("gx")))
        self.outside_y = dict(zip(("below", "above"), ends("gy")))
        self.face_x = dict(zip(("below", "above"), face_x))
        self.face_y = dict(zip(("below", "above"), face_y))
        self.corner = [list(corner[2 * k : 2 * k + 2]) for k in range(y_sides)] + [[None, None]] * (2 - y_sides)

    def from_x(self, where, index, rows):
        return self.face_x[where][index, rows]

    def from_y(self, where, read):
        return read(self.face_y[where])

    def from_corner(self, where_x, where_y, read):
        a = []
        for pair in self.corner:
            if pair[0] is None:
                a.append(None)
            else:
                a.append(choose(self.flag_x[where_x], read(pair[1]), read(pair[0])))
        value = choose(self.flag_y[where_y], a[1], a[0])
        outside = self.outside_x[where_x] | self.outside_y[where_y]
        return jnp.where(outside, jnp.zeros_like(value), value)

    def side_of(self, x, width):
        if x < width:
            return "below", x
        if x >= self.size_x + width:
            return "above", x - self.size_x - width
        return "own", x - width

    def field_plane(self, x, z0, z1):
        rows = slice(z0, z1)
        where, i = self.side_of(x, 2)
        if where == "own":
            middle = self.field[i, rows]
            read = lambda ref: ref[i // 2, rows, (i % 2) * 2 * C : (i % 2 + 1) * 2 * C]
            low, high = self.from_y("below", read), self.from_y("above", read)
        else:
            middle = self.from_x(where, i, rows)
            read = lambda ref: ref[rows, i * 2 * C : (i + 1) * 2 * C]
            low, high = self.from_corner(where, "below", read), self.from_corner(where, "above", read)
        return jnp.concatenate([low, middle, high], axis=1)

    def noise_plane(self, x, z0, z1):
        rows = slice(z0, z1)
        where, i = self.side_of(x, 1)
        if where == "own":
            middle = self.noise[i, rows]
            read = lambda ref: ref[self.size_x // 2 + i // 4, rows, (i % 4) * C : (i % 4 + 1) * C]
            low, high = self.from_y("below", read), self.from_y("above", read)
        else:
            middle = self.from_x(where, 2, rows)

            def read(ref):
                parts = []
                for b in range(4):
                    first, last = max(z0, b * 32), min(z1, (b + 1) * 32)
                    if first < last:
                        parts.append(ref[128 + first - b * 32 : 128 + last - b * 32, b * C : (b + 1) * C])
                return jnp.concatenate(parts, axis=0) if len(parts) > 1 else parts[0]

            low, high = self.from_corner(where, "below", read), self.from_corner(where, "above", read)
        return jnp.concatenate([low, middle, high, jnp.zeros((z1 - z0, 2 * C), BF16)], axis=1)


def take_pieces(y_sides, refs):
    n = 6 + 2 * y_sides
    return Pieces(y_sides, refs[0], refs[1], refs[2:4], refs[4:6], refs[6:n]), refs[n:]


def pack_z(y_sides, *refs):
    pieces, (low_out, high_out, face_a, face_b) = take_pieces(y_sides, refs)
    n_field, n_noise, size_z = pieces.size_x + 4, pieces.size_x + 2, pieces.size_z

    def gather(tile, first, noise_row):
        planes = [pieces.field_plane(x, tile, tile + 16).astype(F32) for x in range(n_field)]
        rows = [plane[first + k - tile : first + k - tile + 1] for k in range(2) for plane in planes]
        for x in range(n_noise):
            rows.append(pieces.noise_plane(x, tile, tile + 16).astype(F32)[noise_row - tile : noise_row - tile + 1])
        while len(rows) % 16:
            rows.append(jnp.zeros_like(rows[0]))
        return jnp.concatenate(rows, axis=0).astype(BF16)

    low = gather(0, 0, 0)
    high = gather(size_z - 16, size_z - 2, size_z - 1)
    low_out[...] = low
    high_out[...] = high
    even = even_index("gz")
    face_a[...] = jnp.where(even, high, low)
    face_b[...] = jnp.where(even, low, high)


def stack(ref, dz, first, count):
    if isinstance(ref, Edged):
        return ref.stack(dz, first, count)
    return ref[dz, first : first + count].reshape(count * ref.shape[2], 256)


def taps(ref, count):
    return jnp.concatenate([stack(ref, dz, dx, count) for dx in range(3) for dz in range(3)], axis=1)


def widen(y_sides, *refs):
    pieces, (a1_ref, ab_ref, xs_ref, pre_ref, back_ref, hid_ref, slope_ref, ns_ref) = take_pieces(y_sides, refs)
    size_z = pieces.size_z
    for ref, read in ((xs_ref, pieces.field_plane), (ns_ref, pieces.noise_plane)):
        for x in range(ref.shape[1]):
            plane = read(x, 0, size_z)
            ref[1, x] = plane
            ref[0, x] = shifted(plane, 0.0, True)
            ref[2, x] = shifted(plane, 0.0, False)
    n_noise = pre_ref.shape[0]
    total = jnp.dot(taps(xs_ref, n_noise), a1_ref[...], preferred_element_type=F32)
    pre_ref[...] = total.reshape(n_noise, size_z, 256)
    size_x = back_ref.shape[0]
    total = jnp.dot(taps(ns_ref, size_x), ab_ref[...], preferred_element_type=F32)
    back_ref[...] = total.reshape(size_x, size_z, 256)

    index = lax.axis_index("gx")
    for x in range(n_noise):
        value = pre_ref[x]
        hidden, s = silu_parts(value)
        gone = outside_y()
        if x == 0:
            gone = gone | (index == 0)
        if x == n_noise - 1:
            gone = gone | (index == lax.axis_size("gx") - 1)
        hidden = jnp.where(gone, 0.0, hidden).astype(BF16)
        hid_ref[1, x] = hidden
        hid_ref[0, x] = shifted(hidden, 0.0, True)
        hid_ref[2, x] = shifted(hidden, 0.0, False)
        if 1 <= x <= size_x:
            slope_ref[x - 1] = slope_of(value, s)


def band(ref, row, taps, shift, lo, hi):
    moved = pltpu.roll(taps, shift % 128, 1) if shift % 128 else taps
    lane = lax.broadcasted_iota(jnp.int32, moved.shape, 1)
    for half in range(ref.shape[1] // 128):
        first = max(shift, lo) - 128 * half
        last = min(shift + 3 * C, hi) - 128 * half
        if last <= 0 or first >= 128:
            value = jnp.zeros_like(moved)
        else:
            value = jnp.where((lane >= first) & (lane < last), moved, 0.0)
        ref[row : row + C, half * 128 : (half + 1) * 128] = value.astype(BF16)


def spread_weights(both_ref, a1_ref, ab_ref, second_out):
    def columns(rows):
        wide = both_ref[rows].astype(F32)
        return jnp.concatenate([wide, jnp.zeros((C, 896 - wide.shape[1]), F32)], axis=1)

    def transposed(wide):
        return jnp.concatenate([wide[:, t * 128 : (t + 1) * 128].T for t in range(7)], axis=0)

    first = transposed(columns(slice(0, C)))
    second_rows = columns(slice(C, 2 * C))
    second = transposed(second_rows)
    fill = jnp.zeros((C, C), F32)
    for dx in range(3):
        for dz in range(3):
            t = 3 * dx + dz
            picks = [9 * dx + 3 * dy + dz for dy in range(3)]
            one = jnp.concatenate([first[k * C : (k + 1) * C, :] for k in picks[::-1]] + [fill], axis=1)
            two = jnp.concatenate([second[k * C : (k + 1) * C, :] for k in picks[::-1]] + [fill], axis=1)
            second_out[t] = two
            picks = [9 * (2 - dx) + 3 * dy + 2 - dz for dy in range(3)]
            back = jnp.concatenate([second_rows[:, k * C : (k + 1) * C] for k in picks] + [fill], axis=1)
            for yi in range(8):
                band(a1_ref, t * 256 + yi * C, one, (yi - 2) * C, 0, 6 * C)
            for yi in range(8):
                if yi < 6:
                    band(ab_ref, t * 256 + yi * C, back, (yi - 1) * C, C, 5 * C)
                else:
                    ab_ref[t * 256 + yi * C : t * 256 + (yi + 1) * C, :] = jnp.zeros((C, 256), BF16)


def shifted(plane, row, down):
    wide = plane.astype(F32)
    rows = wide.shape[0]
    index = lax.broadcasted_iota(jnp.int32, wide.shape, 0)
    if down:
        moved, place = pltpu.roll(wide, 1, 0), 0
    else:
        moved, place = pltpu.roll(wide, rows - 1, 0), rows - 1
    return jnp.where(index == place, row, moved).astype(BF16)


def silu_parts(value):
    s = 0.5 + 0.5 * jnp.tanh(0.5 * value)
    return value * s, s


def edge_tile(ref, dz, x, row):
    rows = ref.shape[2]
    at = slice(rows - 16, rows) if dz else slice(0, 16)
    tile = ref[dz, x, at, :].astype(F32)
    index = lax.broadcasted_iota(jnp.int32, tile.shape, 0)
    return jnp.where(index == (15 if dz else 0), row, tile).astype(BF16)


class Edged:
    def __init__(self, ref, edge_ref, tiles=((0, None), (None, None), (None, 1))):
        self.ref, self.edge_ref, self.tiles = ref, edge_ref, tiles

    def stack(self, dz, first, count):
        parts = []
        begin, end = self.tiles[dz]
        size_z = self.ref.shape[2]
        for x in range(first, first + count):
            if begin is not None:
                parts.append(self.edge_ref[begin, x])
            parts.append(self.ref[dz, x, 0 if begin is None else 16 : size_z if end is None else size_z - 16])
            if end is not None:
                parts.append(self.edge_ref[end, x])
        return jnp.concatenate(parts, axis=0)


HIDDEN_TILES = ((0, None), (1, 2), (None, 3))


def outside_y():
    lane = lax.broadcasted_iota(jnp.int32, (1, 256), 1)
    index = lax.axis_index("gy")
    return ((lane < C) & (index == 0)) | ((lane >= 5 * C) & (index == lax.axis_size("gy") - 1))


def slope_of(value, s):
    return s * (1.0 + value * (1.0 - s))


def mend(
    pre_ref, hid_ref, wide_field_ref, low_ref, high_ref, a1_ref, ab_ref, side_0, side_1, hid_edge, xs_edge, slope_rows, back_rows
):
    n_field, size_z = wide_field_ref.shape[1], wide_field_ref.shape[2]
    n_noise = pre_ref.shape[0]
    even = even_index("gz")
    own_low = low_ref[...].astype(F32)
    own_high = high_ref[...].astype(F32)

    gx, gz = lax.axis_index("gx"), lax.axis_index("gz")
    first_x, last_x = gx == 0, gx == lax.axis_size("gx") - 1
    first_z, last_z = gz == 0, gz == lax.axis_size("gz") - 1
    below_rows = jnp.where(first_z, 0.0, jnp.where(even, side_1[...], side_0[...]).astype(F32))
    above_rows = jnp.where(last_z, 0.0, jnp.where(even, side_0[...], side_1[...]).astype(F32))

    before = jnp.concatenate([below_rows[:n_field], own_high[n_field : 2 * n_field]], axis=0).astype(BF16)
    halo = jnp.concatenate([below_rows[n_field : 2 * n_field], above_rows[:n_field]], axis=0).astype(BF16)
    after = jnp.concatenate([own_low[:n_field], above_rows[n_field : 2 * n_field]], axis=0).astype(BF16)
    base = 2 * n_field
    noise_halo = jnp.concatenate(
        [below_rows[base : base + n_field], above_rows[base : base + n_field]], axis=0
    ).astype(BF16)
    rows = 2 * n_field
    edge_total, row_total, back_total = None, None, None
    for dx in range(3):
        at = lambda ref, dz: ref[(3 * dx + dz) * 256 : (3 * dx + dz + 1) * 256]
        first = jnp.dot(jnp.concatenate([before, halo], axis=0), at(a1_ref, 0), preferred_element_type=F32)
        middle = jnp.dot(halo, at(a1_ref, 1), preferred_element_type=F32)
        last = jnp.dot(jnp.concatenate([after, halo], axis=0), at(a1_ref, 2), preferred_element_type=F32)
        back_first = jnp.dot(noise_halo, at(ab_ref, 0), preferred_element_type=F32)
        back_last = jnp.dot(noise_halo, at(ab_ref, 2), preferred_element_type=F32)
        edge = first[:rows] + middle + last[:rows]
        row = jnp.concatenate([first[rows : rows + n_field], last[rows + n_field :]], axis=0)
        back = jnp.concatenate([back_first[:n_field], back_last[n_field:]], axis=0)
        if dx:
            edge, row, back = [pltpu.roll(part, rows - dx, 0) for part in (edge, row, back)]
        edge_total = edge if edge_total is None else edge_total + edge
        row_total = row if row_total is None else row_total + row
        back_total = back if back_total is None else back_total + back
    back_rows[...] = back_total

    index = lax.broadcasted_iota(jnp.int32, (rows, 256), 0)
    x_row = jnp.where(index < n_field, index, index - n_field)
    drop = outside_y() | ((x_row == 0) & first_x) | ((x_row == n_noise - 1) & last_x)
    drop_edge = drop | ((index < n_field) & first_z) | ((index >= n_field) & last_z)
    edge_hidden = jnp.where(drop_edge, 0.0, silu_parts(edge_total)[0]).astype(BF16).astype(F32)

    zeros = [jnp.zeros((1, 256), F32)] * (n_field - n_noise)
    ends = [pre_ref[x, 0:8][0:1] for x in range(n_noise)] + zeros
    ends += [pre_ref[x, size_z - 8 :][7:8] for x in range(n_noise)] + zeros
    value = jnp.concatenate(ends, axis=0) + row_total
    row_hidden, s = silu_parts(value)
    row_hidden = jnp.where(drop, 0.0, row_hidden).astype(BF16).astype(F32)
    slope_rows[...] = slope_of(value, s)

    tile_row = lax.broadcasted_iota(jnp.int32, (16, 256), 0)
    for x in range(n_noise):
        low, high = row_hidden[x : x + 1], row_hidden[n_field + x : n_field + x + 1]
        below, above = edge_hidden[x : x + 1], edge_hidden[n_field + x : n_field + x + 1]
        begin = [hid_ref[dz, x, 0:16].astype(F32) for dz in range(2)]
        end = [hid_ref[dz, x, size_z - 16 :].astype(F32) for dz in range(1, 3)]
        hid_edge[0, x] = jnp.where(tile_row == 0, below, jnp.where(tile_row == 1, low, begin[0])).astype(BF16)
        hid_edge[1, x] = jnp.where(tile_row == 0, low, begin[1]).astype(BF16)
        hid_edge[2, x] = jnp.where(tile_row == 15, high, end[0]).astype(BF16)
        hid_edge[3, x] = jnp.where(tile_row == 15, above, jnp.where(tile_row == 14, high, end[1])).astype(BF16)
    for x in range(n_field):
        xs_edge[0, x] = edge_tile(wide_field_ref, 0, x, below_rows[n_field + x : n_field + x + 1])
        xs_edge[1, x] = edge_tile(wide_field_ref, 2, x, above_rows[x : x + 1])


def backward(back_ref, slope_ref, slope_rows, back_rows, out_ref):
    size_x, size_z = slope_ref.shape[:2]
    half = slope_rows.shape[0] // 2
    index = lax.broadcasted_iota(jnp.int32, (size_z, 256), 0)
    for x in range(size_x):
        back, slope = back_ref[x], slope_ref[x]
        for row, at in ((0, 0), (size_z - 1, half)):
            back = jnp.where(index == row, back + back_rows[at + x : at + x + 1], back)
            slope = jnp.where(index == row, slope_rows[at + x + 1 : at + x + 2], slope)
        value = (back * slope).astype(BF16)
        rows = jnp.concatenate([value[:, :128].T, value[:, 128:].T], axis=0)
        out_ref[:, x * size_z : (x + 1) * size_z] = rows[C : 5 * C, :]


def collect(left, ref, size_x, skip, offset):
    tiles = [jnp.zeros((C, 128), F32) for _ in range(7)]
    lanes = lax.broadcasted_iota(jnp.int32, (C, 128), 1)
    for dx in range(3):
        for dz in range(3):
            block = jnp.dot(left, stack(ref, dz, dx + skip, size_x), preferred_element_type=F32)
            total = None
            for y in range(4):
                part = block[y * C : (y + 1) * C, :]
                shift = (256 - (y + offset) * C) % 256
                part = pltpu.roll(part, shift, 1) if shift else part
                total = part if total is None else total + part
            total = total[:, :128]
            for dy in range(3):
                tap = 9 * dx + 3 * dy + dz
                shift = ((tap - dy) * C) % 128
                moved = pltpu.roll(total, shift, 1) if shift else total
                at = (tap % 4) * C
                tiles[tap // 4] = jnp.where((lanes >= at) & (lanes < at + C), moved, tiles[tap // 4])
    return jnp.concatenate(tiles, axis=1)


def weight_grad(give, xs_ref, xs_edge, hid_ref, hid_edge, pre_grad_ref, rows_ref, out_ref):
    size_x = rows_ref.shape[0]
    even = even_index("gz")

    @pl.when(even if give else jnp.logical_not(even))
    def _():
        noise_rows = jnp.concatenate([rows_ref[x] for x in range(size_x)], axis=1)
        out_ref[...] = collect(noise_rows, Edged(hid_ref, hid_edge, HIDDEN_TILES), size_x, 0, 0)

    @pl.when(jnp.logical_not(even) if give else even)
    def _():
        out_ref[...] = collect(pre_grad_ref[...], Edged(xs_ref, xs_edge), size_x, 1, 1)


def predict(hid_ref, hid_edge, second_ref, out_ref, acc_ref, a2_ref):
    size_x, size_z = out_ref.shape[0], out_ref.shape[2]
    for t in range(9):
        for yi in range(8):
            band(a2_ref, t * 256 + yi * C, second_ref[t], (yi - 2) * C, 0, 4 * C)
    total = jnp.dot(taps(Edged(hid_ref, hid_edge, HIDDEN_TILES), size_x), a2_ref[...], preferred_element_type=F32)
    acc_ref[...] = total.reshape(size_x, size_z, 128)
    for x in range(size_x):
        out_ref[x] = acc_ref[x].astype(BF16).T


def finish(norm, mine_ref, other_ref, first_ref, second_ref):
    even = even_index("gz")
    mine = mine_ref[...]
    other = other_ref[...]
    first = jnp.where(even, mine, other) * norm
    second = jnp.where(even, other, mine) * norm
    first_ref[...] = (first * first)[:, : 27 * C]
    second_ref[...] = (second * second)[:, : 27 * C]


def first_sum(keep_ref, taken_ref, send_ref):
    send_ref[...] = (keep_ref[...] + taken_ref[...]).astype(BF16)


def round_sum(own_ref, *refs):
    got, out_ref = refs[:-1], refs[-1]
    total = own_ref[...].astype(F32) + got[0][...].astype(F32)
    if len(got) == 3:
        total = total + (got[1][...].astype(F32) + got[2][...].astype(F32))
    out_ref[...] = total.astype(out_ref.dtype)


def flip(x, axis, bit):
    size = lax.axis_size(axis)
    return lax.ppermute(x, axis, [(i, i ^ bit) for i in range(size)])


def masked_swap(x, flip_even, flip_odd):
    target = {}
    for place in all_places():
        to = list(place)
        for axis, bit in flip_odd if place[2] % 2 else flip_even:
            to[AXES.index(axis)] ^= bit
        target[place] = tuple(to)
    return permute(x, target)


def local(inputs, noise, w_first, w_second):
    _, channels, size_x, size_y, size_z = inputs.shape
    cells = size_x * size_y * size_z
    devices = lax.axis_size("gx") * lax.axis_size("gy") * lax.axis_size("gz")
    norm = 1.0 / math.sqrt(cells * devices)
    lanes = size_y * channels

    plane = (size_z, lanes)
    y_sides = 2 if lax.axis_size("gy") > 2 else 1
    y_planes = size_x // 2 + size_x // 4
    face = struct((3,) + plane, BF16)
    y_face = struct((y_planes,) + plane, BF16)
    n_near = 2 + y_sides
    noise_rows, field, wide_noise, *faces = call(
        functools.partial(pack_faces, y_sides),
        [struct((size_x, lanes, size_z), BF16)]
        + [struct((size_x,) + plane, BF16)] * 2
        + [face] * 2
        + [y_face] * y_sides,
    )(jnp.concatenate([inputs, noise], axis=0))
    corners = call(functools.partial(pack_corners, y_sides), [struct((160, 128), BF16)] * (2 * y_sides))(*faces)
    faces = [*faces, *corners]
    moves = [[("gx", side)] for side in range(2)]
    moves += [[("gy", side)] for side in range(y_sides)]
    moves += [[("gx", side), ("gy", k)] for k in range(y_sides) for side in range(2)]
    got = [swap(face, move) for face, move in zip(faces, moves)]

    a1, ab, second = call(
        spread_weights,
        [struct((9 * 256, 256), BF16), struct((9 * 256, 256), BF16), struct((9, C, 128), F32)],
        moved=4_000_000,
    )(jnp.concatenate([w_first, w_second], axis=0))
    *near, a1, ab, second = lax.optimization_barrier((*got[2:n_near], *got[:2], a1, ab, second))
    near = [*near[y_sides:], *near[:y_sides]]
    got = [*call(functools.partial(sort_faces, y_sides), [face] * 2 + [y_face] * 2)(*near), *got[n_near:]]

    n_field, n_noise = size_x + 4, size_x + 2
    z_rows = -(-(2 * n_field + n_noise) // 16) * 16
    low, high, face_a, face_b = call(
        functools.partial(pack_z, y_sides), [struct((z_rows, 256), BF16)] * 4
    )(field, wide_noise, *got)
    z_got = [swap(face, [("gz", side)]) for side, face in enumerate((face_a, face_b))]
    pre_shape = (n_noise, size_z, 256)
    slope_shape = (size_x, size_z, 256)
    xs, pre, back, hidden, slope = call(
        functools.partial(widen, y_sides),
        [
            struct((3, n_field, size_z, 256), BF16),
            struct(pre_shape, F32),
            struct(slope_shape, F32),
            struct((3,) + pre_shape, BF16),
            struct(slope_shape, F32),
        ],
        scratch=[pltpu.VMEM((3,) + pre_shape, BF16)],
        flops=1_000_000_000,
    )(field, wide_noise, *got, a1, ab)
    *z_got, xs, pre, back, hidden, slope = lax.optimization_barrier((*z_got, xs, pre, back, hidden, slope))

    hidden_edge, xs_edge, slope_rows, back_rows = call(
        mend,
        [
            struct((4, n_noise, 16, 256), BF16),
            struct((2, n_field, 16, 256), BF16),
            struct((2 * n_field, 256), F32),
            struct((2 * n_field, 256), F32),
        ],
    )(pre, hidden, xs, low, high, a1, ab, *z_got)
    pre_grad = call(backward, struct((lanes, size_x * size_z), BF16))(back, slope, slope_rows, back_rows)

    half = struct((C, 896), F32)
    rounded = struct((C, 896), BF16)
    parts = (xs, xs_edge, hidden, hidden_edge, pre_grad, noise_rows)
    give = call(functools.partial(weight_grad, True), half, flops=1_000_000_000)(*parts)
    taken = flip(give, "gz", 1)
    keep = call(functools.partial(weight_grad, False), half, flops=1_000_000_000)(*parts)
    send = call(first_sum, rounded)(keep, taken)

    prediction_rows = call(
        predict,
        struct((size_x, lanes, size_z), BF16),
        scratch=[pltpu.VMEM((size_x, size_z, lanes), F32), pltpu.VMEM((9 * 256, 128), BF16)],
        flops=500_000_000,
    )(hidden, hidden_edge, second)
    prediction = prediction_rows.reshape(size_x, size_y, channels, size_z).transpose(2, 0, 1, 3)[None]

    steps = []
    for axis, start in (("gx", 1), ("gz", 2), ("gy", 1)):
        bit = start
        while bit < lax.axis_size(axis):
            steps.append((axis, bit))
            bit *= 2
    rounds = [steps[k : k + 2] for k in range(0, len(steps), 2)]
    turn = len(rounds) // 2 if len(steps) % 2 == 0 else 0
    for k, even in enumerate(rounds):
        odd = rounds[(k + turn) % len(rounds)]
        flips = [(even[:1], odd[:1])]
        if len(even) == 2:
            flips += [(even[1:], odd[1:]), (even, odd)]
        got = [masked_swap(send, *pair) for pair in flips]
        if k == 0:
            *got, prediction = lax.optimization_barrier((*got, prediction))
        send = call(round_sum, half if k == len(rounds) - 1 else rounded)(send, *got)
    mine = send
    other = flip(mine, "gz", 1)
    fisher_first, fisher_second = call(
        functools.partial(finish, norm), [struct((C, 27 * C), F32)] * 2
    )(mine, other)
    return prediction, fisher_first, fisher_second


def solution(mesh):
    in_specs = (P(None, None, "gx", "gy", "gz"), P(None, None, "gx", "gy", "gz"), P(), P())
    out_specs = (P(None, None, "gx", "gy", "gz"), P(), P())
    return jax.shard_map(local, mesh=mesh, in_specs=in_specs, out_specs=out_specs, check_vma=False)
```

```python
import functools
import math

import jax
import jax.numpy as jnp
from jax import lax
from jax.experimental import pallas as pl
from jax.experimental.pallas import tpu as pltpu
from jax.sharding import PartitionSpec as P

F32 = jnp.float32
BF16 = jnp.bfloat16
C = 32


def call(body, out_shapes, scratch=(), flops=1_000_000, moved=1_000_000, vmem=24, **more):
    return pl.pallas_call(
        body,
        **more,
        out_shape=out_shapes,
        scratch_shapes=list(scratch),
        compiler_params=pltpu.CompilerParams(vmem_limit_bytes=vmem * 1024 * 1024),
        cost_estimate=pl.CostEstimate(flops=flops, bytes_accessed=moved, transcendentals=0),
    )


def struct(shape, dtype):
    return jax.ShapeDtypeStruct(shape, dtype)


def even_index(axis):
    return lax.rem(lax.axis_index(axis), 2) == 0


def partner(index, side, size):
    other = index ^ 1 if side == 0 else ((index + 1) ^ 1) - 1
    return other if 0 <= other < size else None


AXES = ("gx", "gy", "gz")


def all_places():
    sizes = [lax.axis_size(axis) for axis in AXES]
    return [(i, j, k) for i in range(sizes[0]) for j in range(sizes[1]) for k in range(sizes[2])]


def permute(x, target):
    sizes = [lax.axis_size(axis) for axis in AXES]
    number = lambda place: (place[0] * sizes[1] + place[1]) * sizes[2] + place[2]
    return lax.ppermute(x, AXES, [(number(place), number(to)) for place, to in target.items()])


def swap(x, moves):
    sizes = [lax.axis_size(axis) for axis in AXES]
    side = dict(moves)
    places = all_places()
    target = {}
    for place in places:
        to = [partner(i, side[axis], size) if axis in side else i for i, axis, size in zip(place, AXES, sizes)]
        if None not in to:
            target[place] = tuple(to)
    if not target:
        return None
    alone = [place for place in places if place not in target]
    fills = (
        lambda i, j, k: (i, j, k ^ 2),
        lambda i, j, k: (i, j ^ 1, k),
        lambda i, j, k: (i ^ 1, j, k),
        lambda i, j, k: (i, j, k),
    )
    for fill in fills:
        if all(fill(*place) in alone for place in alone):
            target.update({place: fill(*place) for place in alone})
            break
    return permute(x, target)


def choose(flag, a, b):
    if a is None and b is None:
        return None
    a = jnp.zeros_like(b) if a is None else a
    b = jnp.zeros_like(a) if b is None else b
    return jnp.where(flag, a, b)


def pack_faces(y_sides, raw_ref, noise_rows_ref, field_ref, wide_noise_ref, *faces):
    size_x, size_z = raw_ref.shape[2], raw_ref.shape[4]
    lanes = raw_ref.shape[1] * raw_ref.shape[3]
    for x in range(size_x):
        for a, ref in enumerate((field_ref, wide_noise_ref)):
            rows = jnp.transpose(raw_ref[a, :, x].astype(F32), (1, 0, 2)).reshape(lanes, size_z).astype(BF16)
            if a:
                noise_rows_ref[x] = rows
            ref[x] = rows.T
    face_x, face_y = faces[:2], faces[2:]
    even = even_index("gx")
    for side in range(2):
        high = even if side == 0 else jnp.logical_not(even)
        face_x[side][0] = jnp.where(high, field_ref[size_x - 2], field_ref[0])
        face_x[side][1] = jnp.where(high, field_ref[size_x - 1], field_ref[1])
        face_x[side][2] = jnp.where(high, wide_noise_ref[size_x - 1], wide_noise_ref[0])
    even = even_index("gy")
    for k in range(y_sides):
        two, one = cut_y(even if k == 0 else jnp.logical_not(even))
        for j in range(0, size_x, 2):
            face_y[k][j // 2] = jnp.concatenate([two(field_ref[j]), two(field_ref[j + 1])], axis=1)
        for j in range(0, size_x, 4):
            face_y[k][size_x // 2 + j // 4] = jnp.concatenate([one(wide_noise_ref[j + i]) for i in range(4)], axis=1)


def cut_y(high):
    two = lambda p: jnp.where(high, p[:, p.shape[1] - 2 * C :], p[:, : 2 * C])
    one = lambda p: jnp.where(high, p[:, p.shape[1] - C :], p[:, :C])
    return two, one


def pack_corners(y_sides, face_0, face_1, *refs):
    corners = refs[y_sides:]
    even = even_index("gy")
    for k in range(y_sides):
        two, one = cut_y(even if k == 0 else jnp.logical_not(even))
        for side, face in enumerate((face_0, face_1)):
            ref = corners[2 * k + side]
            ref[:128] = jnp.concatenate([two(face[0]), two(face[1])], axis=1)
            strip = one(face[2])
            ref[128:] = jnp.concatenate([strip[i * 32 : (i + 1) * 32] for i in range(4)], axis=1)


def sort_faces(y_sides, *refs):
    x_refs, y_refs, out = refs[:2], list(refs[2 : 2 + y_sides]), refs[2 + y_sides :]
    y_refs += [None] * (2 - y_sides)
    for axis, pair, below_ref, above_ref in (("gx", x_refs, *out[:2]), ("gy", y_refs, *out[2:])):
        even = even_index(axis)
        index = lax.axis_index(axis)
        side_0, side_1 = [None if ref is None else ref[...] for ref in pair]
        below, above = choose(even, side_1, side_0), choose(even, side_0, side_1)
        below_ref[...] = jnp.where(index == 0, jnp.zeros_like(below), below)
        above_ref[...] = jnp.where(index == lax.axis_size(axis) - 1, jnp.zeros_like(above), above)


class Pieces:
    def __init__(self, y_sides, field, noise, face_x, face_y, corner):
        self.field, self.noise = field, noise
        self.size_x, self.size_z = field.shape[0], field.shape[1]
        even_x, even_y = even_index("gx"), even_index("gy")
        self.flag_x = {"below": even_x, "above": jnp.logical_not(even_x)}
        self.flag_y = {"below": even_y, "above": jnp.logical_not(even_y)}
        ends = lambda axis: (lax.axis_index(axis) == 0, lax.axis_index(axis) == lax.axis_size(axis) - 1)
        self.outside_x = dict(zip(("below", "above"), ends("gx")))
        self.outside_y = dict(zip(("below", "above"), ends("gy")))
        self.face_x = dict(zip(("below", "above"), face_x))
        self.face_y = dict(zip(("below", "above"), face_y))
        self.corner = [list(corner[2 * k : 2 * k + 2]) for k in range(y_sides)] + [[None, None]] * (2 - y_sides)

    def from_x(self, where, index, rows):
        return self.face_x[where][index, rows]

    def from_y(self, where, read):
        return read(self.face_y[where])

    def from_corner(self, where_x, where_y, read):
        a = []
        for pair in self.corner:
            if pair[0] is None:
                a.append(None)
            else:
                a.append(choose(self.flag_x[where_x], read(pair[1]), read(pair[0])))
        value = choose(self.flag_y[where_y], a[1], a[0])
        outside = self.outside_x[where_x] | self.outside_y[where_y]
        return jnp.where(outside, jnp.zeros_like(value), value)

    def side_of(self, x, width):
        if x < width:
            return "below", x
        if x >= self.size_x + width:
            return "above", x - self.size_x - width
        return "own", x - width

    def field_plane(self, x, z0, z1):
        rows = slice(z0, z1)
        where, i = self.side_of(x, 2)
        if where == "own":
            middle = self.field[i, rows]
            read = lambda ref: ref[i // 2, rows, (i % 2) * 2 * C : (i % 2 + 1) * 2 * C]
            low, high = self.from_y("below", read), self.from_y("above", read)
        else:
            middle = self.from_x(where, i, rows)
            read = lambda ref: ref[rows, i * 2 * C : (i + 1) * 2 * C]
            low, high = self.from_corner(where, "below", read), self.from_corner(where, "above", read)
        return jnp.concatenate([low, middle, high], axis=1)

    def noise_plane(self, x, z0, z1):
        rows = slice(z0, z1)
        where, i = self.side_of(x, 1)
        if where == "own":
            middle = self.noise[i, rows]
            read = lambda ref: ref[self.size_x // 2 + i // 4, rows, (i % 4) * C : (i % 4 + 1) * C]
            low, high = self.from_y("below", read), self.from_y("above", read)
        else:
            middle = self.from_x(where, 2, rows)

            def read(ref):
                parts = []
                for b in range(4):
                    first, last = max(z0, b * 32), min(z1, (b + 1) * 32)
                    if first < last:
                        parts.append(ref[128 + first - b * 32 : 128 + last - b * 32, b * C : (b + 1) * C])
                return jnp.concatenate(parts, axis=0) if len(parts) > 1 else parts[0]

            low, high = self.from_corner(where, "below", read), self.from_corner(where, "above", read)
        return jnp.concatenate([low, middle, high, jnp.zeros((z1 - z0, 2 * C), BF16)], axis=1)


def take_pieces(y_sides, refs):
    n = 6 + 2 * y_sides
    return Pieces(y_sides, refs[0], refs[1], refs[2:4], refs[4:6], refs[6:n]), refs[n:]


def pack_z(y_sides, *refs):
    pieces, (low_out, high_out, face_a, face_b) = take_pieces(y_sides, refs)
    n_field, n_noise, size_z = pieces.size_x + 4, pieces.size_x + 2, pieces.size_z

    def gather(tile, first, noise_row):
        planes = [pieces.field_plane(x, tile, tile + 16).astype(F32) for x in range(n_field)]
        rows = [plane[first + k - tile : first + k - tile + 1] for k in range(2) for plane in planes]
        for x in range(n_noise):
            rows.append(pieces.noise_plane(x, tile, tile + 16).astype(F32)[noise_row - tile : noise_row - tile + 1])
        while len(rows) % 16:
            rows.append(jnp.zeros_like(rows[0]))
        return jnp.concatenate(rows, axis=0).astype(BF16)

    low = gather(0, 0, 0)
    high = gather(size_z - 16, size_z - 2, size_z - 1)
    low_out[...] = low
    high_out[...] = high
    even = even_index("gz")
    face_a[...] = jnp.where(even, high, low)
    face_b[...] = jnp.where(even, low, high)


def stack(ref, dz, first, count):
    if isinstance(ref, Edged):
        return ref.stack(dz, first, count)
    return ref[dz, first : first + count].reshape(count * ref.shape[2], 256)


def taps(ref, count):
    return jnp.concatenate([stack(ref, dz, dx, count) for dx in range(3) for dz in range(3)], axis=1)


def widen(y_sides, *refs):
    pieces, (a1_ref, ab_ref, xs_ref, pre_ref, back_ref, hid_ref, slope_ref, ns_ref) = take_pieces(y_sides, refs)
    size_z = pieces.size_z
    for ref, read in ((xs_ref, pieces.field_plane), (ns_ref, pieces.noise_plane)):
        for x in range(ref.shape[1]):
            plane = read(x, 0, size_z)
            ref[1, x] = plane
            ref[0, x] = shifted(plane, 0.0, True)
            ref[2, x] = shifted(plane, 0.0, False)
    n_noise = pre_ref.shape[0]
    total = jnp.dot(taps(xs_ref, n_noise), a1_ref[...], preferred_element_type=F32)
    pre_ref[...] = total.reshape(n_noise, size_z, 256)
    size_x = back_ref.shape[0]
    total = jnp.dot(taps(ns_ref, size_x), ab_ref[...], preferred_element_type=F32)
    back_ref[...] = total.reshape(size_x, size_z, 256)

    index = lax.axis_index("gx")
    for x in range(n_noise):
        value = pre_ref[x]
        hidden, s = silu_parts(value)
        gone = outside_y()
        if x == 0:
            gone = gone | (index == 0)
        if x == n_noise - 1:
            gone = gone | (index == lax.axis_size("gx") - 1)
        hidden = jnp.where(gone, 0.0, hidden).astype(BF16)
        hid_ref[1, x] = hidden
        hid_ref[0, x] = shifted(hidden, 0.0, True)
        hid_ref[2, x] = shifted(hidden, 0.0, False)
        if 1 <= x <= size_x:
            slope_ref[x - 1] = slope_of(value, s)


def band(ref, row, taps, shift, lo, hi):
    moved = pltpu.roll(taps, shift % 128, 1) if shift % 128 else taps
    lane = lax.broadcasted_iota(jnp.int32, moved.shape, 1)
    for half in range(ref.shape[1] // 128):
        first = max(shift, lo) - 128 * half
        last = min(shift + 3 * C, hi) - 128 * half
        if last <= 0 or first >= 128:
            value = jnp.zeros_like(moved)
        else:
            value = jnp.where((lane >= first) & (lane < last), moved, 0.0)
        ref[row : row + C, half * 128 : (half + 1) * 128] = value.astype(BF16)


def spread_weights(both_ref, a1_ref, ab_ref, second_out):
    def columns(rows):
        wide = both_ref[rows].astype(F32)
        return jnp.concatenate([wide, jnp.zeros((C, 896 - wide.shape[1]), F32)], axis=1)

    def transposed(wide):
        return jnp.concatenate([wide[:, t * 128 : (t + 1) * 128].T for t in range(7)], axis=0)

    first = transposed(columns(slice(0, C)))
    second_rows = columns(slice(C, 2 * C))
    second = transposed(second_rows)
    fill = jnp.zeros((C, C), F32)
    for dx in range(3):
        for dz in range(3):
            t = 3 * dx + dz
            picks = [9 * dx + 3 * dy + dz for dy in range(3)]
            one = jnp.concatenate([first[k * C : (k + 1) * C, :] for k in picks[::-1]] + [fill], axis=1)
            two = jnp.concatenate([second[k * C : (k + 1) * C, :] for k in picks[::-1]] + [fill], axis=1)
            second_out[t] = two
            picks = [9 * (2 - dx) + 3 * dy + 2 - dz for dy in range(3)]
            back = jnp.concatenate([second_rows[:, k * C : (k + 1) * C] for k in picks] + [fill], axis=1)
            for yi in range(8):
                band(a1_ref, t * 256 + yi * C, one, (yi - 2) * C, 0, 6 * C)
            for yi in range(8):
                if yi < 6:
                    band(ab_ref, t * 256 + yi * C, back, (yi - 1) * C, C, 5 * C)
                else:
                    ab_ref[t * 256 + yi * C : t * 256 + (yi + 1) * C, :] = jnp.zeros((C, 256), BF16)


def shifted(plane, row, down):
    wide = plane.astype(F32)
    rows = wide.shape[0]
    index = lax.broadcasted_iota(jnp.int32, wide.shape, 0)
    if down:
        moved, place = pltpu.roll(wide, 1, 0), 0
    else:
        moved, place = pltpu.roll(wide, rows - 1, 0), rows - 1
    return jnp.where(index == place, row, moved).astype(BF16)


def silu_parts(value):
    s = 0.5 + 0.5 * jnp.tanh(0.5 * value)
    return value * s, s


def edge_tile(ref, dz, x, row):
    rows = ref.shape[2]
    at = slice(rows - 16, rows) if dz else slice(0, 16)
    tile = ref[dz, x, at, :].astype(F32)
    index = lax.broadcasted_iota(jnp.int32, tile.shape, 0)
    return jnp.where(index == (15 if dz else 0), row, tile).astype(BF16)


class Edged:
    def __init__(self, ref, edge_ref, tiles=((0, None), (None, None), (None, 1))):
        self.ref, self.edge_ref, self.tiles = ref, edge_ref, tiles

    def stack(self, dz, first, count):
        parts = []
        begin, end = self.tiles[dz]
        size_z = self.ref.shape[2]
        for x in range(first, first + count):
            if begin is not None:
                parts.append(self.edge_ref[begin, x])
            parts.append(self.ref[dz, x, 0 if begin is None else 16 : size_z if end is None else size_z - 16])
            if end is not None:
                parts.append(self.edge_ref[end, x])
        return jnp.concatenate(parts, axis=0)


HIDDEN_TILES = ((0, None), (1, 2), (None, 3))


def outside_y():
    lane = lax.broadcasted_iota(jnp.int32, (1, 256), 1)
    index = lax.axis_index("gy")
    return ((lane < C) & (index == 0)) | ((lane >= 5 * C) & (index == lax.axis_size("gy") - 1))


def slope_of(value, s):
    return s * (1.0 + value * (1.0 - s))


def mend(
    pre_ref, hid_ref, wide_field_ref, low_ref, high_ref, a1_ref, ab_ref, side_0, side_1, hid_edge, xs_edge, slope_rows, back_rows
):
    n_field, size_z = wide_field_ref.shape[1], wide_field_ref.shape[2]
    n_noise = pre_ref.shape[0]
    even = even_index("gz")
    own_low = low_ref[...].astype(F32)
    own_high = high_ref[...].astype(F32)

    gx, gz = lax.axis_index("gx"), lax.axis_index("gz")
    first_x, last_x = gx == 0, gx == lax.axis_size("gx") - 1
    first_z, last_z = gz == 0, gz == lax.axis_size("gz") - 1
    below_rows = jnp.where(first_z, 0.0, jnp.where(even, side_1[...], side_0[...]).astype(F32))
    above_rows = jnp.where(last_z, 0.0, jnp.where(even, side_0[...], side_1[...]).astype(F32))

    before = jnp.concatenate([below_rows[:n_field], own_high[n_field : 2 * n_field]], axis=0).astype(BF16)
    halo = jnp.concatenate([below_rows[n_field : 2 * n_field], above_rows[:n_field]], axis=0).astype(BF16)
    after = jnp.concatenate([own_low[:n_field], above_rows[n_field : 2 * n_field]], axis=0).astype(BF16)
    base = 2 * n_field
    noise_halo = jnp.concatenate(
        [below_rows[base : base + n_field], above_rows[base : base + n_field]], axis=0
    ).astype(BF16)
    rows = 2 * n_field
    edge_total, row_total, back_total = None, None, None
    for dx in range(3):
        at = lambda ref, dz: ref[(3 * dx + dz) * 256 : (3 * dx + dz + 1) * 256]
        first = jnp.dot(jnp.concatenate([before, halo], axis=0), at(a1_ref, 0), preferred_element_type=F32)
        middle = jnp.dot(halo, at(a1_ref, 1), preferred_element_type=F32)
        last = jnp.dot(jnp.concatenate([after, halo], axis=0), at(a1_ref, 2), preferred_element_type=F32)
        back_first = jnp.dot(noise_halo, at(ab_ref, 0), preferred_element_type=F32)
        back_last = jnp.dot(noise_halo, at(ab_ref, 2), preferred_element_type=F32)
        edge = first[:rows] + middle + last[:rows]
        row = jnp.concatenate([first[rows : rows + n_field], last[rows + n_field :]], axis=0)
        back = jnp.concatenate([back_first[:n_field], back_last[n_field:]], axis=0)
        if dx:
            edge, row, back = [pltpu.roll(part, rows - dx, 0) for part in (edge, row, back)]
        edge_total = edge if edge_total is None else edge_total + edge
        row_total = row if row_total is None else row_total + row
        back_total = back if back_total is None else back_total + back
    back_rows[...] = back_total

    index = lax.broadcasted_iota(jnp.int32, (rows, 256), 0)
    x_row = jnp.where(index < n_field, index, index - n_field)
    drop = outside_y() | ((x_row == 0) & first_x) | ((x_row == n_noise - 1) & last_x)
    drop_edge = drop | ((index < n_field) & first_z) | ((index >= n_field) & last_z)
    edge_hidden = jnp.where(drop_edge, 0.0, silu_parts(edge_total)[0]).astype(BF16).astype(F32)

    zeros = [jnp.zeros((1, 256), F32)] * (n_field - n_noise)
    ends = [pre_ref[x, 0:8][0:1] for x in range(n_noise)] + zeros
    ends += [pre_ref[x, size_z - 8 :][7:8] for x in range(n_noise)] + zeros
    value = jnp.concatenate(ends, axis=0) + row_total
    row_hidden, s = silu_parts(value)
    row_hidden = jnp.where(drop, 0.0, row_hidden).astype(BF16).astype(F32)
    slope_rows[...] = slope_of(value, s)

    tile_row = lax.broadcasted_iota(jnp.int32, (16, 256), 0)
    for x in range(n_noise):
        low, high = row_hidden[x : x + 1], row_hidden[n_field + x : n_field + x + 1]
        below, above = edge_hidden[x : x + 1], edge_hidden[n_field + x : n_field + x + 1]
        begin = [hid_ref[dz, x, 0:16].astype(F32) for dz in range(2)]
        end = [hid_ref[dz, x, size_z - 16 :].astype(F32) for dz in range(1, 3)]
        hid_edge[0, x] = jnp.where(tile_row == 0, below, jnp.where(tile_row == 1, low, begin[0])).astype(BF16)
        hid_edge[1, x] = jnp.where(tile_row == 0, low, begin[1]).astype(BF16)
        hid_edge[2, x] = jnp.where(tile_row == 15, high, end[0]).astype(BF16)
        hid_edge[3, x] = jnp.where(tile_row == 15, above, jnp.where(tile_row == 14, high, end[1])).astype(BF16)
    for x in range(n_field):
        xs_edge[0, x] = edge_tile(wide_field_ref, 0, x, below_rows[n_field + x : n_field + x + 1])
        xs_edge[1, x] = edge_tile(wide_field_ref, 2, x, above_rows[x : x + 1])


def backward(back_ref, slope_ref, slope_rows, back_rows, out_ref):
    size_x, size_z = slope_ref.shape[:2]
    half = slope_rows.shape[0] // 2
    index = lax.broadcasted_iota(jnp.int32, (size_z, 256), 0)
    for x in range(size_x):
        back, slope = back_ref[x], slope_ref[x]
        for row, at in ((0, 0), (size_z - 1, half)):
            back = jnp.where(index == row, back + back_rows[at + x : at + x + 1], back)
            slope = jnp.where(index == row, slope_rows[at + x + 1 : at + x + 2], slope)
        value = (back * slope).astype(BF16)
        rows = jnp.concatenate([value[:, :128].T, value[:, 128:].T], axis=0)
        out_ref[:, x * size_z : (x + 1) * size_z] = rows[C : 5 * C, :]


def collect(left, ref, size_x, skip, offset):
    tiles = [jnp.zeros((C, 128), F32) for _ in range(7)]
    lanes = lax.broadcasted_iota(jnp.int32, (C, 128), 1)
    for dx in range(3):
        for dz in range(3):
            block = jnp.dot(left, stack(ref, dz, dx + skip, size_x), preferred_element_type=F32)
            total = None
            for y in range(4):
                part = block[y * C : (y + 1) * C, :]
                shift = (256 - (y + offset) * C) % 256
                part = pltpu.roll(part, shift, 1) if shift else part
                total = part if total is None else total + part
            total = total[:, :128]
            for dy in range(3):
                tap = 9 * dx + 3 * dy + dz
                shift = ((tap - dy) * C) % 128
                moved = pltpu.roll(total, shift, 1) if shift else total
                at = (tap % 4) * C
                tiles[tap // 4] = jnp.where((lanes >= at) & (lanes < at + C), moved, tiles[tap // 4])
    return jnp.concatenate(tiles, axis=1)


def weight_grad(give, xs_ref, xs_edge, hid_ref, hid_edge, pre_grad_ref, rows_ref, out_ref):
    size_x = rows_ref.shape[0]
    even = even_index("gz")

    @pl.when(even if give else jnp.logical_not(even))
    def _():
        noise_rows = jnp.concatenate([rows_ref[x] for x in range(size_x)], axis=1)
        out_ref[...] = collect(noise_rows, Edged(hid_ref, hid_edge, HIDDEN_TILES), size_x, 0, 0)

    @pl.when(jnp.logical_not(even) if give else even)
    def _():
        out_ref[...] = collect(pre_grad_ref[...], Edged(xs_ref, xs_edge), size_x, 1, 1)


def predict(hid_ref, hid_edge, second_ref, out_ref, acc_ref, a2_ref):
    size_x, size_z = out_ref.shape[0], out_ref.shape[2]
    for t in range(9):
        for yi in range(8):
            band(a2_ref, t * 256 + yi * C, second_ref[t], (yi - 2) * C, 0, 4 * C)
    total = jnp.dot(taps(Edged(hid_ref, hid_edge, HIDDEN_TILES), size_x), a2_ref[...], preferred_element_type=F32)
    acc_ref[...] = total.reshape(size_x, size_z, 128)
    for x in range(size_x):
        out_ref[x] = acc_ref[x].astype(BF16).T


def finish(norm, mine_ref, other_ref, first_ref, second_ref):
    even = even_index("gz")
    mine = mine_ref[...]
    other = other_ref[...]
    first = jnp.where(even, mine, other) * norm
    second = jnp.where(even, other, mine) * norm
    first_ref[...] = (first * first)[:, : 27 * C]
    second_ref[...] = (second * second)[:, : 27 * C]


def first_sum(keep_ref, taken_ref, send_ref):
    send_ref[...] = (keep_ref[...] + taken_ref[...]).astype(BF16)


def round_sum(own_ref, *refs):
    got, out_ref = refs[:-1], refs[-1]
    total = own_ref[...].astype(F32) + got[0][...].astype(F32)
    if len(got) == 3:
        total = total + (got[1][...].astype(F32) + got[2][...].astype(F32))
    out_ref[...] = total.astype(out_ref.dtype)


def flip(x, axis, bit):
    size = lax.axis_size(axis)
    return lax.ppermute(x, axis, [(i, i ^ bit) for i in range(size)])


def masked_swap(x, flip_even, flip_odd):
    target = {}
    for place in all_places():
        to = list(place)
        for axis, bit in flip_odd if place[2] % 2 else flip_even:
            to[AXES.index(axis)] ^= bit
        target[place] = tuple(to)
    return permute(x, target)


def local(inputs, noise, w_first, w_second):
    _, channels, size_x, size_y, size_z = inputs.shape
    cells = size_x * size_y * size_z
    devices = lax.axis_size("gx") * lax.axis_size("gy") * lax.axis_size("gz")
    norm = 1.0 / math.sqrt(cells * devices)
    lanes = size_y * channels

    plane = (size_z, lanes)
    y_sides = 2 if lax.axis_size("gy") > 2 else 1
    y_planes = size_x // 2 + size_x // 4
    face = struct((3,) + plane, BF16)
    y_face = struct((y_planes,) + plane, BF16)
    n_near = 2 + y_sides
    noise_rows, field, wide_noise, *faces = call(
        functools.partial(pack_faces, y_sides),
        [struct((size_x, lanes, size_z), BF16)]
        + [struct((size_x,) + plane, BF16)] * 2
        + [face] * 2
        + [y_face] * y_sides,
    )(jnp.concatenate([inputs, noise], axis=0))
    corners = call(functools.partial(pack_corners, y_sides), [struct((160, 128), BF16)] * (2 * y_sides))(*faces)
    faces = [*faces, *corners]
    moves = [[("gx", side)] for side in range(2)]
    moves += [[("gy", side)] for side in range(y_sides)]
    moves += [[("gx", side), ("gy", k)] for k in range(y_sides) for side in range(2)]
    got = [swap(face, move) for face, move in zip(faces, moves)]

    a1, ab, second = call(
        spread_weights,
        [struct((9 * 256, 256), BF16), struct((9 * 256, 256), BF16), struct((9, C, 128), F32)],
        moved=4_000_000,
    )(jnp.concatenate([w_first, w_second], axis=0))
    *near, a1, ab, second = lax.optimization_barrier((*got[:n_near], a1, ab, second))
    got = [*call(functools.partial(sort_faces, y_sides), [face] * 2 + [y_face] * 2)(*near), *got[n_near:]]

    n_field, n_noise = size_x + 4, size_x + 2
    z_rows = -(-(2 * n_field + n_noise) // 16) * 16
    low, high, face_a, face_b = call(
        functools.partial(pack_z, y_sides), [struct((z_rows, 256), BF16)] * 4
    )(field, wide_noise, *got)
    z_got = [swap(face, [("gz", side)]) for side, face in enumerate((face_a, face_b))]
    pre_shape = (n_noise, size_z, 256)
    slope_shape = (size_x, size_z, 256)
    xs, pre, back, hidden, slope = call(
        functools.partial(widen, y_sides),
        [
            struct((3, n_field, size_z, 256), BF16),
            struct(pre_shape, F32),
            struct(slope_shape, F32),
            struct((3,) + pre_shape, BF16),
            struct(slope_shape, F32),
        ],
        scratch=[pltpu.VMEM((3,) + pre_shape, BF16)],
        flops=1_000_000_000,
    )(field, wide_noise, *got, a1, ab)
    *z_got, xs, pre, back, hidden, slope = lax.optimization_barrier((*z_got[::-1], xs, pre, back, hidden, slope))
    z_got = z_got[::-1]

    hidden_edge, xs_edge, slope_rows, back_rows = call(
        mend,
        [
            struct((4, n_noise, 16, 256), BF16),
            struct((2, n_field, 16, 256), BF16),
            struct((2 * n_field, 256), F32),
            struct((2 * n_field, 256), F32),
        ],
    )(pre, hidden, xs, low, high, a1, ab, *z_got)
    pre_grad = call(backward, struct((lanes, size_x * size_z), BF16))(back, slope, slope_rows, back_rows)

    half = struct((C, 896), F32)
    rounded = struct((C, 896), BF16)
    parts = (xs, xs_edge, hidden, hidden_edge, pre_grad, noise_rows)
    give = call(functools.partial(weight_grad, True), half, flops=1_000_000_000)(*parts)
    taken = flip(give, "gz", 1)
    keep = call(functools.partial(weight_grad, False), half, flops=1_000_000_000)(*parts)
    send = call(first_sum, rounded)(keep, taken)

    prediction_rows = call(
        predict,
        struct((size_x, lanes, size_z), BF16),
        scratch=[pltpu.VMEM((size_x, size_z, lanes), F32), pltpu.VMEM((9 * 256, 128), BF16)],
        flops=500_000_000,
    )(hidden, hidden_edge, second)
    prediction = prediction_rows.reshape(size_x, size_y, channels, size_z).transpose(2, 0, 1, 3)[None]

    steps = []
    for axis, start in (("gx", 1), ("gz", 2), ("gy", 1)):
        bit = start
        while bit < lax.axis_size(axis):
            steps.append((axis, bit))
            bit *= 2
    rounds = [steps[k : k + 2] for k in range(0, len(steps), 2)]
    turn = len(rounds) // 2 if len(steps) % 2 == 0 else 0
    for k, even in enumerate(rounds):
        odd = rounds[(k + turn) % len(rounds)]
        flips = [(even[:1], odd[:1])]
        if len(even) == 2:
            flips = [(even, odd), (even[1:], odd[1:])] + flips
        got = [masked_swap(send, *pair) for pair in flips]
        if k == 0:
            *got, prediction = lax.optimization_barrier((*got, prediction))
        send = call(round_sum, half if k == len(rounds) - 1 else rounded)(send, *got)
    mine = send
    other = flip(mine, "gz", 1)
    fisher_first, fisher_second = call(
        functools.partial(finish, norm), [struct((C, 27 * C), F32)] * 2
    )(mine, other)
    return prediction, fisher_first, fisher_second


def solution(mesh):
    in_specs = (P(None, None, "gx", "gy", "gz"), P(None, None, "gx", "gy", "gz"), P(), P())
    out_specs = (P(None, None, "gx", "gy", "gz"), P(), P())
    return jax.shard_map(local, mesh=mesh, in_specs=in_specs, out_specs=out_specs, check_vma=False)
```

```python
import functools
import math

import jax
import jax.numpy as jnp
from jax import lax
from jax.experimental import pallas as pl
from jax.experimental.pallas import tpu as pltpu
from jax.sharding import PartitionSpec as P

F32 = jnp.float32
BF16 = jnp.bfloat16
C = 32


def call(body, out_shapes, scratch=(), flops=1_000_000, moved=1_000_000):
    return pl.pallas_call(
        body,
        out_shape=out_shapes,
        scratch_shapes=list(scratch),
        compiler_params=pltpu.CompilerParams(vmem_limit_bytes=24 * 1024 * 1024),
        cost_estimate=pl.CostEstimate(flops=flops, bytes_accessed=moved, transcendentals=0),
    )


def struct(shape, dtype):
    return jax.ShapeDtypeStruct(shape, dtype)


def even_index(axis):
    return lax.rem(lax.axis_index(axis), 2) == 0


def partner(index, side, size):
    other = index ^ 1 if side == 0 else ((index + 1) ^ 1) - 1
    return other if 0 <= other < size else None


AXES = ("gx", "gy", "gz")


def all_places():
    sizes = [lax.axis_size(axis) for axis in AXES]
    return [(i, j, k) for i in range(sizes[0]) for j in range(sizes[1]) for k in range(sizes[2])]


def permute(x, target):
    sizes = [lax.axis_size(axis) for axis in AXES]
    number = lambda place: (place[0] * sizes[1] + place[1]) * sizes[2] + place[2]
    return lax.ppermute(x, AXES, [(number(place), number(to)) for place, to in target.items()])


def swap(x, moves):
    sizes = [lax.axis_size(axis) for axis in AXES]
    side = dict(moves)
    places = all_places()
    target = {}
    for place in places:
        to = [partner(i, side[axis], size) if axis in side else i for i, axis, size in zip(place, AXES, sizes)]
        if None not in to:
            target[place] = tuple(to)
    if not target:
        return None
    alone = [place for place in places if place not in target]
    fills = (
        lambda i, j, k: (i, j, k ^ 2),
        lambda i, j, k: (i, j ^ 1, k),
        lambda i, j, k: (i ^ 1, j, k),
        lambda i, j, k: (i, j, k),
    )
    for fill in fills:
        if all(fill(*place) in alone for place in alone):
            target.update({place: fill(*place) for place in alone})
            break
    return permute(x, target)


def choose(flag, a, b):
    if a is None and b is None:
        return None
    a = jnp.zeros_like(b) if a is None else a
    b = jnp.zeros_like(a) if b is None else b
    return jnp.where(flag, a, b)


def pack_faces(y_sides, raw_ref, noise_rows_ref, field_ref, wide_noise_ref, *faces):
    size_x, size_z = raw_ref.shape[2], raw_ref.shape[4]
    lanes = raw_ref.shape[1] * raw_ref.shape[3]
    for x in range(size_x):
        for a, ref in enumerate((field_ref, wide_noise_ref)):
            rows = jnp.transpose(raw_ref[a, :, x].astype(F32), (1, 0, 2)).reshape(lanes, size_z).astype(BF16)
            if a:
                noise_rows_ref[x] = rows
            ref[x] = rows.T
    face_x, face_y = faces[:2], faces[2:]
    even = even_index("gx")
    for side in range(2):
        high = even if side == 0 else jnp.logical_not(even)
        face_x[side][0] = jnp.where(high, field_ref[size_x - 2], field_ref[0])
        face_x[side][1] = jnp.where(high, field_ref[size_x - 1], field_ref[1])
        face_x[side][2] = jnp.where(high, wide_noise_ref[size_x - 1], wide_noise_ref[0])
    even = even_index("gy")
    for k in range(y_sides):
        two, one = cut_y(even if k == 0 else jnp.logical_not(even))
        for j in range(0, size_x, 2):
            face_y[k][j // 2] = jnp.concatenate([two(field_ref[j]), two(field_ref[j + 1])], axis=1)
        for j in range(0, size_x, 4):
            face_y[k][size_x // 2 + j // 4] = jnp.concatenate([one(wide_noise_ref[j + i]) for i in range(4)], axis=1)


def cut_y(high):
    two = lambda p: jnp.where(high, p[:, p.shape[1] - 2 * C :], p[:, : 2 * C])
    one = lambda p: jnp.where(high, p[:, p.shape[1] - C :], p[:, :C])
    return two, one


def pack_corners(y_sides, face_0, face_1, *refs):
    corners = refs[y_sides:]
    even = even_index("gy")
    for k in range(y_sides):
        two, one = cut_y(even if k == 0 else jnp.logical_not(even))
        for side, face in enumerate((face_0, face_1)):
            ref = corners[2 * k + side]
            ref[:128] = jnp.concatenate([two(face[0]), two(face[1])], axis=1)
            strip = one(face[2])
            ref[128:] = jnp.concatenate([strip[i * 32 : (i + 1) * 32] for i in range(4)], axis=1)


def sort_faces(y_sides, *refs):
    x_refs, y_refs, out = refs[:2], list(refs[2 : 2 + y_sides]), refs[2 + y_sides :]
    y_refs += [None] * (2 - y_sides)
    for axis, pair, below_ref, above_ref in (("gx", x_refs, *out[:2]), ("gy", y_refs, *out[2:])):
        even = even_index(axis)
        index = lax.axis_index(axis)
        side_0, side_1 = [None if ref is None else ref[...] for ref in pair]
        below, above = choose(even, side_1, side_0), choose(even, side_0, side_1)
        below_ref[...] = jnp.where(index == 0, jnp.zeros_like(below), below)
        above_ref[...] = jnp.where(index == lax.axis_size(axis) - 1, jnp.zeros_like(above), above)


class Pieces:
    def __init__(self, y_sides, field, noise, face_x, face_y, corner):
        self.field, self.noise = field, noise
        self.size_x, self.size_z = field.shape[0], field.shape[1]
        even_x, even_y = even_index("gx"), even_index("gy")
        self.flag_x = {"below": even_x, "above": jnp.logical_not(even_x)}
        self.flag_y = {"below": even_y, "above": jnp.logical_not(even_y)}
        ends = lambda axis: (lax.axis_index(axis) == 0, lax.axis_index(axis) == lax.axis_size(axis) - 1)
        self.outside_x = dict(zip(("below", "above"), ends("gx")))
        self.outside_y = dict(zip(("below", "above"), ends("gy")))
        self.face_x = dict(zip(("below", "above"), face_x))
        self.face_y = dict(zip(("below", "above"), face_y))
        self.corner = [list(corner[2 * k : 2 * k + 2]) for k in range(y_sides)] + [[None, None]] * (2 - y_sides)

    def from_x(self, where, index, rows):
        return self.face_x[where][index, rows]

    def from_y(self, where, read):
        return read(self.face_y[where])

    def from_corner(self, where_x, where_y, read):
        a = []
        for pair in self.corner:
            if pair[0] is None:
                a.append(None)
            else:
                a.append(choose(self.flag_x[where_x], read(pair[1]), read(pair[0])))
        value = choose(self.flag_y[where_y], a[1], a[0])
        outside = self.outside_x[where_x] | self.outside_y[where_y]
        return jnp.where(outside, jnp.zeros_like(value), value)

    def side_of(self, x, width):
        if x < width:
            return "below", x
        if x >= self.size_x + width:
            return "above", x - self.size_x - width
        return "own", x - width

    def field_plane(self, x, z0, z1):
        rows = slice(z0, z1)
        where, i = self.side_of(x, 2)
        if where == "own":
            middle = self.field[i, rows]
            read = lambda ref: ref[i // 2, rows, (i % 2) * 2 * C : (i % 2 + 1) * 2 * C]
            low, high = self.from_y("below", read), self.from_y("above", read)
        else:
            middle = self.from_x(where, i, rows)
            read = lambda ref: ref[rows, i * 2 * C : (i + 1) * 2 * C]
            low, high = self.from_corner(where, "below", read), self.from_corner(where, "above", read)
        return jnp.concatenate([low, middle, high], axis=1)

    def noise_plane(self, x, z0, z1):
        rows = slice(z0, z1)
        where, i = self.side_of(x, 1)
        if where == "own":
            middle = self.noise[i, rows]
            read = lambda ref: ref[self.size_x // 2 + i // 4, rows, (i % 4) * C : (i % 4 + 1) * C]
            low, high = self.from_y("below", read), self.from_y("above", read)
        else:
            middle = self.from_x(where, 2, rows)

            def read(ref):
                parts = []
                for b in range(4):
                    first, last = max(z0, b * 32), min(z1, (b + 1) * 32)
                    if first < last:
                        parts.append(ref[128 + first - b * 32 : 128 + last - b * 32, b * C : (b + 1) * C])
                return jnp.concatenate(parts, axis=0) if len(parts) > 1 else parts[0]

            low, high = self.from_corner(where, "below", read), self.from_corner(where, "above", read)
        return jnp.concatenate([low, middle, high, jnp.zeros((z1 - z0, 2 * C), BF16)], axis=1)


def take_pieces(y_sides, refs):
    n = 6 + 2 * y_sides
    return Pieces(y_sides, refs[0], refs[1], refs[2:4], refs[4:6], refs[6:n]), refs[n:]


def pack_z(y_sides, *refs):
    pieces, (low_out, high_out, face_a, face_b) = take_pieces(y_sides, refs)
    n_field, n_noise, size_z = pieces.size_x + 4, pieces.size_x + 2, pieces.size_z

    def gather(tile, first, noise_row):
        planes = [pieces.field_plane(x, tile, tile + 16).astype(F32) for x in range(n_field)]
        rows = [plane[first + k - tile : first + k - tile + 1] for k in range(2) for plane in planes]
        for x in range(n_noise):
            rows.append(pieces.noise_plane(x, tile, tile + 16).astype(F32)[noise_row - tile : noise_row - tile + 1])
        while len(rows) % 16:
            rows.append(jnp.zeros_like(rows[0]))
        return jnp.concatenate(rows, axis=0).astype(BF16)

    low = gather(0, 0, 0)
    high = gather(size_z - 16, size_z - 2, size_z - 1)
    low_out[...] = low
    high_out[...] = high
    even = even_index("gz")
    face_a[...] = jnp.where(even, high, low)
    face_b[...] = jnp.where(even, low, high)


def stack(ref, dz, first, count):
    if isinstance(ref, Edged):
        return ref.stack(dz, first, count)
    return ref[dz, first : first + count].reshape(count * ref.shape[2], 256)


def taps(ref, count):
    return jnp.concatenate([stack(ref, dz, dx, count) for dx in range(3) for dz in range(3)], axis=1)


def widen(y_sides, *refs):
    pieces, (a1_ref, ab_ref, xs_ref, pre_ref, back_ref, hid_ref, slope_ref, ns_ref) = take_pieces(y_sides, refs)
    size_z = pieces.size_z
    for ref, read in ((xs_ref, pieces.field_plane), (ns_ref, pieces.noise_plane)):
        for x in range(ref.shape[1]):
            plane = read(x, 0, size_z)
            ref[1, x] = plane
            ref[0, x] = shifted(plane, 0.0, True)
            ref[2, x] = shifted(plane, 0.0, False)
    n_noise = pre_ref.shape[0]
    total = jnp.dot(taps(xs_ref, n_noise), a1_ref[...], preferred_element_type=F32)
    pre_ref[...] = total.reshape(n_noise, size_z, 256)
    size_x = back_ref.shape[0]
    total = jnp.dot(taps(ns_ref, size_x), ab_ref[...], preferred_element_type=F32)
    back_ref[...] = total.reshape(size_x, size_z, 256)

    index = lax.axis_index("gx")
    for x in range(n_noise):
        value = pre_ref[x]
        hidden, s = silu_parts(value)
        gone = outside_y()
        if x == 0:
            gone = gone | (index == 0)
        if x == n_noise - 1:
            gone = gone | (index == lax.axis_size("gx") - 1)
        hidden = jnp.where(gone, 0.0, hidden).astype(BF16)
        hid_ref[1, x] = hidden
        hid_ref[0, x] = shifted(hidden, 0.0, True)
        hid_ref[2, x] = shifted(hidden, 0.0, False)
        if 1 <= x <= size_x:
            slope_ref[x - 1] = slope_of(value, s)


def band(ref, row, taps, shift, lo, hi):
    moved = pltpu.roll(taps, shift % 128, 1) if shift % 128 else taps
    lane = lax.broadcasted_iota(jnp.int32, moved.shape, 1)
    for half in range(ref.shape[1] // 128):
        first = max(shift, lo) - 128 * half
        last = min(shift + 3 * C, hi) - 128 * half
        if last <= 0 or first >= 128:
            value = jnp.zeros_like(moved)
        else:
            value = jnp.where((lane >= first) & (lane < last), moved, 0.0)
        ref[row : row + C, half * 128 : (half + 1) * 128] = value.astype(BF16)


def spread_weights(both_ref, a1_ref, ab_ref, second_out):
    def columns(rows):
        wide = both_ref[rows].astype(F32)
        return jnp.concatenate([wide, jnp.zeros((C, 896 - wide.shape[1]), F32)], axis=1)

    def transposed(wide):
        return jnp.concatenate([wide[:, t * 128 : (t + 1) * 128].T for t in range(7)], axis=0)

    first = transposed(columns(slice(0, C)))
    second_rows = columns(slice(C, 2 * C))
    second = transposed(second_rows)
    fill = jnp.zeros((C, C), F32)
    for dx in range(3):
        for dz in range(3):
            t = 3 * dx + dz
            picks = [9 * dx + 3 * dy + dz for dy in range(3)]
            one = jnp.concatenate([first[k * C : (k + 1) * C, :] for k in picks[::-1]] + [fill], axis=1)
            two = jnp.concatenate([second[k * C : (k + 1) * C, :] for k in picks[::-1]] + [fill], axis=1)
            second_out[t] = two
            picks = [9 * (2 - dx) + 3 * dy + 2 - dz for dy in range(3)]
            back = jnp.concatenate([second_rows[:, k * C : (k + 1) * C] for k in picks] + [fill], axis=1)
            for yi in range(8):
                band(a1_ref, t * 256 + yi * C, one, (yi - 2) * C, 0, 6 * C)
            for yi in range(8):
                if yi < 6:
                    band(ab_ref, t * 256 + yi * C, back, (yi - 1) * C, C, 5 * C)
                else:
                    ab_ref[t * 256 + yi * C : t * 256 + (yi + 1) * C, :] = jnp.zeros((C, 256), BF16)


def shifted(plane, row, down):
    wide = plane.astype(F32)
    rows = wide.shape[0]
    index = lax.broadcasted_iota(jnp.int32, wide.shape, 0)
    if down:
        moved, place = pltpu.roll(wide, 1, 0), 0
    else:
        moved, place = pltpu.roll(wide, rows - 1, 0), rows - 1
    return jnp.where(index == place, row, moved).astype(BF16)


def silu_parts(value):
    s = 0.5 + 0.5 * jnp.tanh(0.5 * value)
    return value * s, s


def edge_tile(ref, dz, x, row):
    rows = ref.shape[2]
    at = slice(rows - 16, rows) if dz else slice(0, 16)
    tile = ref[dz, x, at, :].astype(F32)
    index = lax.broadcasted_iota(jnp.int32, tile.shape, 0)
    return jnp.where(index == (15 if dz else 0), row, tile).astype(BF16)


class Edged:
    def __init__(self, ref, edge_ref, tiles=((0, None), (None, None), (None, 1))):
        self.ref, self.edge_ref, self.tiles = ref, edge_ref, tiles

    def stack(self, dz, first, count):
        parts = []
        begin, end = self.tiles[dz]
        size_z = self.ref.shape[2]
        for x in range(first, first + count):
            if begin is not None:
                parts.append(self.edge_ref[begin, x])
            parts.append(self.ref[dz, x, 0 if begin is None else 16 : size_z if end is None else size_z - 16])
            if end is not None:
                parts.append(self.edge_ref[end, x])
        return jnp.concatenate(parts, axis=0)


HIDDEN_TILES = ((0, None), (1, 2), (None, 3))


def outside_y():
    lane = lax.broadcasted_iota(jnp.int32, (1, 256), 1)
    index = lax.axis_index("gy")
    return ((lane < C) & (index == 0)) | ((lane >= 5 * C) & (index == lax.axis_size("gy") - 1))


def slope_of(value, s):
    return s * (1.0 + value * (1.0 - s))


def mend(
    pre_ref, hid_ref, wide_field_ref, low_ref, high_ref, a1_ref, ab_ref, side_0, side_1, hid_edge, xs_edge, slope_rows, back_rows
):
    n_field, size_z = wide_field_ref.shape[1], wide_field_ref.shape[2]
    n_noise = pre_ref.shape[0]
    even = even_index("gz")
    own_low = low_ref[...].astype(F32)
    own_high = high_ref[...].astype(F32)

    gx, gz = lax.axis_index("gx"), lax.axis_index("gz")
    first_x, last_x = gx == 0, gx == lax.axis_size("gx") - 1
    first_z, last_z = gz == 0, gz == lax.axis_size("gz") - 1
    below_rows = jnp.where(first_z, 0.0, jnp.where(even, side_1[...], side_0[...]).astype(F32))
    above_rows = jnp.where(last_z, 0.0, jnp.where(even, side_0[...], side_1[...]).astype(F32))

    before = jnp.concatenate([below_rows[:n_field], own_high[n_field : 2 * n_field]], axis=0).astype(BF16)
    halo = jnp.concatenate([below_rows[n_field : 2 * n_field], above_rows[:n_field]], axis=0).astype(BF16)
    after = jnp.concatenate([own_low[:n_field], above_rows[n_field : 2 * n_field]], axis=0).astype(BF16)
    base = 2 * n_field
    noise_halo = jnp.concatenate(
        [below_rows[base : base + n_field], above_rows[base : base + n_field]], axis=0
    ).astype(BF16)
    rows = 2 * n_field
    edge_total, row_total, back_total = None, None, None
    for dx in range(3):
        at = lambda ref, dz: ref[(3 * dx + dz) * 256 : (3 * dx + dz + 1) * 256]
        first = jnp.dot(jnp.concatenate([before, halo], axis=0), at(a1_ref, 0), preferred_element_type=F32)
        middle = jnp.dot(halo, at(a1_ref, 1), preferred_element_type=F32)
        last = jnp.dot(jnp.concatenate([after, halo], axis=0), at(a1_ref, 2), preferred_element_type=F32)
        back_first = jnp.dot(noise_halo, at(ab_ref, 0), preferred_element_type=F32)
        back_last = jnp.dot(noise_halo, at(ab_ref, 2), preferred_element_type=F32)
        edge = first[:rows] + middle + last[:rows]
        row = jnp.concatenate([first[rows : rows + n_field], last[rows + n_field :]], axis=0)
        back = jnp.concatenate([back_first[:n_field], back_last[n_field:]], axis=0)
        if dx:
            edge, row, back = [pltpu.roll(part, rows - dx, 0) for part in (edge, row, back)]
        edge_total = edge if edge_total is None else edge_total + edge
        row_total = row if row_total is None else row_total + row
        back_total = back if back_total is None else back_total + back
    back_rows[...] = back_total

    index = lax.broadcasted_iota(jnp.int32, (rows, 256), 0)
    x_row = jnp.where(index < n_field, index, index - n_field)
    drop = outside_y() | ((x_row == 0) & first_x) | ((x_row == n_noise - 1) & last_x)
    drop_edge = drop | ((index < n_field) & first_z) | ((index >= n_field) & last_z)
    edge_hidden = jnp.where(drop_edge, 0.0, silu_parts(edge_total)[0]).astype(BF16).astype(F32)

    zeros = [jnp.zeros((1, 256), F32)] * (n_field - n_noise)
    ends = [pre_ref[x, 0:8][0:1] for x in range(n_noise)] + zeros
    ends += [pre_ref[x, size_z - 8 :][7:8] for x in range(n_noise)] + zeros
    value = jnp.concatenate(ends, axis=0) + row_total
    row_hidden, s = silu_parts(value)
    row_hidden = jnp.where(drop, 0.0, row_hidden).astype(BF16).astype(F32)
    slope_rows[...] = slope_of(value, s)

    tile_row = lax.broadcasted_iota(jnp.int32, (16, 256), 0)
    for x in range(n_noise):
        low, high = row_hidden[x : x + 1], row_hidden[n_field + x : n_field + x + 1]
        below, above = edge_hidden[x : x + 1], edge_hidden[n_field + x : n_field + x + 1]
        begin = [hid_ref[dz, x, 0:16].astype(F32) for dz in range(2)]
        end = [hid_ref[dz, x, size_z - 16 :].astype(F32) for dz in range(1, 3)]
        hid_edge[0, x] = jnp.where(tile_row == 0, below, jnp.where(tile_row == 1, low, begin[0])).astype(BF16)
        hid_edge[1, x] = jnp.where(tile_row == 0, low, begin[1]).astype(BF16)
        hid_edge[2, x] = jnp.where(tile_row == 15, high, end[0]).astype(BF16)
        hid_edge[3, x] = jnp.where(tile_row == 15, above, jnp.where(tile_row == 14, high, end[1])).astype(BF16)
    for x in range(n_field):
        xs_edge[0, x] = edge_tile(wide_field_ref, 0, x, below_rows[n_field + x : n_field + x + 1])
        xs_edge[1, x] = edge_tile(wide_field_ref, 2, x, above_rows[x : x + 1])


def backward(back_ref, slope_ref, slope_rows, back_rows, out_ref):
    size_x, size_z = slope_ref.shape[:2]
    half = slope_rows.shape[0] // 2
    index = lax.broadcasted_iota(jnp.int32, (size_z, 256), 0)
    for x in range(size_x):
        back, slope = back_ref[x], slope_ref[x]
        for row, at in ((0, 0), (size_z - 1, half)):
            back = jnp.where(index == row, back + back_rows[at + x : at + x + 1], back)
            slope = jnp.where(index == row, slope_rows[at + x + 1 : at + x + 2], slope)
        value = (back * slope).astype(BF16)
        rows = jnp.concatenate([value[:, :128].T, value[:, 128:].T], axis=0)
        out_ref[:, x * size_z : (x + 1) * size_z] = rows[C : 5 * C, :]


def collect(left, ref, size_x, skip, offset):
    tiles = [jnp.zeros((C, 128), F32) for _ in range(7)]
    lanes = lax.broadcasted_iota(jnp.int32, (C, 128), 1)
    for dx in range(3):
        for dz in range(3):
            block = jnp.dot(left, stack(ref, dz, dx + skip, size_x), preferred_element_type=F32)
            total = None
            for y in range(4):
                part = block[y * C : (y + 1) * C, :]
                shift = (256 - (y + offset) * C) % 256
                part = pltpu.roll(part, shift, 1) if shift else part
                total = part if total is None else total + part
            total = total[:, :128]
            for dy in range(3):
                tap = 9 * dx + 3 * dy + dz
                shift = ((tap - dy) * C) % 128
                moved = pltpu.roll(total, shift, 1) if shift else total
                at = (tap % 4) * C
                tiles[tap // 4] = jnp.where((lanes >= at) & (lanes < at + C), moved, tiles[tap // 4])
    return jnp.concatenate(tiles, axis=1)


def weight_grad(give, xs_ref, xs_edge, hid_ref, hid_edge, pre_grad_ref, rows_ref, out_ref):
    size_x = rows_ref.shape[0]
    even = even_index("gz")

    @pl.when(even if give else jnp.logical_not(even))
    def _():
        noise_rows = jnp.concatenate([rows_ref[x] for x in range(size_x)], axis=1)
        out_ref[...] = collect(noise_rows, Edged(hid_ref, hid_edge, HIDDEN_TILES), size_x, 0, 0)

    @pl.when(jnp.logical_not(even) if give else even)
    def _():
        out_ref[...] = collect(pre_grad_ref[...], Edged(xs_ref, xs_edge), size_x, 1, 1)


def predict(hid_ref, hid_edge, second_ref, out_ref, acc_ref, a2_ref):
    size_x, size_z = out_ref.shape[0], out_ref.shape[2]
    for t in range(9):
        for yi in range(8):
            band(a2_ref, t * 256 + yi * C, second_ref[t], (yi - 2) * C, 0, 4 * C)
    total = jnp.dot(taps(Edged(hid_ref, hid_edge, HIDDEN_TILES), size_x), a2_ref[...], preferred_element_type=F32)
    acc_ref[...] = total.reshape(size_x, size_z, 128)
    for x in range(size_x):
        out_ref[x] = acc_ref[x].astype(BF16).T


def finish(norm, mine_ref, other_ref, first_ref, second_ref):
    even = even_index("gz")
    mine = mine_ref[...]
    other = other_ref[...]
    first = jnp.where(even, mine, other) * norm
    second = jnp.where(even, other, mine) * norm
    first_ref[...] = (first * first)[:, : 27 * C]
    second_ref[...] = (second * second)[:, : 27 * C]


def first_sum(keep_ref, taken_ref, send_ref):
    send_ref[...] = (keep_ref[...] + taken_ref[...]).astype(send_ref.dtype)


def round_sum(own_ref, *refs):
    got, out_ref = refs[:-1], refs[-1]
    total = own_ref[...].astype(F32) + got[0][...].astype(F32)
    if len(got) == 3:
        total = total + (got[1][...].astype(F32) + got[2][...].astype(F32))
    out_ref[...] = total.astype(out_ref.dtype)


def flip(x, axis, bit):
    size = lax.axis_size(axis)
    return lax.ppermute(x, axis, [(i, i ^ bit) for i in range(size)])


def masked_swap(x, flip_even, flip_odd):
    target = {}
    for place in all_places():
        to = list(place)
        for axis, bit in flip_odd if place[2] % 2 else flip_even:
            to[AXES.index(axis)] ^= bit
        target[place] = tuple(to)
    return permute(x, target)


def local(inputs, noise, w_first, w_second):
    _, channels, size_x, size_y, size_z = inputs.shape
    cells = size_x * size_y * size_z
    devices = lax.axis_size("gx") * lax.axis_size("gy") * lax.axis_size("gz")
    norm = 1.0 / math.sqrt(cells * devices)
    lanes = size_y * channels

    plane = (size_z, lanes)
    y_sides = 2 if lax.axis_size("gy") > 2 else 1
    y_planes = size_x // 2 + size_x // 4
    face = struct((3,) + plane, BF16)
    y_face = struct((y_planes,) + plane, BF16)
    n_near = 2 + y_sides
    noise_rows, field, wide_noise, *faces = call(
        functools.partial(pack_faces, y_sides),
        [struct((size_x, lanes, size_z), BF16)]
        + [struct((size_x,) + plane, BF16)] * 2
        + [face] * 2
        + [y_face] * y_sides,
    )(jnp.concatenate([inputs, noise], axis=0))
    corners = call(functools.partial(pack_corners, y_sides), [struct((160, 128), BF16)] * (2 * y_sides))(*faces)
    faces = [*faces, *corners]
    moves = [[("gx", side)] for side in range(2)]
    moves += [[("gy", side)] for side in range(y_sides)]
    moves += [[("gx", side), ("gy", k)] for k in range(y_sides) for side in range(2)]
    got = [swap(face, move) for face, move in zip(faces, moves)]

    a1, ab, second = call(
        spread_weights,
        [struct((9 * 256, 256), BF16), struct((9 * 256, 256), BF16), struct((9, C, 128), F32)],
        moved=4_000_000,
    )(jnp.concatenate([w_first, w_second], axis=0))
    *near, a1, ab, second = lax.optimization_barrier((*got[:n_near], a1, ab, second))
    got = [*call(functools.partial(sort_faces, y_sides), [face] * 2 + [y_face] * 2)(*near), *got[n_near:]]

    n_field, n_noise = size_x + 4, size_x + 2
    z_rows = -(-(2 * n_field + n_noise) // 16) * 16
    low, high, face_a, face_b = call(
        functools.partial(pack_z, y_sides), [struct((z_rows, 256), BF16)] * 4
    )(field, wide_noise, *got)
    z_got = [swap(face, [("gz", side)]) for side, face in enumerate((face_a, face_b))]
    pre_shape = (n_noise, size_z, 256)
    slope_shape = (size_x, size_z, 256)
    xs, pre, back, hidden, slope = call(
        functools.partial(widen, y_sides),
        [
            struct((3, n_field, size_z, 256), BF16),
            struct(pre_shape, F32),
            struct(slope_shape, F32),
            struct((3,) + pre_shape, BF16),
            struct(slope_shape, F32),
        ],
        scratch=[pltpu.VMEM((3,) + pre_shape, BF16)],
        flops=1_000_000_000,
    )(field, wide_noise, *got, a1, ab)
    *z_got, xs, pre, back, hidden, slope = lax.optimization_barrier((*z_got[::-1], xs, pre, back, hidden, slope))
    z_got = z_got[::-1]

    hidden_edge, xs_edge, slope_rows, back_rows = call(
        mend,
        [
            struct((4, n_noise, 16, 256), BF16),
            struct((2, n_field, 16, 256), BF16),
            struct((2 * n_field, 256), F32),
            struct((2 * n_field, 256), F32),
        ],
    )(pre, hidden, xs, low, high, a1, ab, *z_got)
    pre_grad = call(backward, struct((lanes, size_x * size_z), BF16))(back, slope, slope_rows, back_rows)

    half = struct((C, 896), F32)
    rounded = struct((C, 896), BF16)
    parts = (xs, xs_edge, hidden, hidden_edge, pre_grad, noise_rows)
    give = call(functools.partial(weight_grad, True), half, flops=1_000_000_000)(*parts)
    taken = flip(give, "gz", 1)
    keep = call(functools.partial(weight_grad, False), half, flops=1_000_000_000)(*parts)

    prediction_rows = call(
        predict,
        struct((size_x, lanes, size_z), BF16),
        scratch=[pltpu.VMEM((size_x, size_z, lanes), F32), pltpu.VMEM((9 * 256, 128), BF16)],
        flops=500_000_000,
    )(hidden, hidden_edge, second)
    prediction = prediction_rows.reshape(size_x, size_y, channels, size_z).transpose(2, 0, 1, 3)[None]

    steps = []
    for axis, start in (("gx", 1), ("gz", 2), ("gy", 1)):
        bit = start
        while bit < lax.axis_size(axis):
            steps.append((axis, bit))
            bit *= 2
    rounds = [steps[k : k + 2] for k in range(0, len(steps), 2)]
    turn = len(rounds) // 2 if len(steps) % 2 == 0 else 0
    carried = [half] * (len(rounds) - 2) + [rounded] * min(len(rounds), 2) + [half]
    send = call(first_sum, carried[0])(keep, taken)
    for k, even in enumerate(rounds):
        odd = rounds[(k + turn) % len(rounds)]
        flips = [(even[:1], odd[:1])]
        if len(even) == 2:
            flips += [(even[1:], odd[1:]), (even, odd)]
        got = [masked_swap(send, *pair) for pair in flips]
        if k == 0:
            *got, prediction = lax.optimization_barrier((*got, prediction))
        send = call(round_sum, carried[k + 1])(send, *got)
    mine = send
    other = flip(mine, "gz", 1)
    fisher_first, fisher_second = call(
        functools.partial(finish, norm), [struct((C, 27 * C), F32)] * 2
    )(mine, other)
    return prediction, fisher_first, fisher_second


def solution(mesh):
    in_specs = (P(None, None, "gx", "gy", "gz"), P(None, None, "gx", "gy", "gz"), P(), P())
    out_specs = (P(None, None, "gx", "gy", "gz"), P(), P())
    return jax.shard_map(local, mesh=mesh, in_specs=in_specs, out_specs=out_specs, check_vma=False)
```

```python
import functools
import math

import jax
import jax.numpy as jnp
from jax import lax
from jax.experimental import pallas as pl
from jax.experimental.pallas import tpu as pltpu
from jax.sharding import PartitionSpec as P

F32 = jnp.float32
BF16 = jnp.bfloat16
C = 32


def call(body, out_shapes, scratch=(), flops=1_000_000, moved=1_000_000):
    return pl.pallas_call(
        body,
        out_shape=out_shapes,
        scratch_shapes=list(scratch),
        compiler_params=pltpu.CompilerParams(vmem_limit_bytes=24 * 1024 * 1024),
        cost_estimate=pl.CostEstimate(flops=flops, bytes_accessed=moved, transcendentals=0),
    )


def struct(shape, dtype):
    return jax.ShapeDtypeStruct(shape, dtype)


def even_index(axis):
    return lax.rem(lax.axis_index(axis), 2) == 0


def partner(index, side, size):
    other = index ^ 1 if side == 0 else ((index + 1) ^ 1) - 1
    return other if 0 <= other < size else None


AXES = ("gx", "gy", "gz")


def all_places():
    sizes = [lax.axis_size(axis) for axis in AXES]
    return [(i, j, k) for i in range(sizes[0]) for j in range(sizes[1]) for k in range(sizes[2])]


def permute(x, target):
    sizes = [lax.axis_size(axis) for axis in AXES]
    number = lambda place: (place[0] * sizes[1] + place[1]) * sizes[2] + place[2]
    return lax.ppermute(x, AXES, [(number(place), number(to)) for place, to in target.items()])


def swap(x, moves):
    sizes = [lax.axis_size(axis) for axis in AXES]
    side = dict(moves)
    places = all_places()
    target = {}
    for place in places:
        to = [partner(i, side[axis], size) if axis in side else i for i, axis, size in zip(place, AXES, sizes)]
        if None not in to:
            target[place] = tuple(to)
    if not target:
        return None
    alone = [place for place in places if place not in target]
    fills = (
        lambda i, j, k: (i, j, k ^ 1),
        lambda i, j, k: (i, j ^ 1, k),
        lambda i, j, k: (i ^ 1, j, k),
        lambda i, j, k: (i, j, k),
    )
    for fill in fills:
        if all(fill(*place) in alone for place in alone):
            target.update({place: fill(*place) for place in alone})
            break
    return permute(x, target)


def choose(flag, a, b):
    if a is None and b is None:
        return None
    a = jnp.zeros_like(b) if a is None else a
    b = jnp.zeros_like(a) if b is None else b
    return jnp.where(flag, a, b)


def pack_faces(y_sides, raw_ref, noise_rows_ref, field_ref, wide_noise_ref, *faces):
    size_x, size_z = raw_ref.shape[2], raw_ref.shape[4]
    lanes = raw_ref.shape[1] * raw_ref.shape[3]
    for x in range(size_x):
        for a, ref in enumerate((field_ref, wide_noise_ref)):
            rows = jnp.transpose(raw_ref[a, :, x].astype(F32), (1, 0, 2)).reshape(lanes, size_z).astype(BF16)
            if a:
                noise_rows_ref[x] = rows
            ref[x] = rows.T
    face_x, face_y = faces[:2], faces[2:]
    even = even_index("gx")
    for side in range(2):
        high = even if side == 0 else jnp.logical_not(even)
        face_x[side][0] = jnp.where(high, field_ref[size_x - 2], field_ref[0])
        face_x[side][1] = jnp.where(high, field_ref[size_x - 1], field_ref[1])
        face_x[side][2] = jnp.where(high, wide_noise_ref[size_x - 1], wide_noise_ref[0])
    even = even_index("gy")
    for k in range(y_sides):
        two, one = cut_y(even if k == 0 else jnp.logical_not(even))
        for j in range(0, size_x, 2):
            face_y[k][j // 2] = jnp.concatenate([two(field_ref[j]), two(field_ref[j + 1])], axis=1)
        for j in range(0, size_x, 4):
            face_y[k][size_x // 2 + j // 4] = jnp.concatenate([one(wide_noise_ref[j + i]) for i in range(4)], axis=1)


def cut_y(high):
    two = lambda p: jnp.where(high, p[:, p.shape[1] - 2 * C :], p[:, : 2 * C])
    one = lambda p: jnp.where(high, p[:, p.shape[1] - C :], p[:, :C])
    return two, one


def pack_corners(y_sides, face_0, face_1, *refs):
    corners = refs[y_sides:]
    even = even_index("gy")
    for k in range(y_sides):
        two, one = cut_y(even if k == 0 else jnp.logical_not(even))
        for side, face in enumerate((face_0, face_1)):
            ref = corners[2 * k + side]
            ref[:128] = jnp.concatenate([two(face[0]), two(face[1])], axis=1)
            strip = one(face[2])
            ref[128:] = jnp.concatenate([strip[i * 32 : (i + 1) * 32] for i in range(4)], axis=1)


def sort_faces(y_sides, *refs):
    x_refs, y_refs, out = refs[:2], list(refs[2 : 2 + y_sides]), refs[2 + y_sides :]
    y_refs += [None] * (2 - y_sides)
    for axis, pair, below_ref, above_ref in (("gx", x_refs, *out[:2]), ("gy", y_refs, *out[2:])):
        even = even_index(axis)
        index = lax.axis_index(axis)
        side_0, side_1 = [None if ref is None else ref[...] for ref in pair]
        below, above = choose(even, side_1, side_0), choose(even, side_0, side_1)
        below_ref[...] = jnp.where(index == 0, jnp.zeros_like(below), below)
        above_ref[...] = jnp.where(index == lax.axis_size(axis) - 1, jnp.zeros_like(above), above)


class Pieces:
    def __init__(self, y_sides, field, noise, face_x, face_y, corner):
        self.field, self.noise = field, noise
        self.size_x, self.size_z = field.shape[0], field.shape[1]
        even_x, even_y = even_index("gx"), even_index("gy")
        self.flag_x = {"below": even_x, "above": jnp.logical_not(even_x)}
        self.flag_y = {"below": even_y, "above": jnp.logical_not(even_y)}
        ends = lambda axis: (lax.axis_index(axis) == 0, lax.axis_index(axis) == lax.axis_size(axis) - 1)
        self.outside_x = dict(zip(("below", "above"), ends("gx")))
        self.outside_y = dict(zip(("below", "above"), ends("gy")))
        self.face_x = dict(zip(("below", "above"), face_x))
        self.face_y = dict(zip(("below", "above"), face_y))
        self.corner = [list(corner[2 * k : 2 * k + 2]) for k in range(y_sides)] + [[None, None]] * (2 - y_sides)

    def from_x(self, where, index, rows):
        return self.face_x[where][index, rows]

    def from_y(self, where, read):
        return read(self.face_y[where])

    def from_corner(self, where_x, where_y, read):
        a = []
        for pair in self.corner:
            if pair[0] is None:
                a.append(None)
            else:
                a.append(choose(self.flag_x[where_x], read(pair[1]), read(pair[0])))
        value = choose(self.flag_y[where_y], a[1], a[0])
        outside = self.outside_x[where_x] | self.outside_y[where_y]
        return jnp.where(outside, jnp.zeros_like(value), value)

    def side_of(self, x, width):
        if x < width:
            return "below", x
        if x >= self.size_x + width:
            return "above", x - self.size_x - width
        return "own", x - width

    def field_plane(self, x, z0, z1):
        rows = slice(z0, z1)
        where, i = self.side_of(x, 2)
        if where == "own":
            middle = self.field[i, rows]
            read = lambda ref: ref[i // 2, rows, (i % 2) * 2 * C : (i % 2 + 1) * 2 * C]
            low, high = self.from_y("below", read), self.from_y("above", read)
        else:
            middle = self.from_x(where, i, rows)
            read = lambda ref: ref[rows, i * 2 * C : (i + 1) * 2 * C]
            low, high = self.from_corner(where, "below", read), self.from_corner(where, "above", read)
        return jnp.concatenate([low, middle, high], axis=1)

    def noise_plane(self, x, z0, z1):
        rows = slice(z0, z1)
        where, i = self.side_of(x, 1)
        if where == "own":
            middle = self.noise[i, rows]
            read = lambda ref: ref[self.size_x // 2 + i // 4, rows, (i % 4) * C : (i % 4 + 1) * C]
            low, high = self.from_y("below", read), self.from_y("above", read)
        else:
            middle = self.from_x(where, 2, rows)

            def read(ref):
                parts = []
                for b in range(4):
                    first, last = max(z0, b * 32), min(z1, (b + 1) * 32)
                    if first < last:
                        parts.append(ref[128 + first - b * 32 : 128 + last - b * 32, b * C : (b + 1) * C])
                return jnp.concatenate(parts, axis=0) if len(parts) > 1 else parts[0]

            low, high = self.from_corner(where, "below", read), self.from_corner(where, "above", read)
        return jnp.concatenate([low, middle, high, jnp.zeros((z1 - z0, 2 * C), BF16)], axis=1)


def take_pieces(y_sides, refs):
    n = 6 + 2 * y_sides
    return Pieces(y_sides, refs[0], refs[1], refs[2:4], refs[4:6], refs[6:n]), refs[n:]


def pack_z(y_sides, *refs):
    pieces, (low_out, high_out, face_a, face_b) = take_pieces(y_sides, refs)
    n_field, n_noise, size_z = pieces.size_x + 4, pieces.size_x + 2, pieces.size_z

    def gather(tile, first, noise_row):
        planes = [pieces.field_plane(x, tile, tile + 16).astype(F32) for x in range(n_field)]
        rows = [plane[first + k - tile : first + k - tile + 1] for k in range(2) for plane in planes]
        for x in range(n_noise):
            rows.append(pieces.noise_plane(x, tile, tile + 16).astype(F32)[noise_row - tile : noise_row - tile + 1])
        while len(rows) % 16:
            rows.append(jnp.zeros_like(rows[0]))
        return jnp.concatenate(rows, axis=0).astype(BF16)

    low = gather(0, 0, 0)
    high = gather(size_z - 16, size_z - 2, size_z - 1)
    low_out[...] = low
    high_out[...] = high
    even = even_index("gz")
    face_a[...] = jnp.where(even, high, low)
    face_b[...] = jnp.where(even, low, high)


def stack(ref, dz, first, count):
    if isinstance(ref, Edged):
        return ref.stack(dz, first, count)
    return ref[dz, first : first + count].reshape(count * ref.shape[2], 256)


def taps(ref, count):
    return jnp.concatenate([stack(ref, dz, dx, count) for dx in range(3) for dz in range(3)], axis=1)


def widen(y_sides, *refs):
    pieces, (a1_ref, ab_ref, xs_ref, pre_ref, back_ref, hid_ref, slope_ref, ns_ref) = take_pieces(y_sides, refs)
    size_z = pieces.size_z
    for ref, read in ((xs_ref, pieces.field_plane), (ns_ref, pieces.noise_plane)):
        for x in range(ref.shape[1]):
            plane = read(x, 0, size_z)
            ref[1, x] = plane
            ref[0, x] = shifted(plane, 0.0, True)
            ref[2, x] = shifted(plane, 0.0, False)
    n_noise = pre_ref.shape[0]
    total = jnp.dot(taps(xs_ref, n_noise), a1_ref[...], preferred_element_type=F32)
    pre_ref[...] = total.reshape(n_noise, size_z, 256)
    size_x = back_ref.shape[0]
    total = jnp.dot(taps(ns_ref, size_x), ab_ref[...], preferred_element_type=F32)
    back_ref[...] = total.reshape(size_x, size_z, 256)

    index = lax.axis_index("gx")
    for x in range(n_noise):
        value = pre_ref[x]
        hidden, s = silu_parts(value)
        gone = outside_y()
        if x == 0:
            gone = gone | (index == 0)
        if x == n_noise - 1:
            gone = gone | (index == lax.axis_size("gx") - 1)
        hidden = jnp.where(gone, 0.0, hidden).astype(BF16)
        hid_ref[1, x] = hidden
        hid_ref[0, x] = shifted(hidden, 0.0, True)
        hid_ref[2, x] = shifted(hidden, 0.0, False)
        if 1 <= x <= size_x:
            slope_ref[x - 1] = slope_of(value, s)


def band(ref, row, taps, shift, lo, hi):
    moved = pltpu.roll(taps, shift % 128, 1) if shift % 128 else taps
    lane = lax.broadcasted_iota(jnp.int32, moved.shape, 1)
    for half in range(ref.shape[1] // 128):
        first = max(shift, lo) - 128 * half
        last = min(shift + 3 * C, hi) - 128 * half
        if last <= 0 or first >= 128:
            value = jnp.zeros_like(moved)
        else:
            value = jnp.where((lane >= first) & (lane < last), moved, 0.0)
        ref[row : row + C, half * 128 : (half + 1) * 128] = value.astype(BF16)


def spread_weights(both_ref, a1_ref, ab_ref, second_out):
    def columns(rows):
        wide = both_ref[rows].astype(F32)
        return jnp.concatenate([wide, jnp.zeros((C, 896 - wide.shape[1]), F32)], axis=1)

    def transposed(wide):
        return jnp.concatenate([wide[:, t * 128 : (t + 1) * 128].T for t in range(7)], axis=0)

    first = transposed(columns(slice(0, C)))
    second_rows = columns(slice(C, 2 * C))
    second = transposed(second_rows)
    fill = jnp.zeros((C, C), F32)
    for dx in range(3):
        for dz in range(3):
            t = 3 * dx + dz
            picks = [9 * dx + 3 * dy + dz for dy in range(3)]
            one = jnp.concatenate([first[k * C : (k + 1) * C, :] for k in picks[::-1]] + [fill], axis=1)
            two = jnp.concatenate([second[k * C : (k + 1) * C, :] for k in picks[::-1]] + [fill], axis=1)
            second_out[t] = two
            picks = [9 * (2 - dx) + 3 * dy + 2 - dz for dy in range(3)]
            back = jnp.concatenate([second_rows[:, k * C : (k + 1) * C] for k in picks] + [fill], axis=1)
            for yi in range(8):
                band(a1_ref, t * 256 + yi * C, one, (yi - 2) * C, 0, 6 * C)
            for yi in range(8):
                if yi < 6:
                    band(ab_ref, t * 256 + yi * C, back, (yi - 1) * C, C, 5 * C)
                else:
                    ab_ref[t * 256 + yi * C : t * 256 + (yi + 1) * C, :] = jnp.zeros((C, 256), BF16)


def shifted(plane, row, down):
    wide = plane.astype(F32)
    rows = wide.shape[0]
    index = lax.broadcasted_iota(jnp.int32, wide.shape, 0)
    if down:
        moved, place = pltpu.roll(wide, 1, 0), 0
    else:
        moved, place = pltpu.roll(wide, rows - 1, 0), rows - 1
    return jnp.where(index == place, row, moved).astype(BF16)


def silu_parts(value):
    s = 0.5 + 0.5 * jnp.tanh(0.5 * value)
    return value * s, s


def edge_tile(ref, dz, x, row):
    rows = ref.shape[2]
    at = slice(rows - 16, rows) if dz else slice(0, 16)
    tile = ref[dz, x, at, :].astype(F32)
    index = lax.broadcasted_iota(jnp.int32, tile.shape, 0)
    return jnp.where(index == (15 if dz else 0), row, tile).astype(BF16)


class Edged:
    def __init__(self, ref, edge_ref, tiles=((0, None), (None, None), (None, 1))):
        self.ref, self.edge_ref, self.tiles = ref, edge_ref, tiles

    def stack(self, dz, first, count):
        parts = []
        begin, end = self.tiles[dz]
        size_z = self.ref.shape[2]
        for x in range(first, first + count):
            if begin is not None:
                parts.append(self.edge_ref[begin, x])
            parts.append(self.ref[dz, x, 0 if begin is None else 16 : size_z if end is None else size_z - 16])
            if end is not None:
                parts.append(self.edge_ref[end, x])
        return jnp.concatenate(parts, axis=0)


HIDDEN_TILES = ((0, None), (1, 2), (None, 3))


def outside_y():
    lane = lax.broadcasted_iota(jnp.int32, (1, 256), 1)
    index = lax.axis_index("gy")
    return ((lane < C) & (index == 0)) | ((lane >= 5 * C) & (index == lax.axis_size("gy") - 1))


def slope_of(value, s):
    return s * (1.0 + value * (1.0 - s))


def mend(
    pre_ref, hid_ref, wide_field_ref, low_ref, high_ref, a1_ref, ab_ref, side_0, side_1, hid_edge, xs_edge, slope_rows, back_rows
):
    n_field, size_z = wide_field_ref.shape[1], wide_field_ref.shape[2]
    n_noise = pre_ref.shape[0]
    even = even_index("gz")
    own_low = low_ref[...].astype(F32)
    own_high = high_ref[...].astype(F32)

    gx, gz = lax.axis_index("gx"), lax.axis_index("gz")
    first_x, last_x = gx == 0, gx == lax.axis_size("gx") - 1
    first_z, last_z = gz == 0, gz == lax.axis_size("gz") - 1
    below_rows = jnp.where(first_z, 0.0, jnp.where(even, side_1[...], side_0[...]).astype(F32))
    above_rows = jnp.where(last_z, 0.0, jnp.where(even, side_0[...], side_1[...]).astype(F32))

    before = jnp.concatenate([below_rows[:n_field], own_high[n_field : 2 * n_field]], axis=0).astype(BF16)
    halo = jnp.concatenate([below_rows[n_field : 2 * n_field], above_rows[:n_field]], axis=0).astype(BF16)
    after = jnp.concatenate([own_low[:n_field], above_rows[n_field : 2 * n_field]], axis=0).astype(BF16)
    base = 2 * n_field
    noise_halo = jnp.concatenate(
        [below_rows[base : base + n_field], above_rows[base : base + n_field]], axis=0
    ).astype(BF16)
    rows = 2 * n_field
    edge_total, row_total, back_total = None, None, None
    for dx in range(3):
        at = lambda ref, dz: ref[(3 * dx + dz) * 256 : (3 * dx + dz + 1) * 256]
        first = jnp.dot(jnp.concatenate([before, halo], axis=0), at(a1_ref, 0), preferred_element_type=F32)
        middle = jnp.dot(halo, at(a1_ref, 1), preferred_element_type=F32)
        last = jnp.dot(jnp.concatenate([after, halo], axis=0), at(a1_ref, 2), preferred_element_type=F32)
        back_first = jnp.dot(noise_halo, at(ab_ref, 0), preferred_element_type=F32)
        back_last = jnp.dot(noise_halo, at(ab_ref, 2), preferred_element_type=F32)
        edge = first[:rows] + middle + last[:rows]
        row = jnp.concatenate([first[rows : rows + n_field], last[rows + n_field :]], axis=0)
        back = jnp.concatenate([back_first[:n_field], back_last[n_field:]], axis=0)
        if dx:
            edge, row, back = [pltpu.roll(part, rows - dx, 0) for part in (edge, row, back)]
        edge_total = edge if edge_total is None else edge_total + edge
        row_total = row if row_total is None else row_total + row
        back_total = back if back_total is None else back_total + back
    back_rows[...] = back_total

    index = lax.broadcasted_iota(jnp.int32, (rows, 256), 0)
    x_row = jnp.where(index < n_field, index, index - n_field)
    drop = outside_y() | ((x_row == 0) & first_x) | ((x_row == n_noise - 1) & last_x)
    drop_edge = drop | ((index < n_field) & first_z) | ((index >= n_field) & last_z)
    edge_hidden = jnp.where(drop_edge, 0.0, silu_parts(edge_total)[0]).astype(BF16).astype(F32)

    zeros = [jnp.zeros((1, 256), F32)] * (n_field - n_noise)
    ends = [pre_ref[x, 0:8][0:1] for x in range(n_noise)] + zeros
    ends += [pre_ref[x, size_z - 8 :][7:8] for x in range(n_noise)] + zeros
    value = jnp.concatenate(ends, axis=0) + row_total
    row_hidden, s = silu_parts(value)
    row_hidden = jnp.where(drop, 0.0, row_hidden).astype(BF16).astype(F32)
    slope_rows[...] = slope_of(value, s)

    tile_row = lax.broadcasted_iota(jnp.int32, (16, 256), 0)
    for x in range(n_noise):
        low, high = row_hidden[x : x + 1], row_hidden[n_field + x : n_field + x + 1]
        below, above = edge_hidden[x : x + 1], edge_hidden[n_field + x : n_field + x + 1]
        begin = [hid_ref[dz, x, 0:16].astype(F32) for dz in range(2)]
        end = [hid_ref[dz, x, size_z - 16 :].astype(F32) for dz in range(1, 3)]
        hid_edge[0, x] = jnp.where(tile_row == 0, below, jnp.where(tile_row == 1, low, begin[0])).astype(BF16)
        hid_edge[1, x] = jnp.where(tile_row == 0, low, begin[1]).astype(BF16)
        hid_edge[2, x] = jnp.where(tile_row == 15, high, end[0]).astype(BF16)
        hid_edge[3, x] = jnp.where(tile_row == 15, above, jnp.where(tile_row == 14, high, end[1])).astype(BF16)
    for x in range(n_field):
        xs_edge[0, x] = edge_tile(wide_field_ref, 0, x, below_rows[n_field + x : n_field + x + 1])
        xs_edge[1, x] = edge_tile(wide_field_ref, 2, x, above_rows[x : x + 1])


def backward(back_ref, slope_ref, slope_rows, back_rows, out_ref):
    size_x, size_z = slope_ref.shape[:2]
    half = slope_rows.shape[0] // 2
    index = lax.broadcasted_iota(jnp.int32, (size_z, 256), 0)
    for x in range(size_x):
        back, slope = back_ref[x], slope_ref[x]
        for row, at in ((0, 0), (size_z - 1, half)):
            back = jnp.where(index == row, back + back_rows[at + x : at + x + 1], back)
            slope = jnp.where(index == row, slope_rows[at + x + 1 : at + x + 2], slope)
        value = (back * slope).astype(BF16)
        rows = jnp.concatenate([value[:, :128].T, value[:, 128:].T], axis=0)
        out_ref[:, x * size_z : (x + 1) * size_z] = rows[C : 5 * C, :]


def collect(left, ref, size_x, skip, offset):
    tiles = [jnp.zeros((C, 128), F32) for _ in range(7)]
    lanes = lax.broadcasted_iota(jnp.int32, (C, 128), 1)
    for dx in range(3):
        for dz in range(3):
            block = jnp.dot(left, stack(ref, dz, dx + skip, size_x), preferred_element_type=F32)
            total = None
            for y in range(4):
                part = block[y * C : (y + 1) * C, :]
                shift = (256 - (y + offset) * C) % 256
                part = pltpu.roll(part, shift, 1) if shift else part
                total = part if total is None else total + part
            total = total[:, :128]
            for dy in range(3):
                tap = 9 * dx + 3 * dy + dz
                shift = ((tap - dy) * C) % 128
                moved = pltpu.roll(total, shift, 1) if shift else total
                at = (tap % 4) * C
                tiles[tap // 4] = jnp.where((lanes >= at) & (lanes < at + C), moved, tiles[tap // 4])
    return jnp.concatenate(tiles, axis=1)


def weight_grad(give, xs_ref, xs_edge, hid_ref, hid_edge, pre_grad_ref, rows_ref, out_ref):
    size_x = rows_ref.shape[0]
    even = even_index("gz")

    @pl.when(even if give else jnp.logical_not(even))
    def _():
        noise_rows = jnp.concatenate([rows_ref[x] for x in range(size_x)], axis=1)
        out_ref[...] = collect(noise_rows, Edged(hid_ref, hid_edge, HIDDEN_TILES), size_x, 0, 0)

    @pl.when(jnp.logical_not(even) if give else even)
    def _():
        out_ref[...] = collect(pre_grad_ref[...], Edged(xs_ref, xs_edge), size_x, 1, 1)


def predict(hid_ref, hid_edge, second_ref, out_ref, acc_ref, a2_ref):
    size_x, size_z = out_ref.shape[0], out_ref.shape[2]
    for t in range(9):
        for yi in range(8):
            band(a2_ref, t * 256 + yi * C, second_ref[t], (yi - 2) * C, 0, 4 * C)
    total = jnp.dot(taps(Edged(hid_ref, hid_edge, HIDDEN_TILES), size_x), a2_ref[...], preferred_element_type=F32)
    acc_ref[...] = total.reshape(size_x, size_z, 128)
    for x in range(size_x):
        out_ref[x] = acc_ref[x].astype(BF16).T


def finish(norm, mine_ref, other_ref, first_ref, second_ref):
    even = even_index("gz")
    mine = mine_ref[...]
    other = other_ref[...]
    first = jnp.where(even, mine, other) * norm
    second = jnp.where(even, other, mine) * norm
    first_ref[...] = (first * first)[:, : 27 * C]
    second_ref[...] = (second * second)[:, : 27 * C]


def first_sum(keep_ref, taken_ref, send_ref):
    send_ref[...] = (keep_ref[...] + taken_ref[...]).astype(send_ref.dtype)


def round_sum(own_ref, *refs):
    got, out_ref = refs[:-1], refs[-1]
    total = own_ref[...].astype(F32) + got[0][...].astype(F32)
    if len(got) == 3:
        total = total + (got[1][...].astype(F32) + got[2][...].astype(F32))
    out_ref[...] = total.astype(out_ref.dtype)


def flip(x, axis, bit):
    size = lax.axis_size(axis)
    return lax.ppermute(x, axis, [(i, i ^ bit) for i in range(size)])


def masked_swap(x, flip_even, flip_odd):
    target = {}
    for place in all_places():
        to = list(place)
        for axis, bit in flip_odd if place[2] % 2 else flip_even:
            to[AXES.index(axis)] ^= bit
        target[place] = tuple(to)
    return permute(x, target)


def local(inputs, noise, w_first, w_second):
    _, channels, size_x, size_y, size_z = inputs.shape
    cells = size_x * size_y * size_z
    devices = lax.axis_size("gx") * lax.axis_size("gy") * lax.axis_size("gz")
    norm = 1.0 / math.sqrt(cells * devices)
    lanes = size_y * channels

    plane = (size_z, lanes)
    y_sides = 2 if lax.axis_size("gy") > 2 else 1
    y_planes = size_x // 2 + size_x // 4
    face = struct((3,) + plane, BF16)
    y_face = struct((y_planes,) + plane, BF16)
    n_near = 2 + y_sides
    noise_rows, field, wide_noise, *faces = call(
        functools.partial(pack_faces, y_sides),
        [struct((size_x, lanes, size_z), BF16)]
        + [struct((size_x,) + plane, BF16)] * 2
        + [face] * 2
        + [y_face] * y_sides,
    )(jnp.concatenate([inputs, noise], axis=0))
    corners = call(functools.partial(pack_corners, y_sides), [struct((160, 128), BF16)] * (2 * y_sides))(*faces)
    faces = [*faces, *corners]
    moves = [[("gx", side)] for side in range(2)]
    moves += [[("gy", side)] for side in range(y_sides)]
    moves += [[("gx", side), ("gy", k)] for k in range(y_sides) for side in range(2)]
    got = [swap(face, move) for face, move in zip(faces, moves)]

    a1, ab, second = call(
        spread_weights,
        [struct((9 * 256, 256), BF16), struct((9 * 256, 256), BF16), struct((9, C, 128), F32)],
        moved=4_000_000,
    )(jnp.concatenate([w_first, w_second], axis=0))
    *near, a1, ab, second = lax.optimization_barrier((*got[:n_near], a1, ab, second))
    got = [*call(functools.partial(sort_faces, y_sides), [face] * 2 + [y_face] * 2)(*near), *got[n_near:]]

    n_field, n_noise = size_x + 4, size_x + 2
    z_rows = -(-(2 * n_field + n_noise) // 16) * 16
    low, high, face_a, face_b = call(
        functools.partial(pack_z, y_sides), [struct((z_rows, 256), BF16)] * 4
    )(field, wide_noise, *got)
    z_got = [swap(face, [("gz", side)]) for side, face in enumerate((face_a, face_b))]
    pre_shape = (n_noise, size_z, 256)
    slope_shape = (size_x, size_z, 256)
    xs, pre, back, hidden, slope = call(
        functools.partial(widen, y_sides),
        [
            struct((3, n_field, size_z, 256), BF16),
            struct(pre_shape, F32),
            struct(slope_shape, F32),
            struct((3,) + pre_shape, BF16),
            struct(slope_shape, F32),
        ],
        scratch=[pltpu.VMEM((3,) + pre_shape, BF16)],
        flops=1_000_000_000,
    )(field, wide_noise, *got, a1, ab)
    *z_got, xs, pre, back, hidden, slope = lax.optimization_barrier((*z_got[::-1], xs, pre, back, hidden, slope))
    z_got = z_got[::-1]

    hidden_edge, xs_edge, slope_rows, back_rows = call(
        mend,
        [
            struct((4, n_noise, 16, 256), BF16),
            struct((2, n_field, 16, 256), BF16),
            struct((2 * n_field, 256), F32),
            struct((2 * n_field, 256), F32),
        ],
    )(pre, hidden, xs, low, high, a1, ab, *z_got)
    pre_grad = call(backward, struct((lanes, size_x * size_z), BF16))(back, slope, slope_rows, back_rows)

    half = struct((C, 896), F32)
    rounded = struct((C, 896), BF16)
    parts = (xs, xs_edge, hidden, hidden_edge, pre_grad, noise_rows)
    give = call(functools.partial(weight_grad, True), half, flops=1_000_000_000)(*parts)
    taken = flip(give, "gz", 1)
    keep = call(functools.partial(weight_grad, False), half, flops=1_000_000_000)(*parts)

    prediction_rows = call(
        predict,
        struct((size_x, lanes, size_z), BF16),
        scratch=[pltpu.VMEM((size_x, size_z, lanes), F32), pltpu.VMEM((9 * 256, 128), BF16)],
        flops=500_000_000,
    )(hidden, hidden_edge, second)
    prediction = prediction_rows.reshape(size_x, size_y, channels, size_z).transpose(2, 0, 1, 3)[None]

    steps = []
    for axis, start in (("gx", 1), ("gz", 2), ("gy", 1)):
        bit = start
        while bit < lax.axis_size(axis):
            steps.append((axis, bit))
            bit *= 2
    rounds = [steps[k : k + 2] for k in range(0, len(steps), 2)]
    turn = len(rounds) // 2 if len(steps) % 2 == 0 else 0
    carried = [half] * (len(rounds) - 2) + [rounded] * min(len(rounds), 2) + [half]
    send = call(first_sum, carried[0])(keep, taken)
    for k, even in enumerate(rounds):
        odd = rounds[(k + turn) % len(rounds)]
        flips = [(even[:1], odd[:1])]
        if len(even) == 2:
            flips += [(even[1:], odd[1:]), (even, odd)]
        got = [masked_swap(send, *pair) for pair in flips]
        if k == 0:
            *got, prediction = lax.optimization_barrier((*got, prediction))
        send = call(round_sum, carried[k + 1])(send, *got)
    mine = send
    other = flip(mine, "gz", 1)
    fisher_first, fisher_second = call(
        functools.partial(finish, norm), [struct((C, 27 * C), F32)] * 2
    )(mine, other)
    return prediction, fisher_first, fisher_second


def solution(mesh):
    in_specs = (P(None, None, "gx", "gy", "gz"), P(None, None, "gx", "gy", "gz"), P(), P())
    out_specs = (P(None, None, "gx", "gy", "gz"), P(), P())
    return jax.shard_map(local, mesh=mesh, in_specs=in_specs, out_specs=out_specs, check_vma=False)
```

```python
import functools
import math

import jax
import jax.numpy as jnp
from jax import lax
from jax.experimental import pallas as pl
from jax.experimental.pallas import tpu as pltpu
from jax.sharding import PartitionSpec as P

F32 = jnp.float32
BF16 = jnp.bfloat16
C = 32


def call(body, out_shapes, scratch=(), flops=1_000_000, moved=1_000_000):
    return pl.pallas_call(
        body,
        out_shape=out_shapes,
        scratch_shapes=list(scratch),
        compiler_params=pltpu.CompilerParams(vmem_limit_bytes=24 * 1024 * 1024),
        cost_estimate=pl.CostEstimate(flops=flops, bytes_accessed=moved, transcendentals=0),
    )


def struct(shape, dtype):
    return jax.ShapeDtypeStruct(shape, dtype)


def even_index(axis):
    return lax.rem(lax.axis_index(axis), 2) == 0


def partner(index, side, size):
    other = index ^ 1 if side == 0 else ((index + 1) ^ 1) - 1
    return other if 0 <= other < size else None


AXES = ("gx", "gy", "gz")


def all_places():
    sizes = [lax.axis_size(axis) for axis in AXES]
    return [(i, j, k) for i in range(sizes[0]) for j in range(sizes[1]) for k in range(sizes[2])]


def permute(x, target):
    sizes = [lax.axis_size(axis) for axis in AXES]
    number = lambda place: (place[0] * sizes[1] + place[1]) * sizes[2] + place[2]
    return lax.ppermute(x, AXES, [(number(place), number(to)) for place, to in target.items()])


def swap(x, moves):
    sizes = [lax.axis_size(axis) for axis in AXES]
    side = dict(moves)
    places = all_places()
    target = {}
    for place in places:
        to = [partner(i, side[axis], size) if axis in side else i for i, axis, size in zip(place, AXES, sizes)]
        if None not in to:
            target[place] = tuple(to)
    if not target:
        return None
    alone = [place for place in places if place not in target]
    fills = (
        lambda i, j, k: (i, j, k ^ 1),
        lambda i, j, k: (i, j ^ 1, k),
        lambda i, j, k: (i ^ 1, j, k),
        lambda i, j, k: (i, j, k),
    )
    for fill in fills:
        if all(fill(*place) in alone for place in alone):
            target.update({place: fill(*place) for place in alone})
            break
    return permute(x, target)


def choose(flag, a, b):
    if a is None and b is None:
        return None
    a = jnp.zeros_like(b) if a is None else a
    b = jnp.zeros_like(a) if b is None else b
    return jnp.where(flag, a, b)


def pack_faces(y_sides, raw_ref, noise_rows_ref, field_ref, wide_noise_ref, *faces):
    size_x, size_z = raw_ref.shape[2], raw_ref.shape[4]
    lanes = raw_ref.shape[1] * raw_ref.shape[3]
    for x in range(size_x):
        for a, ref in enumerate((field_ref, wide_noise_ref)):
            rows = jnp.transpose(raw_ref[a, :, x].astype(F32), (1, 0, 2)).reshape(lanes, size_z).astype(BF16)
            if a:
                noise_rows_ref[x] = rows
            ref[x] = rows.T
    face_x, face_y = faces[:2], faces[2:]
    even = even_index("gx")
    for side in range(2):
        high = even if side == 0 else jnp.logical_not(even)
        face_x[side][0] = jnp.where(high, field_ref[size_x - 2], field_ref[0])
        face_x[side][1] = jnp.where(high, field_ref[size_x - 1], field_ref[1])
        face_x[side][2] = jnp.where(high, wide_noise_ref[size_x - 1], wide_noise_ref[0])
    even = even_index("gy")
    for k in range(y_sides):
        two, one = cut_y(even if k == 0 else jnp.logical_not(even))
        for j in range(0, size_x, 2):
            face_y[k][j // 2] = jnp.concatenate([two(field_ref[j]), two(field_ref[j + 1])], axis=1)
        for j in range(0, size_x, 4):
            face_y[k][size_x // 2 + j // 4] = jnp.concatenate([one(wide_noise_ref[j + i]) for i in range(4)], axis=1)


def cut_y(high):
    two = lambda p: jnp.where(high, p[:, p.shape[1] - 2 * C :], p[:, : 2 * C])
    one = lambda p: jnp.where(high, p[:, p.shape[1] - C :], p[:, :C])
    return two, one


def pack_corners(y_sides, face_0, face_1, *refs):
    corners = refs[y_sides:]
    even = even_index("gy")
    for k in range(y_sides):
        two, one = cut_y(even if k == 0 else jnp.logical_not(even))
        for side, face in enumerate((face_0, face_1)):
            ref = corners[2 * k + side]
            ref[:128] = jnp.concatenate([two(face[0]), two(face[1])], axis=1)
            strip = one(face[2])
            ref[128:] = jnp.concatenate([strip[i * 32 : (i + 1) * 32] for i in range(4)], axis=1)


def sort_faces(y_sides, *refs):
    x_refs, y_refs, out = refs[:2], list(refs[2 : 2 + y_sides]), refs[2 + y_sides :]
    y_refs += [None] * (2 - y_sides)
    for axis, pair, below_ref, above_ref in (("gx", x_refs, *out[:2]), ("gy", y_refs, *out[2:])):
        even = even_index(axis)
        index = lax.axis_index(axis)
        side_0, side_1 = [None if ref is None else ref[...] for ref in pair]
        below, above = choose(even, side_1, side_0), choose(even, side_0, side_1)
        below_ref[...] = jnp.where(index == 0, jnp.zeros_like(below), below)
        above_ref[...] = jnp.where(index == lax.axis_size(axis) - 1, jnp.zeros_like(above), above)


class Pieces:
    def __init__(self, y_sides, field, noise, face_x, face_y, corner):
        self.field, self.noise = field, noise
        self.size_x, self.size_z = field.shape[0], field.shape[1]
        even_x, even_y = even_index("gx"), even_index("gy")
        self.flag_x = {"below": even_x, "above": jnp.logical_not(even_x)}
        self.flag_y = {"below": even_y, "above": jnp.logical_not(even_y)}
        ends = lambda axis: (lax.axis_index(axis) == 0, lax.axis_index(axis) == lax.axis_size(axis) - 1)
        self.outside_x = dict(zip(("below", "above"), ends("gx")))
        self.outside_y = dict(zip(("below", "above"), ends("gy")))
        self.face_x = dict(zip(("below", "above"), face_x))
        self.face_y = dict(zip(("below", "above"), face_y))
        self.corner = [list(corner[2 * k : 2 * k + 2]) for k in range(y_sides)] + [[None, None]] * (2 - y_sides)

    def from_x(self, where, index, rows):
        return self.face_x[where][index, rows]

    def from_y(self, where, read):
        return read(self.face_y[where])

    def from_corner(self, where_x, where_y, read):
        a = []
        for pair in self.corner:
            if pair[0] is None:
                a.append(None)
            else:
                a.append(choose(self.flag_x[where_x], read(pair[1]), read(pair[0])))
        value = choose(self.flag_y[where_y], a[1], a[0])
        outside = self.outside_x[where_x] | self.outside_y[where_y]
        return jnp.where(outside, jnp.zeros_like(value), value)

    def side_of(self, x, width):
        if x < width:
            return "below", x
        if x >= self.size_x + width:
            return "above", x - self.size_x - width
        return "own", x - width

    def field_plane(self, x, z0, z1):
        rows = slice(z0, z1)
        where, i = self.side_of(x, 2)
        if where == "own":
            middle = self.field[i, rows]
            read = lambda ref: ref[i // 2, rows, (i % 2) * 2 * C : (i % 2 + 1) * 2 * C]
            low, high = self.from_y("below", read), self.from_y("above", read)
        else:
            middle = self.from_x(where, i, rows)
            read = lambda ref: ref[rows, i * 2 * C : (i + 1) * 2 * C]
            low, high = self.from_corner(where, "below", read), self.from_corner(where, "above", read)
        return jnp.concatenate([low, middle, high], axis=1)

    def noise_plane(self, x, z0, z1):
        rows = slice(z0, z1)
        where, i = self.side_of(x, 1)
        if where == "own":
            middle = self.noise[i, rows]
            read = lambda ref: ref[self.size_x // 2 + i // 4, rows, (i % 4) * C : (i % 4 + 1) * C]
            low, high = self.from_y("below", read), self.from_y("above", read)
        else:
            middle = self.from_x(where, 2, rows)

            def read(ref):
                parts = []
                for b in range(4):
                    first, last = max(z0, b * 32), min(z1, (b + 1) * 32)
                    if first < last:
                        parts.append(ref[128 + first - b * 32 : 128 + last - b * 32, b * C : (b + 1) * C])
                return jnp.concatenate(parts, axis=0) if len(parts) > 1 else parts[0]

            low, high = self.from_corner(where, "below", read), self.from_corner(where, "above", read)
        return jnp.concatenate([low, middle, high, jnp.zeros((z1 - z0, 2 * C), BF16)], axis=1)


def take_pieces(y_sides, refs):
    n = 6 + 2 * y_sides
    return Pieces(y_sides, refs[0], refs[1], refs[2:4], refs[4:6], refs[6:n]), refs[n:]


def pack_z(y_sides, *refs):
    pieces, (low_out, high_out, face_a, face_b) = take_pieces(y_sides, refs)
    n_field, n_noise, size_z = pieces.size_x + 4, pieces.size_x + 2, pieces.size_z

    def gather(tile, first, noise_row):
        planes = [pieces.field_plane(x, tile, tile + 16).astype(F32) for x in range(n_field)]
        rows = [plane[first + k - tile : first + k - tile + 1] for k in range(2) for plane in planes]
        for x in range(n_noise):
            rows.append(pieces.noise_plane(x, tile, tile + 16).astype(F32)[noise_row - tile : noise_row - tile + 1])
        while len(rows) % 16:
            rows.append(jnp.zeros_like(rows[0]))
        return jnp.concatenate(rows, axis=0).astype(BF16)

    low = gather(0, 0, 0)
    high = gather(size_z - 16, size_z - 2, size_z - 1)
    low_out[...] = low
    high_out[...] = high
    even = even_index("gz")
    face_a[...] = jnp.where(even, high, low)
    face_b[...] = jnp.where(even, low, high)


def stack(ref, dz, first, count):
    if isinstance(ref, Edged):
        return ref.stack(dz, first, count)
    return ref[dz, first : first + count].reshape(count * ref.shape[2], 256)


def taps(ref, count):
    return jnp.concatenate([stack(ref, dz, dx, count) for dx in range(3) for dz in range(3)], axis=1)


def widen(y_sides, *refs):
    pieces, (a1_ref, ab_ref, xs_ref, pre_ref, back_ref, hid_ref, slope_ref, ns_ref) = take_pieces(y_sides, refs)
    size_z = pieces.size_z
    for ref, read in ((xs_ref, pieces.field_plane), (ns_ref, pieces.noise_plane)):
        for x in range(ref.shape[1]):
            plane = read(x, 0, size_z)
            ref[1, x] = plane
            ref[0, x] = shifted(plane, 0.0, True)
            ref[2, x] = shifted(plane, 0.0, False)
    n_noise = pre_ref.shape[0]
    total = jnp.dot(taps(xs_ref, n_noise), a1_ref[...], preferred_element_type=F32)
    pre_ref[...] = total.reshape(n_noise, size_z, 256)
    size_x = back_ref.shape[0]
    total = jnp.dot(taps(ns_ref, size_x), ab_ref[...], preferred_element_type=F32)
    back_ref[...] = total.reshape(size_x, size_z, 256)

    index = lax.axis_index("gx")
    for x in range(n_noise):
        value = pre_ref[x]
        hidden, s = silu_parts(value)
        gone = outside_y()
        if x == 0:
            gone = gone | (index == 0)
        if x == n_noise - 1:
            gone = gone | (index == lax.axis_size("gx") - 1)
        hidden = jnp.where(gone, 0.0, hidden).astype(BF16)
        hid_ref[1, x] = hidden
        hid_ref[0, x] = shifted(hidden, 0.0, True)
        hid_ref[2, x] = shifted(hidden, 0.0, False)
        if 1 <= x <= size_x:
            slope_ref[x - 1] = slope_of(value, s)


def band(ref, row, taps, shift, lo, hi):
    moved = pltpu.roll(taps, shift % 128, 1) if shift % 128 else taps
    lane = lax.broadcasted_iota(jnp.int32, moved.shape, 1)
    for half in range(ref.shape[1] // 128):
        first = max(shift, lo) - 128 * half
        last = min(shift + 3 * C, hi) - 128 * half
        if last <= 0 or first >= 128:
            value = jnp.zeros_like(moved)
        else:
            value = jnp.where((lane >= first) & (lane < last), moved, 0.0)
        ref[row : row + C, half * 128 : (half + 1) * 128] = value.astype(BF16)


def spread_weights(both_ref, a1_ref, ab_ref, second_out):
    def columns(rows):
        wide = both_ref[rows].astype(F32)
        return jnp.concatenate([wide, jnp.zeros((C, 896 - wide.shape[1]), F32)], axis=1)

    def transposed(wide):
        return jnp.concatenate([wide[:, t * 128 : (t + 1) * 128].T for t in range(7)], axis=0)

    first = transposed(columns(slice(0, C)))
    second_rows = columns(slice(C, 2 * C))
    second = transposed(second_rows)
    fill = jnp.zeros((C, C), F32)
    for dx in range(3):
        for dz in range(3):
            t = 3 * dx + dz
            picks = [9 * dx + 3 * dy + dz for dy in range(3)]
            one = jnp.concatenate([first[k * C : (k + 1) * C, :] for k in picks[::-1]] + [fill], axis=1)
            two = jnp.concatenate([second[k * C : (k + 1) * C, :] for k in picks[::-1]] + [fill], axis=1)
            second_out[t] = two
            picks = [9 * (2 - dx) + 3 * dy + 2 - dz for dy in range(3)]
            back = jnp.concatenate([second_rows[:, k * C : (k + 1) * C] for k in picks] + [fill], axis=1)
            for yi in range(8):
                band(a1_ref, t * 256 + yi * C, one, (yi - 2) * C, 0, 6 * C)
            for yi in range(8):
                if yi < 6:
                    band(ab_ref, t * 256 + yi * C, back, (yi - 1) * C, C, 5 * C)
                else:
                    ab_ref[t * 256 + yi * C : t * 256 + (yi + 1) * C, :] = jnp.zeros((C, 256), BF16)


def shifted(plane, row, down):
    wide = plane.astype(F32)
    rows = wide.shape[0]
    index = lax.broadcasted_iota(jnp.int32, wide.shape, 0)
    if down:
        moved, place = pltpu.roll(wide, 1, 0), 0
    else:
        moved, place = pltpu.roll(wide, rows - 1, 0), rows - 1
    return jnp.where(index == place, row, moved).astype(BF16)


def silu_parts(value):
    s = 0.5 + 0.5 * jnp.tanh(0.5 * value)
    return value * s, s


def edge_tile(ref, dz, x, row):
    rows = ref.shape[2]
    at = slice(rows - 16, rows) if dz else slice(0, 16)
    tile = ref[dz, x, at, :].astype(F32)
    index = lax.broadcasted_iota(jnp.int32, tile.shape, 0)
    return jnp.where(index == (15 if dz else 0), row, tile).astype(BF16)


class Edged:
    def __init__(self, ref, edge_ref, tiles=((0, None), (None, None), (None, 1))):
        self.ref, self.edge_ref, self.tiles = ref, edge_ref, tiles

    def stack(self, dz, first, count):
        parts = []
        begin, end = self.tiles[dz]
        size_z = self.ref.shape[2]
        for x in range(first, first + count):
            if begin is not None:
                parts.append(self.edge_ref[begin, x])
            parts.append(self.ref[dz, x, 0 if begin is None else 16 : size_z if end is None else size_z - 16])
            if end is not None:
                parts.append(self.edge_ref[end, x])
        return jnp.concatenate(parts, axis=0)


HIDDEN_TILES = ((0, None), (1, 2), (None, 3))


def outside_y():
    lane = lax.broadcasted_iota(jnp.int32, (1, 256), 1)
    index = lax.axis_index("gy")
    return ((lane < C) & (index == 0)) | ((lane >= 5 * C) & (index == lax.axis_size("gy") - 1))


def slope_of(value, s):
    return s * (1.0 + value * (1.0 - s))


def mend(
    pre_ref, hid_ref, wide_field_ref, low_ref, high_ref, a1_ref, ab_ref, side_0, side_1, hid_edge, xs_edge, slope_rows, back_rows
):
    n_field, size_z = wide_field_ref.shape[1], wide_field_ref.shape[2]
    n_noise = pre_ref.shape[0]
    even = even_index("gz")
    own_low = low_ref[...].astype(F32)
    own_high = high_ref[...].astype(F32)

    gx, gz = lax.axis_index("gx"), lax.axis_index("gz")
    first_x, last_x = gx == 0, gx == lax.axis_size("gx") - 1
    first_z, last_z = gz == 0, gz == lax.axis_size("gz") - 1
    below_rows = jnp.where(first_z, 0.0, jnp.where(even, side_1[...], side_0[...]).astype(F32))
    above_rows = jnp.where(last_z, 0.0, jnp.where(even, side_0[...], side_1[...]).astype(F32))

    before = jnp.concatenate([below_rows[:n_field], own_high[n_field : 2 * n_field]], axis=0).astype(BF16)
    halo = jnp.concatenate([below_rows[n_field : 2 * n_field], above_rows[:n_field]], axis=0).astype(BF16)
    after = jnp.concatenate([own_low[:n_field], above_rows[n_field : 2 * n_field]], axis=0).astype(BF16)
    base = 2 * n_field
    noise_halo = jnp.concatenate(
        [below_rows[base : base + n_field], above_rows[base : base + n_field]], axis=0
    ).astype(BF16)
    rows = 2 * n_field
    edge_total, row_total, back_total = None, None, None
    for dx in range(3):
        at = lambda ref, dz: ref[(3 * dx + dz) * 256 : (3 * dx + dz + 1) * 256]
        first = jnp.dot(jnp.concatenate([before, halo], axis=0), at(a1_ref, 0), preferred_element_type=F32)
        middle = jnp.dot(halo, at(a1_ref, 1), preferred_element_type=F32)
        last = jnp.dot(jnp.concatenate([after, halo], axis=0), at(a1_ref, 2), preferred_element_type=F32)
        back_first = jnp.dot(noise_halo, at(ab_ref, 0), preferred_element_type=F32)
        back_last = jnp.dot(noise_halo, at(ab_ref, 2), preferred_element_type=F32)
        edge = first[:rows] + middle + last[:rows]
        row = jnp.concatenate([first[rows : rows + n_field], last[rows + n_field :]], axis=0)
        back = jnp.concatenate([back_first[:n_field], back_last[n_field:]], axis=0)
        if dx:
            edge, row, back = [pltpu.roll(part, rows - dx, 0) for part in (edge, row, back)]
        edge_total = edge if edge_total is None else edge_total + edge
        row_total = row if row_total is None else row_total + row
        back_total = back if back_total is None else back_total + back
    back_rows[...] = back_total

    index = lax.broadcasted_iota(jnp.int32, (rows, 256), 0)
    x_row = jnp.where(index < n_field, index, index - n_field)
    drop = outside_y() | ((x_row == 0) & first_x) | ((x_row == n_noise - 1) & last_x)
    drop_edge = drop | ((index < n_field) & first_z) | ((index >= n_field) & last_z)
    edge_hidden = jnp.where(drop_edge, 0.0, silu_parts(edge_total)[0]).astype(BF16).astype(F32)

    zeros = [jnp.zeros((1, 256), F32)] * (n_field - n_noise)
    ends = [pre_ref[x, 0:8][0:1] for x in range(n_noise)] + zeros
    ends += [pre_ref[x, size_z - 8 :][7:8] for x in range(n_noise)] + zeros
    value = jnp.concatenate(ends, axis=0) + row_total
    row_hidden, s = silu_parts(value)
    row_hidden = jnp.where(drop, 0.0, row_hidden).astype(BF16).astype(F32)
    slope_rows[...] = slope_of(value, s)

    tile_row = lax.broadcasted_iota(jnp.int32, (16, 256), 0)
    for x in range(n_noise):
        low, high = row_hidden[x : x + 1], row_hidden[n_field + x : n_field + x + 1]
        below, above = edge_hidden[x : x + 1], edge_hidden[n_field + x : n_field + x + 1]
        begin = [hid_ref[dz, x, 0:16].astype(F32) for dz in range(2)]
        end = [hid_ref[dz, x, size_z - 16 :].astype(F32) for dz in range(1, 3)]
        hid_edge[0, x] = jnp.where(tile_row == 0, below, jnp.where(tile_row == 1, low, begin[0])).astype(BF16)
        hid_edge[1, x] = jnp.where(tile_row == 0, low, begin[1]).astype(BF16)
        hid_edge[2, x] = jnp.where(tile_row == 15, high, end[0]).astype(BF16)
        hid_edge[3, x] = jnp.where(tile_row == 15, above, jnp.where(tile_row == 14, high, end[1])).astype(BF16)
    for x in range(n_field):
        xs_edge[0, x] = edge_tile(wide_field_ref, 0, x, below_rows[n_field + x : n_field + x + 1])
        xs_edge[1, x] = edge_tile(wide_field_ref, 2, x, above_rows[x : x + 1])


def backward(back_ref, slope_ref, slope_rows, back_rows, out_ref):
    size_x, size_z = slope_ref.shape[:2]
    half = slope_rows.shape[0] // 2
    index = lax.broadcasted_iota(jnp.int32, (size_z, 256), 0)
    for x in range(size_x):
        back, slope = back_ref[x], slope_ref[x]
        for row, at in ((0, 0), (size_z - 1, half)):
            back = jnp.where(index == row, back + back_rows[at + x : at + x + 1], back)
            slope = jnp.where(index == row, slope_rows[at + x + 1 : at + x + 2], slope)
        value = (back * slope).astype(BF16)
        rows = jnp.concatenate([value[:, :128].T, value[:, 128:].T], axis=0)
        out_ref[:, x * size_z : (x + 1) * size_z] = rows[C : 5 * C, :]


def collect(left, ref, size_x, skip, offset):
    tiles = [jnp.zeros((C, 128), F32) for _ in range(7)]
    lanes = lax.broadcasted_iota(jnp.int32, (C, 128), 1)
    for dx in range(3):
        for dz in range(3):
            block = jnp.dot(left, stack(ref, dz, dx + skip, size_x), preferred_element_type=F32)
            total = None
            for y in range(4):
                part = block[y * C : (y + 1) * C, :]
                shift = (256 - (y + offset) * C) % 256
                part = pltpu.roll(part, shift, 1) if shift else part
                total = part if total is None else total + part
            total = total[:, :128]
            for dy in range(3):
                tap = 9 * dx + 3 * dy + dz
                shift = ((tap - dy) * C) % 128
                moved = pltpu.roll(total, shift, 1) if shift else total
                at = (tap % 4) * C
                tiles[tap // 4] = jnp.where((lanes >= at) & (lanes < at + C), moved, tiles[tap // 4])
    return jnp.concatenate(tiles, axis=1)


def weight_grad(give, xs_ref, xs_edge, hid_ref, hid_edge, pre_grad_ref, rows_ref, out_ref):
    size_x = rows_ref.shape[0]
    even = even_index("gz")

    @pl.when(even if give else jnp.logical_not(even))
    def _():
        noise_rows = jnp.concatenate([rows_ref[x] for x in range(size_x)], axis=1)
        out_ref[...] = collect(noise_rows, Edged(hid_ref, hid_edge, HIDDEN_TILES), size_x, 0, 0)

    @pl.when(jnp.logical_not(even) if give else even)
    def _():
        out_ref[...] = collect(pre_grad_ref[...], Edged(xs_ref, xs_edge), size_x, 1, 1)


def predict(hid_ref, hid_edge, second_ref, out_ref, acc_ref, a2_ref):
    size_x, size_z = out_ref.shape[0], out_ref.shape[2]
    for t in range(9):
        for yi in range(8):
            band(a2_ref, t * 256 + yi * C, second_ref[t], (yi - 2) * C, 0, 4 * C)
    total = jnp.dot(taps(Edged(hid_ref, hid_edge, HIDDEN_TILES), size_x), a2_ref[...], preferred_element_type=F32)
    acc_ref[...] = total.reshape(size_x, size_z, 128)
    for x in range(size_x):
        out_ref[x] = acc_ref[x].astype(BF16).T


def finish(norm, mine_ref, other_ref, first_ref, second_ref):
    even = even_index("gz")
    mine = mine_ref[...]
    other = other_ref[...]
    first = jnp.where(even, mine, other) * norm
    second = jnp.where(even, other, mine) * norm
    first_ref[...] = (first * first)[:, : 27 * C]
    second_ref[...] = (second * second)[:, : 27 * C]


def first_sum(keep_ref, taken_ref, send_ref):
    send_ref[...] = (keep_ref[...] + taken_ref[...]).astype(send_ref.dtype)


def round_sum(own_ref, *refs):
    got, out_ref = refs[:-1], refs[-1]
    total = own_ref[...].astype(F32) + got[0][...].astype(F32)
    if len(got) == 3:
        total = total + (got[1][...].astype(F32) + got[2][...].astype(F32))
    out_ref[...] = total.astype(out_ref.dtype)


def flip(x, axis, bit):
    size = lax.axis_size(axis)
    return lax.ppermute(x, axis, [(i, i ^ bit) for i in range(size)])


def masked_swap(x, flip_even, flip_odd):
    target = {}
    for place in all_places():
        to = list(place)
        for axis, bit in flip_odd if place[2] % 2 else flip_even:
            to[AXES.index(axis)] ^= bit
        target[place] = tuple(to)
    return permute(x, target)


def local(inputs, noise, w_first, w_second):
    _, channels, size_x, size_y, size_z = inputs.shape
    cells = size_x * size_y * size_z
    devices = lax.axis_size("gx") * lax.axis_size("gy") * lax.axis_size("gz")
    norm = 1.0 / math.sqrt(cells * devices)
    lanes = size_y * channels

    plane = (size_z, lanes)
    y_sides = 2 if lax.axis_size("gy") > 2 else 1
    y_planes = size_x // 2 + size_x // 4
    face = struct((3,) + plane, BF16)
    y_face = struct((y_planes,) + plane, BF16)
    n_near = 2 + y_sides
    noise_rows, field, wide_noise, *faces = call(
        functools.partial(pack_faces, y_sides),
        [struct((size_x, lanes, size_z), BF16)]
        + [struct((size_x,) + plane, BF16)] * 2
        + [face] * 2
        + [y_face] * y_sides,
    )(jnp.concatenate([inputs, noise], axis=0))
    corners = call(functools.partial(pack_corners, y_sides), [struct((160, 128), BF16)] * (2 * y_sides))(*faces)
    faces = [*faces, *corners]
    moves = [[("gx", side)] for side in range(2)]
    moves += [[("gy", side)] for side in range(y_sides)]
    moves += [[("gx", side), ("gy", k)] for k in range(y_sides) for side in range(2)]
    got = [swap(face, move) for face, move in zip(faces, moves)]

    a1, ab, second = call(
        spread_weights,
        [struct((9 * 256, 256), BF16), struct((9 * 256, 256), BF16), struct((9, C, 128), F32)],
        moved=4_000_000,
    )(jnp.concatenate([w_first, w_second], axis=0))
    *near, a1, ab, second = lax.optimization_barrier((got[1], got[0], *got[2:n_near], a1, ab, second))
    near[:2] = near[1::-1]
    got = [*call(functools.partial(sort_faces, y_sides), [face] * 2 + [y_face] * 2)(*near), *got[n_near:]]

    n_field, n_noise = size_x + 4, size_x + 2
    z_rows = -(-(2 * n_field + n_noise) // 16) * 16
    low, high, face_a, face_b = call(
        functools.partial(pack_z, y_sides), [struct((z_rows, 256), BF16)] * 4
    )(field, wide_noise, *got)
    z_got = [swap(face, [("gz", side)]) for side, face in enumerate((face_a, face_b))]
    pre_shape = (n_noise, size_z, 256)
    slope_shape = (size_x, size_z, 256)
    xs, pre, back, hidden, slope = call(
        functools.partial(widen, y_sides),
        [
            struct((3, n_field, size_z, 256), BF16),
            struct(pre_shape, F32),
            struct(slope_shape, F32),
            struct((3,) + pre_shape, BF16),
            struct(slope_shape, F32),
        ],
        scratch=[pltpu.VMEM((3,) + pre_shape, BF16)],
        flops=1_000_000_000,
    )(field, wide_noise, *got, a1, ab)
    *z_got, xs, pre, back, hidden, slope = lax.optimization_barrier((*z_got[::-1], xs, pre, back, hidden, slope))
    z_got = z_got[::-1]

    hidden_edge, xs_edge, slope_rows, back_rows = call(
        mend,
        [
            struct((4, n_noise, 16, 256), BF16),
            struct((2, n_field, 16, 256), BF16),
            struct((2 * n_field, 256), F32),
            struct((2 * n_field, 256), F32),
        ],
    )(pre, hidden, xs, low, high, a1, ab, *z_got)
    pre_grad = call(backward, struct((lanes, size_x * size_z), BF16))(back, slope, slope_rows, back_rows)

    half = struct((C, 896), F32)
    rounded = struct((C, 896), BF16)
    parts = (xs, xs_edge, hidden, hidden_edge, pre_grad, noise_rows)
    give = call(functools.partial(weight_grad, True), half, flops=1_000_000_000)(*parts)
    taken = flip(give, "gz", 1)
    keep = call(functools.partial(weight_grad, False), half, flops=1_000_000_000)(*parts)

    prediction_rows = call(
        predict,
        struct((size_x, lanes, size_z), BF16),
        scratch=[pltpu.VMEM((size_x, size_z, lanes), F32), pltpu.VMEM((9 * 256, 128), BF16)],
        flops=500_000_000,
    )(hidden, hidden_edge, second)
    prediction = prediction_rows.reshape(size_x, size_y, channels, size_z).transpose(2, 0, 1, 3)[None]

    steps = []
    for axis, start in (("gx", 1), ("gz", 2), ("gy", 1)):
        bit = start
        while bit < lax.axis_size(axis):
            steps.append((axis, bit))
            bit *= 2
    rounds = [steps[k : k + 2] for k in range(0, len(steps), 2)]
    turn = len(rounds) // 2 if len(steps) % 2 == 0 else 0
    carried = [half] * (len(rounds) - 2) + [rounded] * min(len(rounds), 2) + [half]
    send = call(first_sum, carried[0])(keep, taken)
    for k, even in enumerate(rounds):
        odd = rounds[(k + turn) % len(rounds)]
        flips = [(even[:1], odd[:1])]
        if len(even) == 2:
            flips += [(even[1:], odd[1:]), (even, odd)]
        got = [masked_swap(send, *pair) for pair in flips]
        if k == 0:
            *got, prediction = lax.optimization_barrier((*got, prediction))
        send = call(round_sum, carried[k + 1])(send, *got)
    mine = send
    other = flip(mine, "gz", 1)
    fisher_first, fisher_second = call(
        functools.partial(finish, norm), [struct((C, 27 * C), F32)] * 2
    )(mine, other)
    return prediction, fisher_first, fisher_second


def solution(mesh):
    in_specs = (P(None, None, "gx", "gy", "gz"), P(None, None, "gx", "gy", "gz"), P(), P())
    out_specs = (P(None, None, "gx", "gy", "gz"), P(), P())
    return jax.shard_map(local, mesh=mesh, in_specs=in_specs, out_specs=out_specs, check_vma=False)
```

```python
import functools
import math

import jax
import jax.numpy as jnp
from jax import lax
from jax.experimental import pallas as pl
from jax.experimental.pallas import tpu as pltpu
from jax.sharding import PartitionSpec as P

F32 = jnp.float32
BF16 = jnp.bfloat16
C = 32


def call(body, out_shapes, scratch=(), flops=1_000_000, moved=1_000_000):
    return pl.pallas_call(
        body,
        out_shape=out_shapes,
        scratch_shapes=list(scratch),
        compiler_params=pltpu.CompilerParams(vmem_limit_bytes=24 * 1024 * 1024),
        cost_estimate=pl.CostEstimate(flops=flops, bytes_accessed=moved, transcendentals=0),
    )


def struct(shape, dtype):
    return jax.ShapeDtypeStruct(shape, dtype)


def even_index(axis):
    return lax.rem(lax.axis_index(axis), 2) == 0


def partner(index, side, size):
    other = index ^ 1 if side == 0 else ((index + 1) ^ 1) - 1
    return other if 0 <= other < size else None


AXES = ("gx", "gy", "gz")


def all_places():
    sizes = [lax.axis_size(axis) for axis in AXES]
    return [(i, j, k) for i in range(sizes[0]) for j in range(sizes[1]) for k in range(sizes[2])]


def permute(x, target):
    sizes = [lax.axis_size(axis) for axis in AXES]
    number = lambda place: (place[0] * sizes[1] + place[1]) * sizes[2] + place[2]
    return lax.ppermute(x, AXES, [(number(place), number(to)) for place, to in target.items()])


def swap(x, moves):
    sizes = [lax.axis_size(axis) for axis in AXES]
    side = dict(moves)
    places = all_places()
    target = {}
    for place in places:
        to = [partner(i, side[axis], size) if axis in side else i for i, axis, size in zip(place, AXES, sizes)]
        if None not in to:
            target[place] = tuple(to)
    if not target:
        return None
    alone = [place for place in places if place not in target]
    fills = (
        lambda i, j, k: (i, j, k ^ 1),
        lambda i, j, k: (i, j ^ 1, k),
        lambda i, j, k: (i ^ 1, j, k),
        lambda i, j, k: (i, j, k),
    )
    for fill in fills:
        if all(fill(*place) in alone for place in alone):
            target.update({place: fill(*place) for place in alone})
            break
    return permute(x, target)


def choose(flag, a, b):
    if a is None and b is None:
        return None
    a = jnp.zeros_like(b) if a is None else a
    b = jnp.zeros_like(a) if b is None else b
    return jnp.where(flag, a, b)


def pack_faces(y_sides, raw_ref, noise_rows_ref, field_ref, wide_noise_ref, *faces):
    size_x, size_z = raw_ref.shape[2], raw_ref.shape[4]
    lanes = raw_ref.shape[1] * raw_ref.shape[3]
    for x in range(size_x):
        for a, ref in enumerate((field_ref, wide_noise_ref)):
            rows = jnp.transpose(raw_ref[a, :, x], (1, 0, 2)).reshape(lanes, size_z)
            if a:
                noise_rows_ref[x] = rows
            ref[x] = rows.T
    face_x, face_y = faces[:2], faces[2:]
    even = even_index("gx")
    for side in range(2):
        high = even if side == 0 else jnp.logical_not(even)
        face_x[side][0] = jnp.where(high, field_ref[size_x - 2], field_ref[0])
        face_x[side][1] = jnp.where(high, field_ref[size_x - 1], field_ref[1])
        face_x[side][2] = jnp.where(high, wide_noise_ref[size_x - 1], wide_noise_ref[0])
    even = even_index("gy")
    for k in range(y_sides):
        two, one = cut_y(even if k == 0 else jnp.logical_not(even))
        for j in range(0, size_x, 2):
            face_y[k][j // 2] = jnp.concatenate([two(field_ref[j]), two(field_ref[j + 1])], axis=1)
        for j in range(0, size_x, 4):
            face_y[k][size_x // 2 + j // 4] = jnp.concatenate([one(wide_noise_ref[j + i]) for i in range(4)], axis=1)


def cut_y(high):
    two = lambda p: jnp.where(high, p[:, p.shape[1] - 2 * C :], p[:, : 2 * C])
    one = lambda p: jnp.where(high, p[:, p.shape[1] - C :], p[:, :C])
    return two, one


def pack_corners(y_sides, face_0, face_1, *refs):
    corners = refs[y_sides:]
    even = even_index("gy")
    for k in range(y_sides):
        two, one = cut_y(even if k == 0 else jnp.logical_not(even))
        for side, face in enumerate((face_0, face_1)):
            ref = corners[2 * k + side]
            ref[:128] = jnp.concatenate([two(face[0]), two(face[1])], axis=1)
            strip = one(face[2])
            ref[128:] = jnp.concatenate([strip[i * 32 : (i + 1) * 32] for i in range(4)], axis=1)


def sort_faces(y_sides, *refs):
    x_refs, y_refs, out = refs[:2], list(refs[2 : 2 + y_sides]), refs[2 + y_sides :]
    y_refs += [None] * (2 - y_sides)
    for axis, pair, below_ref, above_ref in (("gx", x_refs, *out[:2]), ("gy", y_refs, *out[2:])):
        even = even_index(axis)
        index = lax.axis_index(axis)
        side_0, side_1 = [None if ref is None else ref[...] for ref in pair]
        below, above = choose(even, side_1, side_0), choose(even, side_0, side_1)
        below_ref[...] = jnp.where(index == 0, jnp.zeros_like(below), below)
        above_ref[...] = jnp.where(index == lax.axis_size(axis) - 1, jnp.zeros_like(above), above)


class Pieces:
    def __init__(self, y_sides, field, noise, face_x, face_y, corner):
        self.field, self.noise = field, noise
        self.size_x, self.size_z = field.shape[0], field.shape[1]
        even_x, even_y = even_index("gx"), even_index("gy")
        self.flag_x = {"below": even_x, "above": jnp.logical_not(even_x)}
        self.flag_y = {"below": even_y, "above": jnp.logical_not(even_y)}
        ends = lambda axis: (lax.axis_index(axis) == 0, lax.axis_index(axis) == lax.axis_size(axis) - 1)
        self.outside_x = dict(zip(("below", "above"), ends("gx")))
        self.outside_y = dict(zip(("below", "above"), ends("gy")))
        self.face_x = dict(zip(("below", "above"), face_x))
        self.face_y = dict(zip(("below", "above"), face_y))
        self.corner = [list(corner[2 * k : 2 * k + 2]) for k in range(y_sides)] + [[None, None]] * (2 - y_sides)

    def from_x(self, where, index, rows):
        return self.face_x[where][index, rows]

    def from_y(self, where, read):
        return read(self.face_y[where])

    def from_corner(self, where_x, where_y, read):
        a = []
        for pair in self.corner:
            if pair[0] is None:
                a.append(None)
            else:
                a.append(choose(self.flag_x[where_x], read(pair[1]), read(pair[0])))
        value = choose(self.flag_y[where_y], a[1], a[0])
        outside = self.outside_x[where_x] | self.outside_y[where_y]
        return jnp.where(outside, jnp.zeros_like(value), value)

    def side_of(self, x, width):
        if x < width:
            return "below", x
        if x >= self.size_x + width:
            return "above", x - self.size_x - width
        return "own", x - width

    def field_plane(self, x, z0, z1):
        rows = slice(z0, z1)
        where, i = self.side_of(x, 2)
        if where == "own":
            middle = self.field[i, rows]
            read = lambda ref: ref[i // 2, rows, (i % 2) * 2 * C : (i % 2 + 1) * 2 * C]
            low, high = self.from_y("below", read), self.from_y("above", read)
        else:
            middle = self.from_x(where, i, rows)
            read = lambda ref: ref[rows, i * 2 * C : (i + 1) * 2 * C]
            low, high = self.from_corner(where, "below", read), self.from_corner(where, "above", read)
        return jnp.concatenate([low, middle, high], axis=1)

    def noise_plane(self, x, z0, z1):
        rows = slice(z0, z1)
        where, i = self.side_of(x, 1)
        if where == "own":
            middle = self.noise[i, rows]
            read = lambda ref: ref[self.size_x // 2 + i // 4, rows, (i % 4) * C : (i % 4 + 1) * C]
            low, high = self.from_y("below", read), self.from_y("above", read)
        else:
            middle = self.from_x(where, 2, rows)

            def read(ref):
                parts = []
                for b in range(4):
                    first, last = max(z0, b * 32), min(z1, (b + 1) * 32)
                    if first < last:
                        parts.append(ref[128 + first - b * 32 : 128 + last - b * 32, b * C : (b + 1) * C])
                return jnp.concatenate(parts, axis=0) if len(parts) > 1 else parts[0]

            low, high = self.from_corner(where, "below", read), self.from_corner(where, "above", read)
        return jnp.concatenate([low, middle, high, jnp.zeros((z1 - z0, 2 * C), BF16)], axis=1)


def take_pieces(y_sides, refs):
    n = 6 + 2 * y_sides
    return Pieces(y_sides, refs[0], refs[1], refs[2:4], refs[4:6], refs[6:n]), refs[n:]


def pack_z(y_sides, *refs):
    pieces, (low_out, high_out, face_a, face_b) = take_pieces(y_sides, refs)
    n_field, n_noise, size_z = pieces.size_x + 4, pieces.size_x + 2, pieces.size_z

    def gather(tile, first, noise_row):
        planes = [pieces.field_plane(x, tile, tile + 16).astype(F32) for x in range(n_field)]
        rows = [plane[first + k - tile : first + k - tile + 1] for k in range(2) for plane in planes]
        for x in range(n_noise):
            rows.append(pieces.noise_plane(x, tile, tile + 16).astype(F32)[noise_row - tile : noise_row - tile + 1])
        while len(rows) % 16:
            rows.append(jnp.zeros_like(rows[0]))
        return jnp.concatenate(rows, axis=0).astype(BF16)

    low = gather(0, 0, 0)
    high = gather(size_z - 16, size_z - 2, size_z - 1)
    low_out[...] = low
    high_out[...] = high
    even = even_index("gz")
    face_a[...] = jnp.where(even, high, low)
    face_b[...] = jnp.where(even, low, high)


def stack(ref, dz, first, count):
    if isinstance(ref, Edged):
        return ref.stack(dz, first, count)
    return ref[dz, first : first + count].reshape(count * ref.shape[2], 256)


def taps(ref, count):
    return jnp.concatenate([stack(ref, dz, dx, count) for dx in range(3) for dz in range(3)], axis=1)


def widen(y_sides, *refs):
    pieces, (a1_ref, ab_ref, xs_ref, pre_ref, back_ref, hid_ref, slope_ref, ns_ref) = take_pieces(y_sides, refs)
    size_z = pieces.size_z
    for ref, read in ((xs_ref, pieces.field_plane), (ns_ref, pieces.noise_plane)):
        for x in range(ref.shape[1]):
            plane = read(x, 0, size_z)
            ref[1, x] = plane
            ref[0, x] = shifted(plane, 0.0, True)
            ref[2, x] = shifted(plane, 0.0, False)
    n_noise = pre_ref.shape[0]
    total = jnp.dot(taps(xs_ref, n_noise), a1_ref[...], preferred_element_type=F32)
    pre_ref[...] = total.reshape(n_noise, size_z, 256)
    size_x = back_ref.shape[0]
    total = jnp.dot(taps(ns_ref, size_x), ab_ref[...], preferred_element_type=F32)
    back_ref[...] = total.reshape(size_x, size_z, 256)

    index = lax.axis_index("gx")
    for x in range(n_noise):
        value = pre_ref[x]
        hidden, s = silu_parts(value)
        gone = outside_y()
        if x == 0:
            gone = gone | (index == 0)
        if x == n_noise - 1:
            gone = gone | (index == lax.axis_size("gx") - 1)
        hidden = jnp.where(gone, 0.0, hidden).astype(BF16)
        hid_ref[1, x] = hidden
        hid_ref[0, x] = shifted(hidden, 0.0, True)
        hid_ref[2, x] = shifted(hidden, 0.0, False)
        if 1 <= x <= size_x:
            slope_ref[x - 1] = slope_of(value, s)


def band(ref, row, taps, shift, lo, hi):
    moved = pltpu.roll(taps, shift % 128, 1) if shift % 128 else taps
    lane = lax.broadcasted_iota(jnp.int32, moved.shape, 1)
    for half in range(ref.shape[1] // 128):
        first = max(shift, lo) - 128 * half
        last = min(shift + 3 * C, hi) - 128 * half
        if last <= 0 or first >= 128:
            value = jnp.zeros_like(moved)
        else:
            value = jnp.where((lane >= first) & (lane < last), moved, 0.0)
        ref[row : row + C, half * 128 : (half + 1) * 128] = value.astype(BF16)


def spread_weights(both_ref, a1_ref, ab_ref, second_out):
    def columns(rows):
        wide = both_ref[rows].astype(F32)
        return jnp.concatenate([wide, jnp.zeros((C, 896 - wide.shape[1]), F32)], axis=1)

    def transposed(wide):
        return jnp.concatenate([wide[:, t * 128 : (t + 1) * 128].T for t in range(7)], axis=0)

    first = transposed(columns(slice(0, C)))
    second_rows = columns(slice(C, 2 * C))
    second = transposed(second_rows)
    fill = jnp.zeros((C, C), F32)
    for dx in range(3):
        for dz in range(3):
            t = 3 * dx + dz
            picks = [9 * dx + 3 * dy + dz for dy in range(3)]
            one = jnp.concatenate([first[k * C : (k + 1) * C, :] for k in picks[::-1]] + [fill], axis=1)
            two = jnp.concatenate([second[k * C : (k + 1) * C, :] for k in picks[::-1]] + [fill], axis=1)
            second_out[t] = two
            picks = [9 * (2 - dx) + 3 * dy + 2 - dz for dy in range(3)]
            back = jnp.concatenate([second_rows[:, k * C : (k + 1) * C] for k in picks] + [fill], axis=1)
            for yi in range(8):
                band(a1_ref, t * 256 + yi * C, one, (yi - 2) * C, 0, 6 * C)
            for yi in range(8):
                if yi < 6:
                    band(ab_ref, t * 256 + yi * C, back, (yi - 1) * C, C, 5 * C)
                else:
                    ab_ref[t * 256 + yi * C : t * 256 + (yi + 1) * C, :] = jnp.zeros((C, 256), BF16)


def shifted(plane, row, down):
    wide = plane.astype(F32)
    rows = wide.shape[0]
    index = lax.broadcasted_iota(jnp.int32, wide.shape, 0)
    if down:
        moved, place = pltpu.roll(wide, 1, 0), 0
    else:
        moved, place = pltpu.roll(wide, rows - 1, 0), rows - 1
    return jnp.where(index == place, row, moved).astype(BF16)


def silu_parts(value):
    s = 0.5 + 0.5 * jnp.tanh(0.5 * value)
    return value * s, s


def edge_tile(ref, dz, x, row):
    rows = ref.shape[2]
    at = slice(rows - 16, rows) if dz else slice(0, 16)
    tile = ref[dz, x, at, :].astype(F32)
    index = lax.broadcasted_iota(jnp.int32, tile.shape, 0)
    return jnp.where(index == (15 if dz else 0), row, tile).astype(BF16)


class Edged:
    def __init__(self, ref, edge_ref, tiles=((0, None), (None, None), (None, 1))):
        self.ref, self.edge_ref, self.tiles = ref, edge_ref, tiles

    def stack(self, dz, first, count):
        parts = []
        begin, end = self.tiles[dz]
        size_z = self.ref.shape[2]
        for x in range(first, first + count):
            if begin is not None:
                parts.append(self.edge_ref[begin, x])
            parts.append(self.ref[dz, x, 0 if begin is None else 16 : size_z if end is None else size_z - 16])
            if end is not None:
                parts.append(self.edge_ref[end, x])
        return jnp.concatenate(parts, axis=0)


HIDDEN_TILES = ((0, None), (1, 2), (None, 3))


def outside_y():
    lane = lax.broadcasted_iota(jnp.int32, (1, 256), 1)
    index = lax.axis_index("gy")
    return ((lane < C) & (index == 0)) | ((lane >= 5 * C) & (index == lax.axis_size("gy") - 1))


def slope_of(value, s):
    return s * (1.0 + value * (1.0 - s))


def mend(
    pre_ref, hid_ref, wide_field_ref, low_ref, high_ref, a1_ref, ab_ref, side_0, side_1, hid_edge, xs_edge, slope_rows, back_rows
):
    n_field, size_z = wide_field_ref.shape[1], wide_field_ref.shape[2]
    n_noise = pre_ref.shape[0]
    even = even_index("gz")
    own_low = low_ref[...].astype(F32)
    own_high = high_ref[...].astype(F32)

    gx, gz = lax.axis_index("gx"), lax.axis_index("gz")
    first_x, last_x = gx == 0, gx == lax.axis_size("gx") - 1
    first_z, last_z = gz == 0, gz == lax.axis_size("gz") - 1
    below_rows = jnp.where(first_z, 0.0, jnp.where(even, side_1[...], side_0[...]).astype(F32))
    above_rows = jnp.where(last_z, 0.0, jnp.where(even, side_0[...], side_1[...]).astype(F32))

    before = jnp.concatenate([below_rows[:n_field], own_high[n_field : 2 * n_field]], axis=0).astype(BF16)
    halo = jnp.concatenate([below_rows[n_field : 2 * n_field], above_rows[:n_field]], axis=0).astype(BF16)
    after = jnp.concatenate([own_low[:n_field], above_rows[n_field : 2 * n_field]], axis=0).astype(BF16)
    base = 2 * n_field
    noise_halo = jnp.concatenate(
        [below_rows[base : base + n_field], above_rows[base : base + n_field]], axis=0
    ).astype(BF16)
    rows = 2 * n_field
    edge_total, row_total, back_total = None, None, None
    for dx in range(3):
        at = lambda ref, dz: ref[(3 * dx + dz) * 256 : (3 * dx + dz + 1) * 256]
        first = jnp.dot(jnp.concatenate([before, halo], axis=0), at(a1_ref, 0), preferred_element_type=F32)
        middle = jnp.dot(halo, at(a1_ref, 1), preferred_element_type=F32)
        last = jnp.dot(jnp.concatenate([after, halo], axis=0), at(a1_ref, 2), preferred_element_type=F32)
        back_first = jnp.dot(noise_halo, at(ab_ref, 0), preferred_element_type=F32)
        back_last = jnp.dot(noise_halo, at(ab_ref, 2), preferred_element_type=F32)
        edge = first[:rows] + middle + last[:rows]
        row = jnp.concatenate([first[rows : rows + n_field], last[rows + n_field :]], axis=0)
        back = jnp.concatenate([back_first[:n_field], back_last[n_field:]], axis=0)
        if dx:
            edge, row, back = [pltpu.roll(part, rows - dx, 0) for part in (edge, row, back)]
        edge_total = edge if edge_total is None else edge_total + edge
        row_total = row if row_total is None else row_total + row
        back_total = back if back_total is None else back_total + back
    back_rows[...] = back_total

    index = lax.broadcasted_iota(jnp.int32, (rows, 256), 0)
    x_row = jnp.where(index < n_field, index, index - n_field)
    drop = outside_y() | ((x_row == 0) & first_x) | ((x_row == n_noise - 1) & last_x)
    drop_edge = drop | ((index < n_field) & first_z) | ((index >= n_field) & last_z)
    edge_hidden = jnp.where(drop_edge, 0.0, silu_parts(edge_total)[0]).astype(BF16).astype(F32)

    zeros = [jnp.zeros((1, 256), F32)] * (n_field - n_noise)
    ends = [pre_ref[x, 0:8][0:1] for x in range(n_noise)] + zeros
    ends += [pre_ref[x, size_z - 8 :][7:8] for x in range(n_noise)] + zeros
    value = jnp.concatenate(ends, axis=0) + row_total
    row_hidden, s = silu_parts(value)
    row_hidden = jnp.where(drop, 0.0, row_hidden).astype(BF16).astype(F32)
    slope_rows[...] = slope_of(value, s)

    tile_row = lax.broadcasted_iota(jnp.int32, (16, 256), 0)
    for x in range(n_noise):
        low, high = row_hidden[x : x + 1], row_hidden[n_field + x : n_field + x + 1]
        below, above = edge_hidden[x : x + 1], edge_hidden[n_field + x : n_field + x + 1]
        begin = [hid_ref[dz, x, 0:16].astype(F32) for dz in range(2)]
        end = [hid_ref[dz, x, size_z - 16 :].astype(F32) for dz in range(1, 3)]
        hid_edge[0, x] = jnp.where(tile_row == 0, below, jnp.where(tile_row == 1, low, begin[0])).astype(BF16)
        hid_edge[1, x] = jnp.where(tile_row == 0, low, begin[1]).astype(BF16)
        hid_edge[2, x] = jnp.where(tile_row == 15, high, end[0]).astype(BF16)
        hid_edge[3, x] = jnp.where(tile_row == 15, above, jnp.where(tile_row == 14, high, end[1])).astype(BF16)
    for x in range(n_field):
        xs_edge[0, x] = edge_tile(wide_field_ref, 0, x, below_rows[n_field + x : n_field + x + 1])
        xs_edge[1, x] = edge_tile(wide_field_ref, 2, x, above_rows[x : x + 1])


def backward(back_ref, slope_ref, slope_rows, back_rows, out_ref):
    size_x, size_z = slope_ref.shape[:2]
    half = slope_rows.shape[0] // 2
    index = lax.broadcasted_iota(jnp.int32, (size_z, 256), 0)
    for x in range(size_x):
        back, slope = back_ref[x], slope_ref[x]
        for row, at in ((0, 0), (size_z - 1, half)):
            back = jnp.where(index == row, back + back_rows[at + x : at + x + 1], back)
            slope = jnp.where(index == row, slope_rows[at + x + 1 : at + x + 2], slope)
        value = (back * slope).astype(BF16)
        rows = jnp.concatenate([value[:, :128].T, value[:, 128:].T], axis=0)
        out_ref[:, x * size_z : (x + 1) * size_z] = rows[C : 5 * C, :]


def collect(left, ref, size_x, skip, offset):
    tiles = [jnp.zeros((C, 128), F32) for _ in range(7)]
    lanes = lax.broadcasted_iota(jnp.int32, (C, 128), 1)
    for dx in range(3):
        for dz in range(3):
            block = jnp.dot(left, stack(ref, dz, dx + skip, size_x), preferred_element_type=F32)
            total = None
            for y in range(4):
                part = block[y * C : (y + 1) * C, :]
                shift = (256 - (y + offset) * C) % 256
                part = pltpu.roll(part, shift, 1) if shift else part
                total = part if total is None else total + part
            total = total[:, :128]
            for dy in range(3):
                tap = 9 * dx + 3 * dy + dz
                shift = ((tap - dy) * C) % 128
                moved = pltpu.roll(total, shift, 1) if shift else total
                at = (tap % 4) * C
                tiles[tap // 4] = jnp.where((lanes >= at) & (lanes < at + C), moved, tiles[tap // 4])
    return jnp.concatenate(tiles, axis=1)


def weight_grad(give, xs_ref, xs_edge, hid_ref, hid_edge, pre_grad_ref, rows_ref, out_ref):
    size_x = rows_ref.shape[0]
    even = even_index("gz")

    @pl.when(even if give else jnp.logical_not(even))
    def _():
        noise_rows = jnp.concatenate([rows_ref[x] for x in range(size_x)], axis=1)
        out_ref[...] = collect(noise_rows, Edged(hid_ref, hid_edge, HIDDEN_TILES), size_x, 0, 0)

    @pl.when(jnp.logical_not(even) if give else even)
    def _():
        out_ref[...] = collect(pre_grad_ref[...], Edged(xs_ref, xs_edge), size_x, 1, 1)


def predict(hid_ref, hid_edge, second_ref, out_ref, acc_ref, a2_ref):
    size_x, size_z = out_ref.shape[0], out_ref.shape[2]
    for t in range(9):
        for yi in range(8):
            band(a2_ref, t * 256 + yi * C, second_ref[t], (yi - 2) * C, 0, 4 * C)
    total = jnp.dot(taps(Edged(hid_ref, hid_edge, HIDDEN_TILES), size_x), a2_ref[...], preferred_element_type=F32)
    acc_ref[...] = total.reshape(size_x, size_z, 128)
    for x in range(size_x):
        out_ref[x] = acc_ref[x].astype(BF16).T


def finish(norm, mine_ref, other_ref, first_ref, second_ref):
    even = even_index("gz")
    mine = mine_ref[...]
    other = other_ref[...]
    first = jnp.where(even, mine, other) * norm
    second = jnp.where(even, other, mine) * norm
    first_ref[...] = (first * first)[:, : 27 * C]
    second_ref[...] = (second * second)[:, : 27 * C]


def first_sum(keep_ref, taken_ref, send_ref):
    send_ref[...] = (keep_ref[...] + taken_ref[...]).astype(send_ref.dtype)


def round_sum(own_ref, *refs):
    got, out_ref = refs[:-1], refs[-1]
    total = own_ref[...].astype(F32) + got[0][...].astype(F32)
    if len(got) == 3:
        total = total + (got[1][...].astype(F32) + got[2][...].astype(F32))
    out_ref[...] = total.astype(out_ref.dtype)


def flip(x, axis, bit):
    size = lax.axis_size(axis)
    return lax.ppermute(x, axis, [(i, i ^ bit) for i in range(size)])


def masked_swap(x, flip_even, flip_odd):
    target = {}
    for place in all_places():
        to = list(place)
        for axis, bit in flip_odd if place[2] % 2 else flip_even:
            to[AXES.index(axis)] ^= bit
        target[place] = tuple(to)
    return permute(x, target)


def local(inputs, noise, w_first, w_second):
    _, channels, size_x, size_y, size_z = inputs.shape
    cells = size_x * size_y * size_z
    devices = lax.axis_size("gx") * lax.axis_size("gy") * lax.axis_size("gz")
    norm = 1.0 / math.sqrt(cells * devices)
    lanes = size_y * channels

    plane = (size_z, lanes)
    y_sides = 2 if lax.axis_size("gy") > 2 else 1
    y_planes = size_x // 2 + size_x // 4
    face = struct((3,) + plane, BF16)
    y_face = struct((y_planes,) + plane, BF16)
    n_near = 2 + y_sides
    noise_rows, field, wide_noise, *faces = call(
        functools.partial(pack_faces, y_sides),
        [struct((size_x, lanes, size_z), BF16)]
        + [struct((size_x,) + plane, BF16)] * 2
        + [face] * 2
        + [y_face] * y_sides,
    )(jnp.concatenate([inputs, noise], axis=0))
    corners = call(functools.partial(pack_corners, y_sides), [struct((160, 128), BF16)] * (2 * y_sides))(*faces)
    faces = [*faces, *corners]
    moves = [[("gx", side)] for side in range(2)]
    moves += [[("gy", side)] for side in range(y_sides)]
    moves += [[("gx", side), ("gy", k)] for k in range(y_sides) for side in range(2)]
    got = [swap(face, move) for face, move in zip(faces, moves)]

    a1, ab, second = call(
        spread_weights,
        [struct((9 * 256, 256), BF16), struct((9 * 256, 256), BF16), struct((9, C, 128), F32)],
        moved=4_000_000,
    )(jnp.concatenate([w_first, w_second], axis=0))
    *near, a1, ab, second = lax.optimization_barrier((*got[:n_near], a1, ab, second))
    got = [*call(functools.partial(sort_faces, y_sides), [face] * 2 + [y_face] * 2)(*near), *got[n_near:]]

    n_field, n_noise = size_x + 4, size_x + 2
    z_rows = -(-(2 * n_field + n_noise) // 16) * 16
    low, high, face_a, face_b = call(
        functools.partial(pack_z, y_sides), [struct((z_rows, 256), BF16)] * 4
    )(field, wide_noise, *got)
    z_got = [swap(face, [("gz", side)]) for side, face in enumerate((face_a, face_b))]
    pre_shape = (n_noise, size_z, 256)
    slope_shape = (size_x, size_z, 256)
    xs, pre, back, hidden, slope = call(
        functools.partial(widen, y_sides),
        [
            struct((3, n_field, size_z, 256), BF16),
            struct(pre_shape, F32),
            struct(slope_shape, F32),
            struct((3,) + pre_shape, BF16),
            struct(slope_shape, F32),
        ],
        scratch=[pltpu.VMEM((3,) + pre_shape, BF16)],
        flops=1_000_000_000,
    )(field, wide_noise, *got, a1, ab)
    *z_got, xs, pre, back, hidden, slope = lax.optimization_barrier((*z_got[::-1], xs, pre, back, hidden, slope))
    z_got = z_got[::-1]

    hidden_edge, xs_edge, slope_rows, back_rows = call(
        mend,
        [
            struct((4, n_noise, 16, 256), BF16),
            struct((2, n_field, 16, 256), BF16),
            struct((2 * n_field, 256), F32),
            struct((2 * n_field, 256), F32),
        ],
    )(pre, hidden, xs, low, high, a1, ab, *z_got)
    pre_grad = call(backward, struct((lanes, size_x * size_z), BF16))(back, slope, slope_rows, back_rows)

    half = struct((C, 896), F32)
    rounded = struct((C, 896), BF16)
    parts = (xs, xs_edge, hidden, hidden_edge, pre_grad, noise_rows)
    give = call(functools.partial(weight_grad, True), half, flops=1_000_000_000)(*parts)
    taken = flip(give, "gz", 1)
    keep = call(functools.partial(weight_grad, False), half, flops=1_000_000_000)(*parts)

    prediction_rows = call(
        predict,
        struct((size_x, lanes, size_z), BF16),
        scratch=[pltpu.VMEM((size_x, size_z, lanes), F32), pltpu.VMEM((9 * 256, 128), BF16)],
        flops=500_000_000,
    )(hidden, hidden_edge, second)
    prediction = prediction_rows.reshape(size_x, size_y, channels, size_z).transpose(2, 0, 1, 3)[None]

    steps = []
    for axis, start in (("gx", 1), ("gz", 2), ("gy", 1)):
        bit = start
        while bit < lax.axis_size(axis):
            steps.append((axis, bit))
            bit *= 2
    rounds = [steps[k : k + 2] for k in range(0, len(steps), 2)]
    turn = len(rounds) // 2 if len(steps) % 2 == 0 else 0
    carried = [half] * (len(rounds) - 2) + [rounded] * min(len(rounds), 2) + [half]
    send = call(first_sum, carried[0])(keep, taken)
    for k, even in enumerate(rounds):
        odd = rounds[(k + turn) % len(rounds)]
        flips = [(even[:1], odd[:1])]
        if len(even) == 2:
            flips += [(even[1:], odd[1:]), (even, odd)]
        got = [masked_swap(send, *pair) for pair in flips]
        if k == 0:
            *got, prediction = lax.optimization_barrier((*got, prediction))
        send = call(round_sum, carried[k + 1])(send, *got)
    mine = send
    other = flip(mine, "gz", 1)
    fisher_first, fisher_second = call(
        functools.partial(finish, norm), [struct((C, 27 * C), F32)] * 2
    )(mine, other)
    return prediction, fisher_first, fisher_second


def solution(mesh):
    in_specs = (P(None, None, "gx", "gy", "gz"), P(None, None, "gx", "gy", "gz"), P(), P())
    out_specs = (P(None, None, "gx", "gy", "gz"), P(), P())
    return jax.shard_map(local, mesh=mesh, in_specs=in_specs, out_specs=out_specs, check_vma=False)
```
